512 devices in a mesh: tm: 8 (over y_lo, x), rows: 64 (over z, y_hi, core).
Axes of the slice: x: 4, y: 4 (y_hi: 2, y_lo: 2; y = y_hi * 2 + y_lo), z: 16, core: 2. Of those that a mesh axis runs over, the one named last changes fastest.
Arguments:
- frames_in: bfloat16 [16, 128, 512, 128], P('tm', 'rows'), may hold values from -6 to 6
- temporal_weight: bfloat16 [3, 3, 3, 128, 128], replicated, may hold values from -0.109375 to 0.109375
- first_weight: bfloat16 [3, 3, 128, 128], replicated, may hold values from -0.1875 to 0.1875
- second_weight: bfloat16 [3, 3, 128, 128], replicated, may hold values from -0.1875 to 0.1875
Outputs:
- encoded: bfloat16 [8, 128, 512, 128], P(None, 'rows', 'tm')
The draws below stay inside these ranges and needn't reach their ends.
All inputs are finite; a program needn't handle non-finite values.
Results may differ from the reference program's by a relative error of at most 0.0052.
Values may be sent and summed in bfloat16 or wider, within the bound.
No kernel may reach another device: no remote copies, remote signals or barrier semaphores. Data moves between devices by JAX's collectives and lax.ppermute only.
A program may use at most 64 MiB of HBM per device.

```python
import jax
import jax.numpy as jnp
from jax import lax

C = 128
COLS = 512
FRAMES = 16
HEIGHT = 128


def block_levels(stream_key, dims, shards, smallest, top_value):
    gain = 1.0
    for dim, parts in shards:
        draws = jax.random.uniform(jax.random.fold_in(jax.random.fold_in(stream_key, 6), dim), (parts,), jnp.float32, smallest / len(shards), top_value / len(shards))
        gain = gain * jnp.repeat(jnp.exp(draws), dims[dim] // parts).reshape((-1,) + (1,) * (len(dims) - 1 - dim))
    return gain


def bell_draw(rng, extent, width, limit, split=(), kind=jnp.bfloat16):
    level = block_levels(rng, extent, split, -0.22, 0.18) if split else 1.0
    drawn = jax.random.normal(rng, extent, jnp.float32) * width * level
    return jnp.minimum(jnp.maximum(drawn, -limit), limit).astype(kind)


def setup_inputs(seed: int = 0) -> dict:
    streams_of = jax.random.split(jax.random.key(seed), 5)
    frames_in = bell_draw(streams_of[0], (FRAMES, HEIGHT, COLS, C), 1.0, 6.0, ((0, 8), (1, 64)))
    temporal_weight = bell_draw(streams_of[1], (3, 3, 3, C, C), (27 * C) ** -0.5, 0.109375)
    first_weight = bell_draw(streams_of[2], (3, 3, C, C), (9 * C) ** -0.5, 0.1875)
    second_weight = bell_draw(streams_of[3], (3, 3, C, C), (9 * C) ** -0.5, 0.1875)
    return {"frames_in": frames_in, "temporal_weight": temporal_weight, "first_weight": first_weight, "second_weight": second_weight}


def plane_conv(plane, weight, row_count, col_count):
    summed = jnp.zeros((row_count, col_count, weight.shape[-1]), jnp.float32)
    for tap_row in range(3):
        for tap_col in range(3):
            sliced = plane[tap_row:tap_row + row_count, tap_col:tap_col + col_count]
            summed = summed + jnp.einsum("rwc,cd->rwd", sliced, weight[tap_row, tap_col], precision=lax.Precision.HIGHEST)
    return summed


def reference(frames_in, temporal_weight, first_weight, second_weight):
    frame_count, row_count, col_count, chans = frames_in.shape
    out_count = frame_count // 2
    padded = jnp.pad(frames_in, ((1, 0), (1, 1), (1, 1), (0, 0)))
    temporal_f = temporal_weight.astype(jnp.float32)
    first_f = first_weight.astype(jnp.float32)
    second_f = second_weight.astype(jnp.float32)

    def one_frame(frame_at):
        window = lax.dynamic_slice_in_dim(padded, 2 * frame_at, 3, 0).astype(jnp.float32)
        summed = jnp.zeros((row_count, col_count, chans), jnp.float32)
        for tap_frame in range(3):
            summed = summed + plane_conv(window[tap_frame], temporal_f[tap_frame], row_count, col_count)
        return summed.astype(jnp.bfloat16)

    temporal = lax.map(one_frame, jnp.arange(out_count, dtype=jnp.int32))

    def spatial_frame(plane):
        plane_f = plane.astype(jnp.float32)
        hidden = jax.nn.silu(plane_conv(jnp.pad(plane_f, ((1, 1), (1, 1), (0, 0))), first_f, row_count, col_count)).astype(jnp.bfloat16)
        hidden_f = jnp.pad(hidden.astype(jnp.float32), ((1, 1), (1, 1), (0, 0)))
        return (plane_f + plane_conv(hidden_f, second_f, row_count, col_count)).astype(jnp.bfloat16)

    return lax.map(spatial_frame, temporal)
```

```python
import functools

import jax
import jax.numpy as jnp
from jax import lax
from jax.experimental import pallas as pl
from jax.experimental.pallas import tpu as pltpu
from jax.sharding import PartitionSpec as P

SLABS = 4
HALO = 4


def windows(frames, count, width):
    frame_count, row_count, col_count, chans = frames.shape
    padded = jnp.pad(frames, ((0, 0), (0, 0), (HALO, width - HALO), (0, 0)))
    body = padded[:, :, :col_count].reshape(frame_count, row_count, count, width, chans)
    tail = padded[:, :, width:].reshape(frame_count, row_count, count, width, chans)
    joined = jnp.concatenate([body, tail[:, :, :, : 2 * HALO]], axis=3)
    return jnp.transpose(joined, (2, 0, 1, 3, 4))


def conv_kernel(place, own, swap_a, swap_b, w_temporal, w_first, w_second, out, xs, ts, hs, wt, w1, w2):
    frames, rows, span, chans = own.shape[0], 8, own.shape[4], own.shape[5]
    pitch = frames * span
    even, first_col, first_row = place[0], place[1], place[2]
    last_col, last_row = place[3], place[4]

    for a in range(3):
        for b in range(3):
            for c in range(3):
                k = (a * 3 + b) * chans
                wt[k : k + chans, c * chans : (c + 1) * chans] = w_temporal[a, b, c]
    for b in range(3):
        for c in range(3):
            w1[b * chans : (b + 1) * chans, c * chans : (c + 1) * chans] = w_first[b, c]
            w2[b * chans : (b + 1) * chans, c * chans : (c + 1) * chans] = w_second[b, c]

    def put(row, pick):
        for t in range(0, frames, 2):
            at = row * pitch + t * span
            for a, f in ((1, 0), (2, 1)):
                pair = jnp.concatenate([pick(t, f), pick(t + 1, f)], axis=0)
                xs[a, at : at + 2 * span] = pair.astype(jnp.bfloat16)
            before = pick(t - 1, 1) if t else jnp.zeros((span, chans), jnp.float32)
            pair = jnp.concatenate([before, pick(t, 1)], axis=0)
            xs[0, at : at + 2 * span] = pair.astype(jnp.bfloat16)

    for row in range(rows):
        put(row + 3, lambda m, f: own[m, row // 2, f, row % 2].astype(jnp.float32))
    for row in range(3):
        def above(m, f):
            return jnp.where(even == 1, swap_b[m, f, row], swap_a[m, f, row]).astype(jnp.float32)

        def below(m, f):
            return jnp.where(even == 1, swap_a[m, f, row], swap_b[m, f, row]).astype(jnp.float32)

        put(row, above)
        put(row + 3 + rows, below)

    def taps(sum3):
        left, mid, right = sum3[:, :chans], sum3[:, chans : 2 * chans], sum3[:, 2 * chans :]
        return mid + pltpu.roll(left, 1, 0) + pltpu.roll(right, sum3.shape[0] - 1, 0)

    def inside(value, row):
        shape = (value.shape[0] // pitch, frames, span, chans)
        col = lax.broadcasted_iota(jnp.int32, shape, 2) + first_col
        r = lax.broadcasted_iota(jnp.int32, shape, 0) + (first_row + row)
        keep = (col >= 0) & (col < last_col) & (r >= 0) & (r < last_row)
        return jnp.where(keep, value.reshape(shape), 0.0).reshape(value.shape)

    step = 2
    block = step * pitch

    @pl.loop(0, (rows + 4) // step)
    def _(i):
        base = pl.multiple_of(i * block, block)
        lhs = jnp.concatenate(
            [xs[a, pl.ds(base + b * pitch, block)] for a in range(3) for b in range(3)], axis=1
        )
        sums = taps(jnp.dot(lhs, wt[...], preferred_element_type=jnp.float32))
        ts[pl.ds(base, block)] = inside(sums, i * step - 2).astype(jnp.bfloat16)

    @pl.loop(0, (rows + 2) // step)
    def _(i):
        base = pl.multiple_of(i * block, block)
        lhs = jnp.concatenate([ts[pl.ds(base + b * pitch, block)] for b in range(3)], axis=1)
        sums = taps(jnp.dot(lhs, w1[...], preferred_element_type=jnp.float32))
        active = sums / (1.0 + jnp.exp(-sums))
        hs[pl.ds(base, block)] = inside(active, i * step - 1).astype(jnp.bfloat16)

    @pl.loop(0, rows // step)
    def _(i):
        base = pl.multiple_of(i * block, block)
        lhs = jnp.concatenate([hs[pl.ds(base + b * pitch, block)] for b in range(3)], axis=1)
        sums = taps(jnp.dot(lhs, w2[...], preferred_element_type=jnp.float32))
        sums = sums + ts[pl.ds(base + 2 * pitch, block)].astype(jnp.float32)
        sums = sums.reshape(step, frames, span, chans)[:, :, HALO : span - HALO]
        for r in range(step):
            out[i, :, r] = sums[r].astype(jnp.bfloat16)


def per_device(frames_in, temporal_weight, first_weight, second_weight):
    tm, slabs = lax.axis_size("tm"), lax.axis_size("rows")
    planes = slabs // SLABS
    frame_count, row_count, col_count, chans = frames_in.shape
    windows_count = tm * SLABS
    width = col_count // windows_count
    span = width + 2 * HALO
    plane_rows = SLABS * row_count
    column, slab = lax.axis_index("tm"), lax.axis_index("rows")
    plane = slab // SLABS

    members = [[m * slabs + z * SLABS + j for m in range(tm) for j in range(SLABS)] for z in range(planes)]
    own = lax.all_to_all(
        windows(frames_in, windows_count, width),
        ("tm", "rows"),
        split_axis=0,
        concat_axis=0,
        tiled=True,
        axis_index_groups=members,
    ).reshape(tm, SLABS, frame_count, row_count, span, chans)

    bottom = jnp.concatenate([own[:, 2, :, 1:], own[:, 3]], axis=2)
    top = jnp.concatenate([own[:, 0], own[:, 1, :, :1]], axis=2)
    even = plane % 2 == 0

    def swap(parity):
        pairs = []
        for z in range(parity, planes - 1, 2):
            for j in range(SLABS):
                low, high = z * SLABS + j, (z + 1) * SLABS + j
                pairs += [(low, high), (high, low)]
        return pairs

    swap_a = lax.ppermute(jnp.where(even, bottom, top), "rows", swap(0))
    swap_b = lax.ppermute(jnp.where(even, top, bottom), "rows", swap(1))

    place = jnp.stack(
        [
            even.astype(jnp.int32),
            (column * SLABS + slab % SLABS) * width - HALO,
            plane * plane_rows,
            jnp.int32(col_count),
            jnp.int32(slabs * row_count),
        ]
    ).astype(jnp.int32)
    pitch = tm * span
    vmem = pl.BlockSpec(memory_space=pltpu.VMEM)
    encoded = pl.pallas_call(
        conv_kernel,
        out_shape=jax.ShapeDtypeStruct((SLABS, tm, row_count, width, chans), jnp.bfloat16),
        in_specs=[pl.BlockSpec(memory_space=pltpu.SMEM)] + [vmem] * 6,
        out_specs=vmem,
        scratch_shapes=[
            pltpu.VMEM((3, (plane_rows + 6) * pitch, chans), jnp.bfloat16),
            pltpu.VMEM(((plane_rows + 4) * pitch, chans), jnp.bfloat16),
            pltpu.VMEM(((plane_rows + 2) * pitch, chans), jnp.bfloat16),
            pltpu.VMEM((9 * chans, 3 * chans), jnp.bfloat16),
            pltpu.VMEM((3 * chans, 3 * chans), jnp.bfloat16),
            pltpu.VMEM((3 * chans, 3 * chans), jnp.bfloat16),
        ],
        compiler_params=pltpu.CompilerParams(vmem_limit_bytes=32 * 1024 * 1024),
        name="convs",
    )(place, own, swap_a, swap_b, temporal_weight, first_weight, second_weight)

    groups = [[z * SLABS + j for j in range(SLABS)] for z in range(planes)]
    encoded = lax.all_to_all(
        encoded, "rows", split_axis=0, concat_axis=0, tiled=True, axis_index_groups=groups
    )
    return jnp.transpose(encoded, (1, 2, 0, 3, 4)).reshape(tm, row_count, SLABS * width, chans)


def solution(mesh):
    placed = (P("tm", "rows", None, None), P(), P(), P())
    return jax.shard_map(
        per_device,
        mesh=mesh,
        in_specs=placed,
        out_specs=P(None, "rows", "tm", None),
        check_vma=False,
    )
```

```python
import jax
import jax.numpy as jnp
from jax import lax
from jax.experimental import pallas as pl
from jax.experimental.pallas import tpu as pltpu
from jax.sharding import PartitionSpec as P

SLABS = 4
HALO = 4
VMEM_BYTES = 32 * 1024 * 1024


def windows_kernel(frames, out):
    count, span = out.shape[0], out.shape[3]
    width = span - 2 * HALO
    for f in range(out.shape[1]):
        for r in range(out.shape[2]):
            row = frames[f, r].astype(jnp.float32)
            edge = jnp.zeros((HALO, row.shape[1]), jnp.float32)
            row = jnp.concatenate([edge, row, edge], axis=0)
            for k in range(count):
                out[k, f, r] = row[k * width : k * width + span].astype(jnp.bfloat16)


def column_taps(sums):
    chans = sums.shape[1] // 3
    left, mid, right = sums[:, :chans], sums[:, chans : 2 * chans], sums[:, 2 * chans :]
    return mid + pltpu.roll(left, 1, 0) + pltpu.roll(right, sums.shape[0] - 1, 0)


def inside(place, value, row, frames, span):
    first_col, first_row, last_col, last_row = place[1], place[2], place[3], place[4]
    shape = (value.shape[0] // (frames * span), frames, span, value.shape[1])
    col = lax.broadcasted_iota(jnp.int32, shape, 2) + first_col
    r = lax.broadcasted_iota(jnp.int32, shape, 0) + (first_row + row)
    keep = (col >= 0) & (col < last_col) & (r >= 0) & (r < last_row)
    return jnp.where(keep, value.reshape(shape), 0.0).reshape(value.shape)


def temporal_kernel(place, own, weight, ts, edges, send_a, send_b, xs, wt):
    frames, span, chans = own.shape[0], own.shape[4], own.shape[5]
    rows = own.shape[1] * own.shape[3]
    pitch = frames * span

    for a in range(3):
        for b in range(3):
            for c in range(3):
                k = (a * 3 + b) * chans
                wt[k : k + chans, c * chans : (c + 1) * chans] = weight[a, b, c]

    for row in range(rows):
        def pick(m, f):
            return own[m, row // 2, f, row % 2].astype(jnp.float32)

        for t in range(0, frames, 2):
            at = (row + 1) * pitch + t * span
            for a, f in ((1, 0), (2, 1)):
                pair = jnp.concatenate([pick(t, f), pick(t + 1, f)], axis=0)
                xs[a, at : at + 2 * span] = pair.astype(jnp.bfloat16)
            before = pick(t - 1, 1) if t else jnp.zeros((span, chans), jnp.float32)
            pair = jnp.concatenate([before, pick(t, 1)], axis=0)
            xs[0, at : at + 2 * span] = pair.astype(jnp.bfloat16)
    for a in range(3):
        for row in (0, rows + 1):
            xs[a, row * pitch : (row + 1) * pitch] = jnp.zeros((pitch, chans), jnp.bfloat16)

    step = rows // 2
    block = step * pitch
    for i in range(2):
        base = i * block
        lhs = jnp.concatenate(
            [xs[a, base + b * pitch : base + b * pitch + block] for a in range(3) for b in range(3)],
            axis=1,
        )
        sums = column_taps(jnp.dot(lhs, wt[...], preferred_element_type=jnp.float32))
        ts[base : base + block] = inside(place, sums, i * step, frames, span).astype(jnp.bfloat16)
        edges[i] = sums[:pitch] if i == 0 else sums[block - pitch :]

    for i, row, b in ((2, 1, 2), (3, rows, 0)):
        lhs = jnp.concatenate([xs[a, row * pitch : (row + 1) * pitch] for a in range(3)], axis=1)
        rhs = jnp.concatenate(
            [wt[(a * 3 + b) * chans : (a * 3 + b + 1) * chans] for a in range(3)], axis=0
        )
        edges[i] = column_taps(jnp.dot(lhs, rhs, preferred_element_type=jnp.float32))

    even = place[0] == 1
    up = (ts[(rows - 2) * pitch : (rows - 1) * pitch], edges[1].astype(jnp.bfloat16), edges[3].astype(jnp.bfloat16))
    down = (ts[pitch : 2 * pitch], edges[0].astype(jnp.bfloat16), edges[2].astype(jnp.bfloat16))
    for i in range(3):
        send_a[i] = jnp.where(even, up[i], down[i])
        send_b[i] = jnp.where(even, down[i], up[i])


def spatial_kernel(frames, place, ts, edges, swap_a, swap_b, w_first, w_second, out, tall, hs, w1, w2):
    rows = out.shape[0] * out.shape[2]
    chans = out.shape[4]
    pitch = ts.shape[0] // rows
    span = pitch // frames

    for b in range(3):
        for c in range(3):
            w1[b * chans : (b + 1) * chans, c * chans : (c + 1) * chans] = w_first[b, c]
            w2[b * chans : (b + 1) * chans, c * chans : (c + 1) * chans] = w_second[b, c]

    even = place[0] == 1

    def above(i):
        return jnp.where(even, swap_b[i], swap_a[i]).astype(jnp.float32)

    def below(i):
        return jnp.where(even, swap_a[i], swap_b[i]).astype(jnp.float32)

    def fill(row, value):
        at = (row + 2) * pitch
        tall[at : at + pitch] = inside(place, value, row, frames, span).astype(jnp.bfloat16)

    fill(-2, above(0))
    fill(-1, above(1) + edges[2])
    fill(0, above(2) + edges[0])
    tall[3 * pitch : (rows + 1) * pitch] = ts[pitch : (rows - 1) * pitch]
    fill(rows - 1, below(2) + edges[1])
    fill(rows, below(1) + edges[3])
    fill(rows + 1, below(0))

    step = rows // 2 + 1
    block = step * pitch
    for i in range(2):
        base = i * block
        lhs = jnp.concatenate([tall[base + b * pitch : base + b * pitch + block] for b in range(3)], axis=1)
        sums = column_taps(jnp.dot(lhs, w1[...], preferred_element_type=jnp.float32))
        active = sums / (1.0 + jnp.exp(-sums))
        hs[base : base + block] = inside(place, active, i * step - 1, frames, span).astype(jnp.bfloat16)

    step = rows // 2
    block = step * pitch
    for i in range(2):
        base = i * block
        lhs = jnp.concatenate([hs[base + b * pitch : base + b * pitch + block] for b in range(3)], axis=1)
        sums = column_taps(jnp.dot(lhs, w2[...], preferred_element_type=jnp.float32))
        sums = sums + tall[base + 2 * pitch : base + 2 * pitch + block].astype(jnp.float32)
        sums = sums.reshape(step // 2, 2, frames, span, chans)[:, :, :, HALO : span - HALO]
        for j in range(step // 2):
            for r in range(2):
                out[i * (step // 2) + j, :, r] = sums[j, r].astype(jnp.bfloat16)


def per_device(frames_in, temporal_weight, first_weight, second_weight):
    tm, slabs = lax.axis_size("tm"), lax.axis_size("rows")
    planes = slabs // SLABS
    frame_count, row_count, col_count, chans = frames_in.shape
    count = tm * SLABS
    width = col_count // count
    span = width + 2 * HALO
    plane_rows = SLABS * row_count
    pitch = tm * span
    column, slab = lax.axis_index("tm"), lax.axis_index("rows")
    plane = slab // SLABS
    place = jnp.stack(
        [
            (plane % 2 == 0).astype(jnp.int32),
            (column * SLABS + slab % SLABS) * width - HALO,
            plane * plane_rows,
            jnp.int32(col_count),
            jnp.int32(slabs * row_count),
        ]
    ).astype(jnp.int32)
    frames_in, place = lax.optimization_barrier((frames_in, place))
    vmem, smem = pl.BlockSpec(memory_space=pltpu.VMEM), pl.BlockSpec(memory_space=pltpu.SMEM)
    params = pltpu.CompilerParams(vmem_limit_bytes=VMEM_BYTES)

    cut = pl.pallas_call(
        windows_kernel,
        out_shape=jax.ShapeDtypeStruct((count, frame_count, row_count, span, chans), jnp.bfloat16),
        in_specs=[vmem],
        out_specs=vmem,
        compiler_params=params,
        name="windows",
    )(frames_in)
    members = [[m * slabs + z * SLABS + j for m in range(tm) for j in range(SLABS)] for z in range(planes)]
    own = lax.all_to_all(
        cut, ("tm", "rows"), split_axis=0, concat_axis=0, tiled=True, axis_index_groups=members
    ).reshape(tm, SLABS, frame_count, row_count, span, chans)

    line = (pitch, chans)
    ts, edges, send_a, send_b = pl.pallas_call(
        temporal_kernel,
        out_shape=[
            jax.ShapeDtypeStruct((plane_rows * pitch, chans), jnp.bfloat16),
            jax.ShapeDtypeStruct((4, *line), jnp.float32),
            jax.ShapeDtypeStruct((3, *line), jnp.bfloat16),
            jax.ShapeDtypeStruct((3, *line), jnp.bfloat16),
        ],
        in_specs=[smem, vmem, vmem],
        out_specs=[vmem] * 4,
        scratch_shapes=[
            pltpu.VMEM((3, (plane_rows + 2) * pitch, chans), jnp.bfloat16),
            pltpu.VMEM((9 * chans, 3 * chans), jnp.bfloat16),
        ],
        compiler_params=params,
        name="temporal",
    )(place, own, temporal_weight)

    def swap(parity):
        pairs = []
        for z in range(parity, planes - 1, 2):
            for j in range(SLABS):
                low, high = z * SLABS + j, (z + 1) * SLABS + j
                pairs += [(low, high), (high, low)]
        return pairs

    swap_a = lax.ppermute(send_a, "rows", swap(0))
    swap_b = lax.ppermute(send_b, "rows", swap(1))

    encoded = pl.pallas_call(
        lambda *refs: spatial_kernel(tm, *refs),
        out_shape=jax.ShapeDtypeStruct((SLABS, tm, row_count, width, chans), jnp.bfloat16),
        in_specs=[smem] + [vmem] * 6,
        out_specs=vmem,
        scratch_shapes=[
            pltpu.VMEM(((plane_rows + 4) * pitch, chans), jnp.bfloat16),
            pltpu.VMEM(((plane_rows + 2) * pitch, chans), jnp.bfloat16),
            pltpu.VMEM((3 * chans, 3 * chans), jnp.bfloat16),
            pltpu.VMEM((3 * chans, 3 * chans), jnp.bfloat16),
        ],
        compiler_params=params,
        name="spatial",
    )(place, ts, edges, swap_a, swap_b, first_weight, second_weight)

    groups = [[z * SLABS + j for j in range(SLABS)] for z in range(planes)]
    encoded = lax.all_to_all(
        encoded, "rows", split_axis=0, concat_axis=0, tiled=True, axis_index_groups=groups
    )
    return jnp.transpose(encoded, (1, 2, 0, 3, 4)).reshape(tm, row_count, SLABS * width, chans)


def solution(mesh):
    placed = (P("tm", "rows", None, None), P(), P(), P())
    return jax.shard_map(
        per_device,
        mesh=mesh,
        in_specs=placed,
        out_specs=P(None, "rows", "tm", None),
        check_vma=False,
    )
```

```python
import jax
import jax.numpy as jnp
from jax import lax
from jax.experimental import pallas as pl
from jax.experimental.pallas import tpu as pltpu
from jax.sharding import PartitionSpec as P

SLABS = 4
HALO = 4
VMEM_BYTES = 32 * 1024 * 1024


def windows_kernel(frames, out):
    count, span = out.shape[0], out.shape[3]
    width = span - 2 * HALO
    for f in range(out.shape[1]):
        for r in range(out.shape[2]):
            row = frames[f, r].astype(jnp.float32)
            edge = jnp.zeros((HALO, row.shape[1]), jnp.float32)
            row = jnp.concatenate([edge, row, edge], axis=0)
            for k in range(count):
                out[k, f, r] = row[k * width : k * width + span].astype(jnp.bfloat16)


def column_taps(sums):
    chans = sums.shape[1] // 3
    left, mid, right = sums[:, :chans], sums[:, chans : 2 * chans], sums[:, 2 * chans :]
    return mid + pltpu.roll(left, 1, 0) + pltpu.roll(right, sums.shape[0] - 1, 0)


def inside(place, value, row, frames, span):
    first_col, first_row, last_col, last_row = place[1], place[2], place[3], place[4]
    count, chans = value.shape[0] // (frames * span), value.shape[1]
    col = lax.broadcasted_iota(jnp.int32, (span, chans), 0) + first_col
    keep = (col >= 0) & (col < last_col)
    value = jnp.where(keep[None], value.reshape(count * frames, span, chans), 0.0)
    value = value.reshape(count, frames * span, chans)
    kept = []
    for i in range(count):
        r = first_row + row + i
        shown = jnp.where((r >= 0) & (r < last_row), 1.0, 0.0) if row + i < 0 or row + i >= 8 else None
        kept.append(value[i] if shown is None else value[i] * shown)
    return jnp.concatenate(kept, axis=0)


def temporal_weight_to(wt, weight):
    chans = weight.shape[3]
    for a in range(3):
        for b in range(3):
            for c in range(3):
                k = (b * 3 + a) * chans
                wt[k : k + chans, c * chans : (c + 1) * chans] = weight[a, b, c]


def plane_weight_to(wt, weight):
    chans = weight.shape[2]
    for b in range(3):
        for c in range(3):
            wt[b * chans : (b + 1) * chans, c * chans : (c + 1) * chans] = weight[b, c]


def frames_to(xs, at, own, row):
    frames, span, chans = own.shape[0], own.shape[4], own.shape[5]

    def pick(m, f):
        return own[m, row // 2, f, row % 2].astype(jnp.float32)

    for t in range(0, frames, 2):
        here = at + t * span
        for a, f in ((1, 0), (2, 1)):
            pair = jnp.concatenate([pick(t, f), pick(t + 1, f)], axis=0)
            xs[a, here : here + 2 * span] = pair.astype(jnp.bfloat16)
        before = pick(t - 1, 1) if t else jnp.zeros((span, chans), jnp.float32)
        pair = jnp.concatenate([before, pick(t, 1)], axis=0)
        xs[0, here : here + 2 * span] = pair.astype(jnp.bfloat16)


def rows_of(ref, first, count, pitch):
    return ref[first * pitch : (first + count) * pitch]


def row_taps(ref, first, count, pitch):
    return jnp.concatenate([rows_of(ref, first + b, count, pitch) for b in range(3)], axis=1)


def edge_kernel(place, own, weight, t_edge, edges, send_a, send_b, xs, wt):
    frames, span, chans = own.shape[0], own.shape[4], own.shape[5]
    rows = own.shape[1] * own.shape[3]
    pitch = frames * span
    temporal_weight_to(wt, weight)

    for i in range(3):
        frames_to(xs, i * pitch, own, i)
        frames_to(xs, (3 + i) * pitch, own, rows - 3 + i)

    def taps_of(i):
        return jnp.concatenate([xs[a, i * pitch : (i + 1) * pitch] for a in range(3)], axis=1)

    def dot(lhs, rhs):
        return column_taps(jnp.dot(lhs, rhs, preferred_element_type=jnp.float32))

    deep = 3 * chans
    x = [taps_of(i) for i in range(6)]
    low = dot(
        jnp.concatenate([jnp.concatenate(x[0:2], axis=1), jnp.concatenate(x[1:3], axis=1)], axis=0),
        wt[deep:],
    )
    high = dot(
        jnp.concatenate([jnp.concatenate(x[3:5], axis=1), jnp.concatenate(x[4:6], axis=1)], axis=0),
        wt[: 2 * deep],
    )
    outer = jnp.dot(
        jnp.concatenate([x[0], x[5]], axis=0),
        jnp.concatenate([wt[:deep], wt[2 * deep :]], axis=1),
        preferred_element_type=jnp.float32,
    )
    upper, lower = column_taps(outer[:, :deep]), column_taps(outer[:, deep:])
    first, last = low[:pitch], high[pitch:]
    before, after = lower[:pitch], upper[pitch:]
    edges[0], edges[1], edges[2], edges[3] = first, last, before, after
    near = inside(place, low[pitch:] + upper[:pitch], 1, frames, span).astype(jnp.bfloat16)
    far = inside(place, high[:pitch] + lower[pitch:], rows - 2, frames, span).astype(jnp.bfloat16)
    t_edge[0], t_edge[1] = near, far

    even = place[0] == 1
    up = (far, last.astype(jnp.bfloat16), after.astype(jnp.bfloat16))
    down = (near, first.astype(jnp.bfloat16), before.astype(jnp.bfloat16))
    for i in range(3):
        send_a[i] = jnp.where(even, up[i], down[i])
        send_b[i] = jnp.where(even, down[i], up[i])


def crop(value, frames, span):
    shape = (value.shape[0] // (frames * span), frames, span, value.shape[1])
    return value.reshape(shape)[:, :, HALO : span - HALO].astype(jnp.bfloat16)


def inner_kernel(place, own, weight, t_edge, w_first, w_second, t_mid, h_mid, o_mid, xs, tall, wt, w1, w2):
    frames, span = own.shape[0], own.shape[4]
    rows = own.shape[1] * own.shape[3]
    pitch = frames * span
    temporal_weight_to(wt, weight)
    plane_weight_to(w1, w_first)
    plane_weight_to(w2, w_second)
    for row in range(1, rows - 1):
        frames_to(xs, (row - 1) * pitch, own, row)
    lhs = jnp.concatenate(
        [xs[a, b * pitch : (b + rows - 4) * pitch] for b in range(3) for a in range(3)], axis=1
    )
    sums = column_taps(jnp.dot(lhs, wt[...], preferred_element_type=jnp.float32))
    middle = inside(place, sums, 2, frames, span).astype(jnp.bfloat16)
    t_mid[...] = middle
    tall[:pitch] = t_edge[0]
    tall[pitch : (rows - 3) * pitch] = middle
    tall[(rows - 3) * pitch :] = t_edge[1]

    sums = column_taps(
        jnp.dot(row_taps(tall, 0, rows - 4, pitch), w1[...], preferred_element_type=jnp.float32)
    )
    active = sums * (0.5 * jnp.tanh(0.5 * sums) + 0.5)
    h_mid[...] = inside(place, active, 2, frames, span).astype(jnp.bfloat16)

    sums = column_taps(
        jnp.dot(row_taps(h_mid, 0, rows - 6, pitch), w2[...], preferred_element_type=jnp.float32)
    )
    sums = sums + rows_of(t_mid, 1, rows - 6, pitch).astype(jnp.float32)
    o_mid[...] = crop(sums, frames, span)


def outer_kernel(
    frames, place, t_edge, edges, t_mid, h_mid, o_mid, swap_a, swap_b, w_first, w_second,
    out, tall, hs, w1, w2,
):
    rows = out.shape[0] * out.shape[2]
    pitch = t_edge.shape[1]
    span = pitch // frames
    plane_weight_to(w1, w_first)
    plane_weight_to(w2, w_second)

    even = place[0] == 1

    def above(i):
        return jnp.where(even, swap_b[i], swap_a[i]).astype(jnp.float32)

    def below(i):
        return jnp.where(even, swap_a[i], swap_b[i]).astype(jnp.float32)

    def fill(at, row, value):
        value = inside(place, value, row, frames, span)
        tall[at * pitch : (at + 1) * pitch] = value.astype(jnp.bfloat16)

    fill(0, -2, above(0))
    fill(1, -1, above(1) + edges[2])
    fill(2, 0, above(2) + edges[0])
    tall[3 * pitch : 4 * pitch] = t_edge[0]
    tall[4 * pitch : 5 * pitch] = rows_of(t_mid, 0, 1, pitch)
    tall[5 * pitch : 6 * pitch] = rows_of(t_mid, rows - 5, 1, pitch)
    tall[6 * pitch : 7 * pitch] = t_edge[1]
    fill(7, rows - 1, below(2) + edges[1])
    fill(8, rows, below(1) + edges[3])
    fill(9, rows + 1, below(0))

    lhs = jnp.concatenate([row_taps(tall, s, 3, pitch) for s in (0, 5)], axis=0)
    sums = column_taps(jnp.dot(lhs, w1[...], preferred_element_type=jnp.float32))
    active = sums * (0.5 * jnp.tanh(0.5 * sums) + 0.5)
    half = 3 * pitch
    hs[:half] = inside(place, active[:half], -1, frames, span).astype(jnp.bfloat16)
    hs[half : 5 * pitch] = rows_of(h_mid, 0, 2, pitch)
    hs[5 * pitch : 7 * pitch] = rows_of(h_mid, rows - 6, 2, pitch)
    hs[7 * pitch :] = inside(place, active[half:], rows - 2, frames, span).astype(jnp.bfloat16)

    lhs = jnp.concatenate([row_taps(hs, s, 3, pitch) for s in (0, 5)], axis=0)
    sums = column_taps(jnp.dot(lhs, w2[...], preferred_element_type=jnp.float32))
    skip = jnp.concatenate([rows_of(tall, s, 3, pitch) for s in (2, 5)], axis=0)
    done = crop(sums + skip.astype(jnp.float32), frames, span)
    for i in range(3):
        out[i // 2, :, i % 2] = done[i]
        row = rows - 3 + i
        out[row // 2, :, row % 2] = done[3 + i]
    for row in range(3, rows - 3):
        out[row // 2, :, row % 2] = o_mid[row - 3]


def per_device(frames_in, temporal_weight, first_weight, second_weight):
    tm, slabs = lax.axis_size("tm"), lax.axis_size("rows")
    planes = slabs // SLABS
    frame_count, row_count, col_count, chans = frames_in.shape
    count = tm * SLABS
    width = col_count // count
    span = width + 2 * HALO
    plane_rows = SLABS * row_count
    pitch = tm * span
    column, slab = lax.axis_index("tm"), lax.axis_index("rows")
    plane = slab // SLABS
    place = jnp.stack(
        [
            (plane % 2 == 0).astype(jnp.int32),
            (column * SLABS + slab % SLABS) * width - HALO,
            plane * plane_rows,
            jnp.int32(col_count),
            jnp.int32(slabs * row_count),
        ]
    ).astype(jnp.int32)
    frames_in, place = lax.optimization_barrier((frames_in, place))
    vmem, smem = pl.BlockSpec(memory_space=pltpu.VMEM), pl.BlockSpec(memory_space=pltpu.SMEM)
    params = pltpu.CompilerParams(vmem_limit_bytes=VMEM_BYTES)

    def brain(*shape):
        return jax.ShapeDtypeStruct(shape, jnp.bfloat16)

    def held(*shape):
        return pltpu.VMEM(shape, jnp.bfloat16)

    cut = pl.pallas_call(
        windows_kernel,
        out_shape=brain(count, frame_count, row_count, span, chans),
        in_specs=[vmem],
        out_specs=vmem,
        compiler_params=params,
        name="windows",
    )(frames_in)
    members = [[m * slabs + z * SLABS + j for m in range(tm) for j in range(SLABS)] for z in range(planes)]
    own = lax.all_to_all(
        cut, ("tm", "rows"), split_axis=0, concat_axis=0, tiled=True, axis_index_groups=members
    ).reshape(tm, SLABS, frame_count, row_count, span, chans)

    t_edge, edges, send_a, send_b = pl.pallas_call(
        edge_kernel,
        out_shape=[
            brain(2, pitch, chans),
            jax.ShapeDtypeStruct((4, pitch, chans), jnp.float32),
            brain(3, pitch, chans),
            brain(3, pitch, chans),
        ],
        in_specs=[smem, vmem, vmem],
        out_specs=[vmem] * 4,
        scratch_shapes=[held(3, 6 * pitch, chans), held(9 * chans, 3 * chans)],
        compiler_params=params,
        name="edge",
    )(place, own, temporal_weight)

    def swap(parity):
        pairs = []
        for z in range(parity, planes - 1, 2):
            for j in range(SLABS):
                low, high = z * SLABS + j, (z + 1) * SLABS + j
                pairs += [(low, high), (high, low)]
        return pairs

    swap_a = lax.ppermute(send_a, "rows", swap(0))
    swap_b = lax.ppermute(send_b, "rows", swap(1))

    inner = plane_rows - 4
    t_mid, h_mid, o_mid = pl.pallas_call(
        inner_kernel,
        out_shape=[
            brain(inner * pitch, chans),
            brain(inner * pitch, chans),
            brain(inner - 2, tm, width, chans),
        ],
        in_specs=[smem] + [vmem] * 5,
        out_specs=[vmem] * 3,
        scratch_shapes=[
            held(3, (inner + 2) * pitch, chans),
            held((inner + 2) * pitch, chans),
            held(9 * chans, 3 * chans),
            held(3 * chans, 3 * chans),
            held(3 * chans, 3 * chans),
        ],
        compiler_params=params,
        cost_estimate=pl.CostEstimate(flops=10**9, bytes_accessed=4 * 10**6, transcendentals=10**5),
        name="inner",
    )(place, own, temporal_weight, t_edge, first_weight, second_weight)
    encoded = pl.pallas_call(
        lambda *refs: outer_kernel(tm, *refs),
        out_shape=brain(SLABS, tm, row_count, width, chans),
        in_specs=[smem] + [vmem] * 9,
        out_specs=vmem,
        scratch_shapes=[
            held(10 * pitch, chans),
            held(10 * pitch, chans),
            held(3 * chans, 3 * chans),
            held(3 * chans, 3 * chans),
        ],
        compiler_params=params,
        name="outer",
    )(place, t_edge, edges, t_mid, h_mid, o_mid, swap_a, swap_b, first_weight, second_weight)

    groups = [[z * SLABS + j for j in range(SLABS)] for z in range(planes)]
    encoded = lax.all_to_all(
        encoded, "rows", split_axis=0, concat_axis=0, tiled=True, axis_index_groups=groups
    )
    return jnp.transpose(encoded, (1, 2, 0, 3, 4)).reshape(tm, row_count, SLABS * width, chans)


def solution(mesh):
    placed = (P("tm", "rows", None, None), P(), P(), P())
    return jax.shard_map(
        per_device,
        mesh=mesh,
        in_specs=placed,
        out_specs=P(None, "rows", "tm", None),
        check_vma=False,
    )
```

```python
import jax
import jax.numpy as jnp
from jax import lax
from jax.experimental import pallas as pl
from jax.experimental.pallas import tpu as pltpu
from jax.sharding import PartitionSpec as P

SLABS = 4
HALO = 4
VMEM_BYTES = 32 * 1024 * 1024


def windows_kernel(frames, out):
    count, span = out.shape[0], out.shape[3]
    width = span - 2 * HALO
    for f in range(out.shape[1]):
        for r in range(out.shape[2]):
            row = frames[f, r].astype(jnp.float32)
            edge = jnp.zeros((HALO, row.shape[1]), jnp.float32)
            row = jnp.concatenate([edge, row, edge], axis=0)
            for k in range(count):
                out[k, f, r] = row[k * width : k * width + span].astype(jnp.bfloat16)


def column_taps(sums):
    chans = sums.shape[1] // 3
    left, mid, right = sums[:, :chans], sums[:, chans : 2 * chans], sums[:, 2 * chans :]
    return mid + pltpu.roll(left, 1, 0) + pltpu.roll(right, sums.shape[0] - 1, 0)


def inside(place, value, row, frames, span):
    first_col, first_row, last_col, last_row = place[0], place[1], place[2], place[3]
    count, chans = value.shape[0] // (frames * span), value.shape[1]
    col = lax.broadcasted_iota(jnp.int32, (span, chans), 0) + first_col
    keep = (col >= 0) & (col < last_col)
    value = jnp.where(keep[None], value.reshape(count * frames, span, chans), 0.0)
    value = value.reshape(count, frames * span, chans)
    kept = []
    for i in range(count):
        r = first_row + row + i
        shown = jnp.where((r >= 0) & (r < last_row), 1.0, 0.0) if row + i < 0 or row + i >= 8 else None
        kept.append(value[i] if shown is None else value[i] * shown)
    return jnp.concatenate(kept, axis=0)


def temporal_weight_to(wt, weight):
    chans = weight.shape[3]
    for a in range(3):
        for b in range(3):
            for c in range(3):
                k = (b * 3 + a) * chans
                wt[k : k + chans, c * chans : (c + 1) * chans] = weight[a, b, c]


def plane_weight_to(wt, weight):
    chans = weight.shape[2]
    for b in range(3):
        for c in range(3):
            wt[b * chans : (b + 1) * chans, c * chans : (c + 1) * chans] = weight[b, c]


def frames_to(xs, at, own, row):
    frames, span, chans = own.shape[0], own.shape[4], own.shape[5]

    def pick(m, f):
        return own[m, row // 2, f, row % 2].astype(jnp.float32)

    for t in range(0, frames, 2):
        here = at + t * span
        for a, f in ((1, 0), (2, 1)):
            pair = jnp.concatenate([pick(t, f), pick(t + 1, f)], axis=0)
            xs[a, here : here + 2 * span] = pair.astype(jnp.bfloat16)
        before = pick(t - 1, 1) if t else jnp.zeros((span, chans), jnp.float32)
        pair = jnp.concatenate([before, pick(t, 1)], axis=0)
        xs[0, here : here + 2 * span] = pair.astype(jnp.bfloat16)


def silu(value):
    return value * (0.5 * jnp.tanh(0.5 * value) + 0.5)


def rows_of(ref, first, count, pitch):
    return ref[first * pitch : (first + count) * pitch]


def row_taps(ref, first, count, pitch):
    return jnp.concatenate([rows_of(ref, first + b, count, pitch) for b in range(3)], axis=1)


def temporal_taps(weight, row_taps):
    return jnp.concatenate(
        [
            jnp.concatenate([weight[a, b, c] for c in range(3)], axis=1)
            for b in row_taps
            for a in range(3)
        ],
        axis=0,
    )


def edge_kernel(place, own, weight, t_edge, edges, send_down, send_up, xs):
    frames, span, chans = own.shape[0], own.shape[4], own.shape[5]
    rows = own.shape[1] * own.shape[3]
    pitch = frames * span

    for i in range(3):
        frames_to(xs, i * pitch, own, i)
        frames_to(xs, (3 + i) * pitch, own, rows - 3 + i)

    def taps_of(i):
        return jnp.concatenate([xs[a, i * pitch : (i + 1) * pitch] for a in range(3)], axis=1)

    def dot(lhs, rhs):
        return column_taps(jnp.dot(lhs, rhs, preferred_element_type=jnp.float32))

    deep = 3 * chans
    x = [taps_of(i) for i in range(6)]
    low = dot(
        jnp.concatenate([jnp.concatenate(x[0:2], axis=1), jnp.concatenate(x[1:3], axis=1)], axis=0),
        temporal_taps(weight, (1, 2)),
    )
    high = dot(
        jnp.concatenate([jnp.concatenate(x[3:5], axis=1), jnp.concatenate(x[4:6], axis=1)], axis=0),
        temporal_taps(weight, (0, 1)),
    )
    outer = jnp.dot(
        jnp.concatenate([x[0], x[5]], axis=0),
        jnp.concatenate([temporal_taps(weight, (b,)) for b in (0, 2)], axis=1),
        preferred_element_type=jnp.float32,
    )
    upper, lower = column_taps(outer[:, :deep]), column_taps(outer[:, deep:])
    first, last = low[:pitch], high[pitch:]
    before, after = lower[:pitch], upper[pitch:]
    edges[0], edges[1], edges[2], edges[3] = first, last, before, after
    near = inside(place, low[pitch:] + upper[:pitch], 1, frames, span).astype(jnp.bfloat16)
    far = inside(place, high[:pitch] + lower[pitch:], rows - 2, frames, span).astype(jnp.bfloat16)
    t_edge[0], t_edge[1] = near, far

    for i, value in enumerate((far, last.astype(jnp.bfloat16), after.astype(jnp.bfloat16))):
        send_up[i] = value
    for i, value in enumerate((near, first.astype(jnp.bfloat16), before.astype(jnp.bfloat16))):
        send_down[i] = value


def crop(value, frames, span):
    shape = (value.shape[0] // (frames * span), frames, span, value.shape[1])
    return value.reshape(shape)[:, :, HALO : span - HALO].astype(jnp.bfloat16)


def dot_taps(lhs, rhs):
    lhs = jnp.concatenate([jnp.concatenate(blocks, axis=1) for blocks in lhs], axis=0)
    return column_taps(jnp.dot(lhs, rhs, preferred_element_type=jnp.float32))


def split_rows(value, pitch):
    return [value[at : at + pitch] for at in range(0, value.shape[0], pitch)]


def known_rows(first, second, before_last, last, weight):
    pitch, chans = first.shape
    none = jnp.zeros_like(first)
    top = dot_taps([[none, first], [first, second]], weight[chans:])
    end = dot_taps([[before_last, last], [last, none]], weight[: 2 * chans])
    return split_rows(top, pitch) + split_rows(end, pitch)


def outer_rows(top, end, weight, known):
    pitch, chans = top[0].shape
    none = jnp.zeros_like(top[0])
    first, last = split_rows(dot_taps([top, end], weight[...]), pitch)
    near = split_rows(dot_taps([top[1:], [top[2], none]], weight[: 2 * chans]), pitch)
    far = split_rows(dot_taps([[none, end[0]], end[:2]], weight[chans:]), pitch)
    inner = [value + known[i] for i, value in enumerate(near + far)]
    return [first, *inner, last]


def inner_kernel(
    place, own, weight, t_edge, w_first, w_second, known_h, known_o, o_mid, w1, w2,
    xs, tall, hs, wt,
):
    frames, span = own.shape[0], own.shape[4]
    rows = own.shape[1] * own.shape[3]
    pitch = frames * span
    temporal_weight_to(wt, weight)
    plane_weight_to(w1, w_first)
    plane_weight_to(w2, w_second)
    for row in range(1, rows - 1):
        frames_to(xs, (row - 1) * pitch, own, row)
    lhs = jnp.concatenate(
        [xs[a, b * pitch : (b + rows - 4) * pitch] for b in range(3) for a in range(3)], axis=1
    )
    sums = column_taps(jnp.dot(lhs, wt[...], preferred_element_type=jnp.float32))

    tall[:pitch] = t_edge[0]
    tall[pitch : (rows - 3) * pitch] = inside(place, sums, 2, frames, span).astype(jnp.bfloat16)
    tall[(rows - 3) * pitch :] = t_edge[1]
    inner = rows - 4
    sums = column_taps(
        jnp.dot(row_taps(tall, 0, inner, pitch), w1[...], preferred_element_type=jnp.float32)
    )
    hs[...] = inside(place, silu(sums), 2, frames, span).astype(jnp.bfloat16)
    temporal = [rows_of(tall, i, 1, pitch) for i in (0, 1, inner, inner + 1)]
    for i, value in enumerate(known_rows(*temporal, w1)):
        known_h[i] = value

    sums = column_taps(
        jnp.dot(row_taps(hs, 0, inner - 2, pitch), w2[...], preferred_element_type=jnp.float32)
    )
    sums = sums + rows_of(tall, 2, inner - 2, pitch).astype(jnp.float32)
    o_mid[...] = crop(sums, frames, span)
    hidden = [rows_of(hs, i, 1, pitch) for i in (0, 1, inner - 2, inner - 1)]
    for i, value in enumerate(known_rows(*hidden, w2)):
        known_o[i] = value + temporal[i].astype(jnp.float32)


def outer_kernel(frames, place, edges, known_h, known_o, o_mid, below, above, w1, w2, out):
    rows = out.shape[0] * out.shape[2]
    pitch = edges.shape[1]
    span = pitch // frames

    def shown(value, row):
        return inside(place, value, row, frames, span).astype(jnp.bfloat16)

    top = [
        shown(above[0].astype(jnp.float32), -2),
        shown(above[1] + edges[2], -1),
        shown(above[2] + edges[0], 0),
    ]
    end = [
        shown(below[2] + edges[1], rows - 1),
        shown(below[1] + edges[3], rows),
        shown(below[0].astype(jnp.float32), rows + 1),
    ]
    sums = outer_rows(top, end, w1, known_h)
    places = (-1, 0, 1, rows - 2, rows - 1, rows)
    hidden = [shown(silu(value), row) for value, row in zip(sums, places)]

    sums = outer_rows(hidden[:3], hidden[3:], w2, known_o)
    sums[0] = sums[0] + top[2].astype(jnp.float32)
    sums[5] = sums[5] + end[0].astype(jnp.float32)
    for value, row in zip(sums, (0, 1, 2, rows - 3, rows - 2, rows - 1)):
        out[row // 2, :, row % 2] = crop(value, frames, span)[0]
    for row in range(3, rows - 3):
        out[row // 2, :, row % 2] = o_mid[row - 3]


def per_device(frames_in, temporal_weight, first_weight, second_weight):
    tm, slabs = lax.axis_size("tm"), lax.axis_size("rows")
    planes = slabs // SLABS
    frame_count, row_count, col_count, chans = frames_in.shape
    count = tm * SLABS
    width = col_count // count
    span = width + 2 * HALO
    plane_rows = SLABS * row_count
    pitch = tm * span
    column, slab = lax.axis_index("tm"), lax.axis_index("rows")
    plane = slab // SLABS
    place = jnp.stack(
        [
            (column * SLABS + slab % SLABS) * width - HALO,
            plane * plane_rows,
            jnp.int32(col_count),
            jnp.int32(slabs * row_count),
        ]
    ).astype(jnp.int32)
    frames_in, place = lax.optimization_barrier((frames_in, place))
    vmem, smem = pl.BlockSpec(memory_space=pltpu.VMEM), pl.BlockSpec(memory_space=pltpu.SMEM)
    params = pltpu.CompilerParams(vmem_limit_bytes=VMEM_BYTES)

    def brain(*shape):
        return jax.ShapeDtypeStruct(shape, jnp.bfloat16)

    def held(*shape):
        return pltpu.VMEM(shape, jnp.bfloat16)

    cut = pl.pallas_call(
        windows_kernel,
        out_shape=brain(count, frame_count, row_count, span, chans),
        in_specs=[vmem],
        out_specs=vmem,
        compiler_params=params,
        name="windows",
    )(frames_in)
    members = [[m * slabs + z * SLABS + j for m in range(tm) for j in range(SLABS)] for z in range(planes)]
    own = lax.all_to_all(
        cut, ("tm", "rows"), split_axis=0, concat_axis=0, tiled=True, axis_index_groups=members
    ).reshape(tm, SLABS, frame_count, row_count, span, chans)

    t_edge, edges, send_down, send_up = pl.pallas_call(
        edge_kernel,
        out_shape=[
            brain(2, pitch, chans),
            jax.ShapeDtypeStruct((4, pitch, chans), jnp.float32),
            brain(3, pitch, chans),
            brain(3, pitch, chans),
        ],
        in_specs=[smem, vmem, vmem],
        out_specs=[vmem] * 4,
        scratch_shapes=[held(3, 6 * pitch, chans)],
        compiler_params=params,
        name="edge",
    )(place, own, temporal_weight)

    reach = range(slabs - SLABS)
    above = lax.ppermute(send_up, "rows", [(r, r + SLABS) for r in reach])
    below = lax.ppermute(send_down, "rows", [(r + SLABS, r) for r in reach])

    inner = plane_rows - 4
    partial = jax.ShapeDtypeStruct((4, pitch, chans), jnp.float32)
    known_h, known_o, o_mid, w1, w2 = pl.pallas_call(
        inner_kernel,
        out_shape=[
            partial,
            partial,
            brain(inner - 2, tm, width, chans),
            brain(3 * chans, 3 * chans),
            brain(3 * chans, 3 * chans),
        ],
        in_specs=[smem] + [vmem] * 5,
        out_specs=[vmem] * 5,
        scratch_shapes=[
            held(3, (inner + 2) * pitch, chans),
            held((inner + 2) * pitch, chans),
            held(inner * pitch, chans),
            held(9 * chans, 3 * chans),
        ],
        compiler_params=params,
        cost_estimate=pl.CostEstimate(flops=10**9, bytes_accessed=4 * 10**6, transcendentals=10**5),
        name="inner",
    )(place, own, temporal_weight, t_edge, first_weight, second_weight)
    encoded = pl.pallas_call(
        lambda *refs: outer_kernel(tm, *refs),
        out_shape=brain(SLABS, tm, row_count, width, chans),
        in_specs=[smem] + [vmem] * 8,
        out_specs=vmem,
        compiler_params=params,
        name="outer",
    )(place, edges, known_h, known_o, o_mid, below, above, w1, w2)

    groups = [[z * SLABS + j for j in range(SLABS)] for z in range(planes)]
    encoded = lax.all_to_all(
        encoded, "rows", split_axis=0, concat_axis=0, tiled=True, axis_index_groups=groups
    )
    return jnp.transpose(encoded, (1, 2, 0, 3, 4)).reshape(tm, row_count, SLABS * width, chans)


def solution(mesh):
    placed = (P("tm", "rows", None, None), P(), P(), P())
    return jax.shard_map(
        per_device,
        mesh=mesh,
        in_specs=placed,
        out_specs=P(None, "rows", "tm", None),
        check_vma=False,
    )
```

```python
import jax
import jax.numpy as jnp
from jax import lax
from jax.experimental import pallas as pl
from jax.experimental.pallas import tpu as pltpu
from jax.sharding import PartitionSpec as P

SLABS = 4
HALO = 4
VMEM_BYTES = 32 * 1024 * 1024


def windows_kernel(frames, out):
    count, span = out.shape[0], out.shape[3]
    width = span - 2 * HALO
    for f in range(out.shape[1]):
        for r in range(out.shape[2]):
            row = frames[f, r].astype(jnp.float32)
            edge = jnp.zeros((HALO, row.shape[1]), jnp.float32)
            row = jnp.concatenate([edge, row, edge], axis=0)
            for k in range(count):
                out[k, f, r] = row[k * width : k * width + span].astype(jnp.bfloat16)


def column_taps(sums):
    chans = sums.shape[1] // 3
    left, mid, right = sums[:, :chans], sums[:, chans : 2 * chans], sums[:, 2 * chans :]
    return mid + pltpu.roll(left, 1, 0) + pltpu.roll(right, sums.shape[0] - 1, 0)


def inside(value, mask):
    rows, chans = value.shape
    shown = value.reshape(rows // mask.shape[0], *mask.shape) * mask[...][None]
    return shown.reshape(rows, chans)


def temporal_weight_to(wt, weight):
    chans = weight.shape[3]
    for a in range(3):
        for b in range(3):
            for c in range(3):
                k = (b * 3 + a) * chans
                wt[k : k + chans, c * chans : (c + 1) * chans] = weight[a, b, c]


def plane_weight_to(wt, weight):
    chans = weight.shape[2]
    for b in range(3):
        for c in range(3):
            wt[b * chans : (b + 1) * chans, c * chans : (c + 1) * chans] = weight[b, c]


def frames_to(xs, at, own, row):
    frames, span, chans = own.shape[0], own.shape[4], own.shape[5]

    def pick(m, f):
        return own[m, row // 2, f, row % 2].astype(jnp.float32)

    for t in range(0, frames, 2):
        here = at + t * span
        for a, f in ((1, 0), (2, 1)):
            pair = jnp.concatenate([pick(t, f), pick(t + 1, f)], axis=0)
            xs[a, here : here + 2 * span] = pair.astype(jnp.bfloat16)
        before = pick(t - 1, 1) if t else jnp.zeros((span, chans), jnp.float32)
        pair = jnp.concatenate([before, pick(t, 1)], axis=0)
        xs[0, here : here + 2 * span] = pair.astype(jnp.bfloat16)


def silu(value):
    return value * (0.5 * jnp.tanh(0.5 * value) + 0.5)


def rows_of(ref, first, count, pitch):
    return ref[first * pitch : (first + count) * pitch]


def row_taps(ref, first, count, pitch):
    return jnp.concatenate([rows_of(ref, first + b, count, pitch) for b in range(3)], axis=1)


def temporal_taps(weight, row_taps):
    return jnp.concatenate(
        [
            jnp.concatenate([weight[a, b, c] for c in range(3)], axis=1)
            for b in row_taps
            for a in range(3)
        ],
        axis=0,
    )


def edge_kernel(masks, own, weight, t_edge, edges, send_down, send_up, xs):
    frames, span, chans = own.shape[0], own.shape[4], own.shape[5]
    rows = own.shape[1] * own.shape[3]
    pitch = frames * span

    for i in range(3):
        frames_to(xs, i * pitch, own, i)
        frames_to(xs, (3 + i) * pitch, own, rows - 3 + i)

    def taps_of(i):
        return jnp.concatenate([xs[a, i * pitch : (i + 1) * pitch] for a in range(3)], axis=1)

    def dot(lhs, rhs):
        return column_taps(jnp.dot(lhs, rhs, preferred_element_type=jnp.float32))

    deep = 3 * chans
    x = [taps_of(i) for i in range(6)]
    low = dot(
        jnp.concatenate([jnp.concatenate(x[0:2], axis=1), jnp.concatenate(x[1:3], axis=1)], axis=0),
        temporal_taps(weight, (1, 2)),
    )
    high = dot(
        jnp.concatenate([jnp.concatenate(x[3:5], axis=1), jnp.concatenate(x[4:6], axis=1)], axis=0),
        temporal_taps(weight, (0, 1)),
    )
    outer = jnp.dot(
        jnp.concatenate([x[0], x[5]], axis=0),
        jnp.concatenate([temporal_taps(weight, (b,)) for b in (0, 2)], axis=1),
        preferred_element_type=jnp.float32,
    )
    upper, lower = column_taps(outer[:, :deep]), column_taps(outer[:, deep:])
    first, last = low[:pitch], high[pitch:]
    before, after = lower[:pitch], upper[pitch:]
    edges[0], edges[1], edges[2], edges[3] = first, last, before, after
    near = inside(low[pitch:] + upper[:pitch], masks[0]).astype(jnp.bfloat16)
    far = inside(high[:pitch] + lower[pitch:], masks[0]).astype(jnp.bfloat16)
    t_edge[0], t_edge[1] = near, far

    for i, value in enumerate((far, last.astype(jnp.bfloat16), after.astype(jnp.bfloat16))):
        send_up[i] = value
    for i, value in enumerate((near, first.astype(jnp.bfloat16), before.astype(jnp.bfloat16))):
        send_down[i] = value


def crop(value, frames, span):
    shape = (value.shape[0] // (frames * span), frames, span, value.shape[1])
    return value.reshape(shape)[:, :, HALO : span - HALO].astype(jnp.bfloat16)


def dot_taps(lhs, rhs):
    lhs = jnp.concatenate([jnp.concatenate(blocks, axis=1) for blocks in lhs], axis=0)
    return column_taps(jnp.dot(lhs, rhs, preferred_element_type=jnp.float32))


def split_rows(value, pitch):
    return [value[at : at + pitch] for at in range(0, value.shape[0], pitch)]


def known_rows(first, second, before_last, last, weight):
    pitch, chans = first.shape
    none = jnp.zeros_like(first)
    top = dot_taps([[none, first], [first, second]], weight[chans:])
    end = dot_taps([[before_last, last], [last, none]], weight[: 2 * chans])
    return split_rows(top, pitch) + split_rows(end, pitch)


def outer_rows(top, end, weight, known):
    pitch, chans = top[0].shape
    none = jnp.zeros_like(top[0])
    first, last = split_rows(dot_taps([top, end], weight[...]), pitch)
    near = split_rows(dot_taps([top[1:], [top[2], none]], weight[: 2 * chans]), pitch)
    far = split_rows(dot_taps([[none, end[0]], end[:2]], weight[chans:]), pitch)
    inner = [value + known[i] for i, value in enumerate(near + far)]
    return [first, *inner, last]


def inner_kernel(
    masks, own, weight, t_edge, w_first, w_second, known_h, known_o, o_mid, w1, w2,
    xs, tall, hs, wt,
):
    frames, span = own.shape[0], own.shape[4]
    rows = own.shape[1] * own.shape[3]
    pitch = frames * span
    temporal_weight_to(wt, weight)
    plane_weight_to(w1, w_first)
    plane_weight_to(w2, w_second)
    for row in range(1, rows - 1):
        frames_to(xs, (row - 1) * pitch, own, row)
    lhs = jnp.concatenate(
        [xs[a, b * pitch : (b + rows - 4) * pitch] for b in range(3) for a in range(3)], axis=1
    )
    sums = column_taps(jnp.dot(lhs, wt[...], preferred_element_type=jnp.float32))

    tall[:pitch] = t_edge[0]
    tall[pitch : (rows - 3) * pitch] = inside(sums, masks[0]).astype(jnp.bfloat16)
    tall[(rows - 3) * pitch :] = t_edge[1]
    inner = rows - 4
    sums = column_taps(
        jnp.dot(row_taps(tall, 0, inner, pitch), w1[...], preferred_element_type=jnp.float32)
    )
    hs[...] = inside(silu(sums), masks[0]).astype(jnp.bfloat16)
    temporal = [rows_of(tall, i, 1, pitch) for i in (0, 1, inner, inner + 1)]
    for i, value in enumerate(known_rows(*temporal, w1)):
        known_h[i] = value

    sums = column_taps(
        jnp.dot(row_taps(hs, 0, inner - 2, pitch), w2[...], preferred_element_type=jnp.float32)
    )
    sums = sums + rows_of(tall, 2, inner - 2, pitch).astype(jnp.float32)
    o_mid[...] = crop(sums, frames, span)
    hidden = [rows_of(hs, i, 1, pitch) for i in (0, 1, inner - 2, inner - 1)]
    for i, value in enumerate(known_rows(*hidden, w2)):
        known_o[i] = value + temporal[i].astype(jnp.float32)


def outer_kernel(frames, masks, edges, known_h, known_o, o_mid, below, above, w1, w2, out):
    rows = out.shape[0] * out.shape[2]
    pitch = edges.shape[1]
    span = pitch // frames

    def shown(value, row):
        mask = masks[1] if row < 0 else masks[2] if row >= rows else masks[0]
        return inside(value, mask).astype(jnp.bfloat16)

    top = [
        shown(above[0].astype(jnp.float32), -2),
        shown(above[1] + edges[2], -1),
        shown(above[2] + edges[0], 0),
    ]
    end = [
        shown(below[2] + edges[1], rows - 1),
        shown(below[1] + edges[3], rows),
        shown(below[0].astype(jnp.float32), rows + 1),
    ]
    sums = outer_rows(top, end, w1, known_h)
    places = (-1, 0, 1, rows - 2, rows - 1, rows)
    hidden = [shown(silu(value), row) for value, row in zip(sums, places)]

    sums = outer_rows(hidden[:3], hidden[3:], w2, known_o)
    sums[0] = sums[0] + top[2].astype(jnp.float32)
    sums[5] = sums[5] + end[0].astype(jnp.float32)
    for value, row in zip(sums, (0, 1, 2, rows - 3, rows - 2, rows - 1)):
        out[row // 2, :, row % 2] = crop(value, frames, span)[0]
    for row in range(3, rows - 3):
        out[row // 2, :, row % 2] = o_mid[row - 3]


def per_device(frames_in, temporal_weight, first_weight, second_weight):
    tm, slabs = lax.axis_size("tm"), lax.axis_size("rows")
    planes = slabs // SLABS
    frame_count, row_count, col_count, chans = frames_in.shape
    count = tm * SLABS
    width = col_count // count
    span = width + 2 * HALO
    plane_rows = SLABS * row_count
    pitch = tm * span
    column, slab = lax.axis_index("tm"), lax.axis_index("rows")
    plane = slab // SLABS
    first_col = (column * SLABS + slab % SLABS) * width - HALO
    col = lax.broadcasted_iota(jnp.int32, (3, span, chans), 1) + first_col
    part = lax.broadcasted_iota(jnp.int32, (3, span, chans), 0)
    shown = (col >= 0) & (col < col_count)
    shown &= ((part != 1) | (plane > 0)) & ((part != 2) | (plane < planes - 1))
    masks = shown.astype(jnp.float32)
    vmem = pl.BlockSpec(memory_space=pltpu.VMEM)
    params = pltpu.CompilerParams(vmem_limit_bytes=VMEM_BYTES)

    def brain(*shape):
        return jax.ShapeDtypeStruct(shape, jnp.bfloat16)

    def held(*shape):
        return pltpu.VMEM(shape, jnp.bfloat16)

    cut = pl.pallas_call(
        windows_kernel,
        out_shape=brain(count, frame_count, row_count, span, chans),
        in_specs=[vmem],
        out_specs=vmem,
        compiler_params=params,
        name="windows",
    )(frames_in)
    cut, masks = lax.optimization_barrier((cut, masks))
    members = [[m * slabs + z * SLABS + j for m in range(tm) for j in range(SLABS)] for z in range(planes)]
    own = lax.all_to_all(
        cut, ("tm", "rows"), split_axis=0, concat_axis=0, tiled=True, axis_index_groups=members
    ).reshape(tm, SLABS, frame_count, row_count, span, chans)

    t_edge, edges, send_down, send_up = pl.pallas_call(
        edge_kernel,
        out_shape=[
            brain(2, pitch, chans),
            jax.ShapeDtypeStruct((4, pitch, chans), jnp.float32),
            brain(3, pitch, chans),
            brain(3, pitch, chans),
        ],
        in_specs=[vmem] * 3,
        out_specs=[vmem] * 4,
        scratch_shapes=[held(3, 6 * pitch, chans)],
        compiler_params=params,
        name="edge",
    )(masks, own, temporal_weight)

    reach = range(slabs - SLABS)
    above = lax.ppermute(send_up, "rows", [(r, r + SLABS) for r in reach])
    below = lax.ppermute(send_down, "rows", [(r + SLABS, r) for r in reach])

    inner = plane_rows - 4
    partial = jax.ShapeDtypeStruct((4, pitch, chans), jnp.float32)
    known_h, known_o, o_mid, w1, w2 = pl.pallas_call(
        inner_kernel,
        out_shape=[
            partial,
            partial,
            brain(inner - 2, tm, width, chans),
            brain(3 * chans, 3 * chans),
            brain(3 * chans, 3 * chans),
        ],
        in_specs=[vmem] * 6,
        out_specs=[vmem] * 5,
        scratch_shapes=[
            held(3, (inner + 2) * pitch, chans),
            held((inner + 2) * pitch, chans),
            held(inner * pitch, chans),
            held(9 * chans, 3 * chans),
        ],
        compiler_params=params,
        cost_estimate=pl.CostEstimate(flops=10**9, bytes_accessed=4 * 10**6, transcendentals=10**5),
        name="inner",
    )(masks, own, temporal_weight, t_edge, first_weight, second_weight)
    encoded = pl.pallas_call(
        lambda *refs: outer_kernel(tm, *refs),
        out_shape=brain(SLABS, tm, row_count, width, chans),
        in_specs=[vmem] * 9,
        out_specs=vmem,
        compiler_params=params,
        name="outer",
    )(masks, edges, known_h, known_o, o_mid, below, above, w1, w2)

    groups = [[z * SLABS + j for j in range(SLABS)] for z in range(planes)]
    encoded = lax.all_to_all(
        encoded, "rows", split_axis=0, concat_axis=0, tiled=True, axis_index_groups=groups
    )
    return jnp.transpose(encoded, (1, 2, 0, 3, 4)).reshape(tm, row_count, SLABS * width, chans)


def solution(mesh):
    placed = (P("tm", "rows", None, None), P(), P(), P())
    return jax.shard_map(
        per_device,
        mesh=mesh,
        in_specs=placed,
        out_specs=P(None, "rows", "tm", None),
        check_vma=False,
    )
```

```python
import jax
import jax.numpy as jnp
from jax import lax
from jax.experimental import pallas as pl
from jax.experimental.pallas import tpu as pltpu
from jax.sharding import PartitionSpec as P

SLABS = 4
HALO = 3
PLANE_ROWS = 8
WIDTH = 16
SPAN = 24
KEPT = 20
VMEM_BYTES = 32 * 1024 * 1024


def windows_kernel(frames, out):
    count = out.shape[0]
    parts = [(f, r) for f in range(frames.shape[0]) for r in range(frames.shape[1])]
    size = out.shape[1] // len(parts)
    width = size - 2 * HALO
    padded = []
    for f, r in parts:
        row = frames[f, r].astype(jnp.float32)
        edge = jnp.zeros((HALO, row.shape[1]), jnp.float32)
        padded.append(jnp.concatenate([edge, row, edge], axis=0))
    for k in range(count):
        cut = [row[k * width : k * width + size] for row in padded]
        out[k] = jnp.concatenate(cut, axis=0).astype(jnp.bfloat16)


def column_taps(sums):
    chans = sums.shape[1] // 3
    left, mid, right = sums[:, :chans], sums[:, chans : 2 * chans], sums[:, 2 * chans :]
    return mid + pltpu.roll(left, 1, 0) + pltpu.roll(right, sums.shape[0] - 1, 0)


def inside(value, mask):
    rows, chans = value.shape
    shown = value.reshape(rows // mask.shape[0], *mask.shape) * mask[...][None]
    return shown.reshape(rows, chans)


def temporal_weight_to(wt, weight):
    chans = weight.shape[3]
    for a in range(3):
        for b in range(3):
            for c in range(3):
                k = (b * 3 + a) * chans
                wt[k : k + chans, c * chans : (c + 1) * chans] = weight[a, b, c]


def plane_weight_to(wt, weight):
    chans = weight.shape[2]
    for b in range(3):
        for c in range(3):
            wt[b * chans : (b + 1) * chans, c * chans : (c + 1) * chans] = weight[b, c]


def frames_to(xs, at, own, row, rows_each):
    frames, chans = own.shape[0], own.shape[3]
    size = own.shape[2] // (2 * rows_each)

    def pick(m, f):
        part = own[m, row // rows_each].astype(jnp.float32)
        start = (f * rows_each + row % rows_each) * size
        part = part[start : start + SPAN]
        if part.shape[0] < SPAN:
            part = jnp.concatenate([part, jnp.zeros((SPAN - part.shape[0], chans), jnp.float32)], axis=0)
        return part

    for t in range(0, frames, 2):
        here = at + t * SPAN
        for a, f in ((1, 0), (2, 1)):
            pair = jnp.concatenate([pick(t, f), pick(t + 1, f)], axis=0)
            xs[a, here : here + 2 * SPAN] = pair.astype(jnp.bfloat16)
        before = pick(t - 1, 1) if t else jnp.zeros((SPAN, chans), jnp.float32)
        pair = jnp.concatenate([before, pick(t, 1)], axis=0)
        xs[0, here : here + 2 * SPAN] = pair.astype(jnp.bfloat16)


def silu(value):
    return value * (0.5 * jnp.tanh(0.5 * value) + 0.5)


def rows_of(ref, first, count, pitch):
    return ref[first * pitch : (first + count) * pitch]


def row_taps(ref, first, count, pitch):
    return jnp.concatenate([rows_of(ref, first + b, count, pitch) for b in range(3)], axis=1)


def temporal_taps(weight, row_taps):
    return jnp.concatenate(
        [
            jnp.concatenate([weight[a, b, c] for c in range(3)], axis=1)
            for b in row_taps
            for a in range(3)
        ],
        axis=0,
    )


def pack(value):
    kept = [value[at + 1 : at + 1 + KEPT] for at in range(0, value.shape[0], SPAN)]
    return jnp.concatenate(kept, axis=0).astype(jnp.bfloat16)


def unpack(packed):
    value = packed.astype(jnp.float32)
    before = jnp.zeros((1, value.shape[1]), jnp.float32)
    after = jnp.zeros((SPAN - KEPT - 1, value.shape[1]), jnp.float32)
    parts = []
    for at in range(0, value.shape[0], KEPT):
        parts += [before, value[at : at + KEPT], after]
    return jnp.concatenate(parts, axis=0)


def edge_kernel(masks, own, weight, t_edge, edges, send_down, send_up, xs):
    frames, span, chans = own.shape[0], SPAN, own.shape[3]
    rows_each = PLANE_ROWS // own.shape[1]
    rows = own.shape[1] * rows_each
    pitch = frames * span

    for i in range(3):
        frames_to(xs, i * pitch, own, i, rows_each)
        frames_to(xs, (3 + i) * pitch, own, rows - 3 + i, rows_each)

    def taps_of(i):
        return jnp.concatenate([xs[a, i * pitch : (i + 1) * pitch] for a in range(3)], axis=1)

    def dot(lhs, rhs):
        return column_taps(jnp.dot(lhs, rhs, preferred_element_type=jnp.float32))

    deep = 3 * chans
    x = [taps_of(i) for i in range(6)]
    low = dot(
        jnp.concatenate([jnp.concatenate(x[0:2], axis=1), jnp.concatenate(x[1:3], axis=1)], axis=0),
        temporal_taps(weight, (1, 2)),
    )
    high = dot(
        jnp.concatenate([jnp.concatenate(x[3:5], axis=1), jnp.concatenate(x[4:6], axis=1)], axis=0),
        temporal_taps(weight, (0, 1)),
    )
    outer = jnp.dot(
        jnp.concatenate([x[0], x[5]], axis=0),
        jnp.concatenate([temporal_taps(weight, (b,)) for b in (0, 2)], axis=1),
        preferred_element_type=jnp.float32,
    )
    upper, lower = column_taps(outer[:, :deep]), column_taps(outer[:, deep:])
    first, last = low[:pitch], high[pitch:]
    before, after = lower[:pitch], upper[pitch:]
    edges[0], edges[1], edges[2], edges[3] = first, last, before, after
    near = inside(low[pitch:] + upper[:pitch], masks[0])
    far = inside(high[:pitch] + lower[pitch:], masks[0])
    t_edge[0], t_edge[1] = near.astype(jnp.bfloat16), far.astype(jnp.bfloat16)
    for i, value in enumerate((far, last, after)):
        send_up[i] = pack(value)
    for i, value in enumerate((near, first, before)):
        send_down[i] = pack(value)


def crop(value, frames, span):
    shape = (value.shape[0] // (frames * span), frames, span, value.shape[1])
    return value.reshape(shape)[:, :, HALO : HALO + WIDTH].astype(jnp.bfloat16)


def dot_taps(lhs, rhs):
    lhs = jnp.concatenate([jnp.concatenate(blocks, axis=1) for blocks in lhs], axis=0)
    return column_taps(jnp.dot(lhs, rhs, preferred_element_type=jnp.float32))


def split_rows(value, pitch):
    return [value[at : at + pitch] for at in range(0, value.shape[0], pitch)]


def known_rows(first, second, before_last, last, weight):
    pitch, chans = first.shape
    none = jnp.zeros_like(first)
    top = dot_taps([[none, first], [first, second]], weight[chans:])
    end = dot_taps([[before_last, last], [last, none]], weight[: 2 * chans])
    return split_rows(top, pitch) + split_rows(end, pitch)


def outer_rows(top, end, weight, known):
    pitch, chans = top[0].shape
    none = jnp.zeros_like(top[0])
    first, last = split_rows(dot_taps([top, end], weight[...]), pitch)
    near = split_rows(dot_taps([top[1:], [top[2], none]], weight[: 2 * chans]), pitch)
    far = split_rows(dot_taps([[none, end[0]], end[:2]], weight[chans:]), pitch)
    inner = [value + known[i] for i, value in enumerate(near + far)]
    return [first, *inner, last]


def inner_kernel(
    masks, own, weight, t_edge, w_first, w_second, known_h, known_o, o_mid, w1, w2,
    xs, tall, hs, wt,
):
    frames, span = own.shape[0], SPAN
    rows_each = PLANE_ROWS // own.shape[1]
    rows = own.shape[1] * rows_each
    pitch = frames * span
    temporal_weight_to(wt, weight)
    plane_weight_to(w1, w_first)
    plane_weight_to(w2, w_second)
    for row in range(1, rows - 1):
        frames_to(xs, (row - 1) * pitch, own, row, rows_each)
    lhs = jnp.concatenate(
        [xs[a, b * pitch : (b + rows - 4) * pitch] for b in range(3) for a in range(3)], axis=1
    )
    sums = column_taps(jnp.dot(lhs, wt[...], preferred_element_type=jnp.float32))

    tall[:pitch] = t_edge[0]
    tall[pitch : (rows - 3) * pitch] = inside(sums, masks[0]).astype(jnp.bfloat16)
    tall[(rows - 3) * pitch :] = t_edge[1]
    inner = rows - 4
    sums = column_taps(
        jnp.dot(row_taps(tall, 0, inner, pitch), w1[...], preferred_element_type=jnp.float32)
    )
    hs[...] = inside(silu(sums), masks[0]).astype(jnp.bfloat16)
    temporal = [rows_of(tall, i, 1, pitch) for i in (0, 1, inner, inner + 1)]
    for i, value in enumerate(known_rows(*temporal, w1)):
        known_h[i] = value

    sums = column_taps(
        jnp.dot(row_taps(hs, 0, inner - 2, pitch), w2[...], preferred_element_type=jnp.float32)
    )
    sums = sums + rows_of(tall, 2, inner - 2, pitch).astype(jnp.float32)
    o_mid[...] = crop(sums, frames, span)
    hidden = [rows_of(hs, i, 1, pitch) for i in (0, 1, inner - 2, inner - 1)]
    for i, value in enumerate(known_rows(*hidden, w2)):
        known_o[i] = value + temporal[i].astype(jnp.float32)


def outer_kernel(frames, masks, edges, known_h, known_o, o_mid, below, above, w1, w2, out):
    rows = out.shape[0] * out.shape[2]
    pitch = edges.shape[1]
    span = pitch // frames

    def shown(value, row):
        mask = masks[1] if row < 0 else masks[2] if row >= rows else masks[0]
        return inside(value, mask).astype(jnp.bfloat16)

    top = [
        shown(unpack(above[0]), -2),
        shown(unpack(above[1]) + edges[2], -1),
        shown(unpack(above[2]) + edges[0], 0),
    ]
    end = [
        shown(unpack(below[2]) + edges[1], rows - 1),
        shown(unpack(below[1]) + edges[3], rows),
        shown(unpack(below[0]), rows + 1),
    ]
    sums = outer_rows(top, end, w1, known_h)
    places = (-1, 0, 1, rows - 2, rows - 1, rows)
    hidden = [shown(silu(value), row) for value, row in zip(sums, places)]

    sums = outer_rows(hidden[:3], hidden[3:], w2, known_o)
    sums[0] = sums[0] + top[2].astype(jnp.float32)
    sums[5] = sums[5] + end[0].astype(jnp.float32)
    for value, row in zip(sums, (0, 1, 2, rows - 3, rows - 2, rows - 1)):
        out[row // 2, :, row % 2] = crop(value, frames, span)[0]
    for row in range(3, rows - 3):
        out[row // 2, :, row % 2] = o_mid[row - 3]


def per_device(frames_in, temporal_weight, first_weight, second_weight):
    tm, slabs = lax.axis_size("tm"), lax.axis_size("rows")
    planes = slabs // SLABS
    frame_count, row_count, col_count, chans = frames_in.shape
    count = tm * SLABS
    width = col_count // count
    span = SPAN
    size = width + 2 * HALO
    plane_rows = SLABS * row_count
    pitch = tm * span
    column, slab = lax.axis_index("tm"), lax.axis_index("rows")
    plane = slab // SLABS
    first_col = (column * SLABS + slab % SLABS) * width - HALO
    col = lax.broadcasted_iota(jnp.int32, (3, span, chans), 1) + first_col
    part = lax.broadcasted_iota(jnp.int32, (3, span, chans), 0)
    shown = (col >= 0) & (col < col_count)
    shown &= ((part != 1) | (plane > 0)) & ((part != 2) | (plane < planes - 1))
    masks = shown.astype(jnp.float32)
    vmem = pl.BlockSpec(memory_space=pltpu.VMEM)
    params = pltpu.CompilerParams(vmem_limit_bytes=VMEM_BYTES)

    def brain(*shape):
        return jax.ShapeDtypeStruct(shape, jnp.bfloat16)

    def held(*shape):
        return pltpu.VMEM(shape, jnp.bfloat16)

    cut = pl.pallas_call(
        windows_kernel,
        out_shape=brain(count, frame_count * row_count * size, chans),
        in_specs=[vmem],
        out_specs=vmem,
        compiler_params=params,
        name="windows",
    )(frames_in)
    cut, masks = lax.optimization_barrier((cut, masks))
    members = [[m * slabs + z * SLABS + j for m in range(tm) for j in range(SLABS)] for z in range(planes)]
    own = lax.all_to_all(
        cut, ("tm", "rows"), split_axis=0, concat_axis=0, tiled=True, axis_index_groups=members
    ).reshape(tm, SLABS, frame_count * row_count * size, chans)

    t_edge, edges, send_down, send_up = pl.pallas_call(
        edge_kernel,
        out_shape=[
            brain(2, pitch, chans),
            jax.ShapeDtypeStruct((4, pitch, chans), jnp.float32),
            brain(3, tm * KEPT, chans),
            brain(3, tm * KEPT, chans),
        ],
        in_specs=[vmem] * 3,
        out_specs=[vmem] * 4,
        scratch_shapes=[held(3, 6 * pitch, chans)],
        compiler_params=params,
        name="edge",
    )(masks, own, temporal_weight)

    reach = range(slabs - SLABS)
    above = lax.ppermute(send_up, "rows", [(r, r + SLABS) for r in reach])
    below = lax.ppermute(send_down, "rows", [(r + SLABS, r) for r in reach])

    inner = plane_rows - 4
    partial = jax.ShapeDtypeStruct((4, pitch, chans), jnp.float32)
    known_h, known_o, o_mid, w1, w2 = pl.pallas_call(
        inner_kernel,
        out_shape=[
            partial,
            partial,
            brain(inner - 2, tm, width, chans),
            brain(3 * chans, 3 * chans),
            brain(3 * chans, 3 * chans),
        ],
        in_specs=[vmem] * 6,
        out_specs=[vmem] * 5,
        scratch_shapes=[
            held(3, (inner + 2) * pitch, chans),
            held((inner + 2) * pitch, chans),
            held(inner * pitch, chans),
            held(9 * chans, 3 * chans),
        ],
        compiler_params=params,
        cost_estimate=pl.CostEstimate(flops=10**9, bytes_accessed=4 * 10**6, transcendentals=10**5),
        name="inner",
    )(masks, own, temporal_weight, t_edge, first_weight, second_weight)
    encoded = pl.pallas_call(
        lambda *refs: outer_kernel(tm, *refs),
        out_shape=brain(SLABS, tm, row_count, width, chans),
        in_specs=[vmem] * 9,
        out_specs=vmem,
        compiler_params=params,
        name="outer",
    )(masks, edges, known_h, known_o, o_mid, below, above, w1, w2)

    groups = [[z * SLABS + j for j in range(SLABS)] for z in range(planes)]
    encoded = lax.all_to_all(
        encoded, "rows", split_axis=0, concat_axis=0, tiled=True, axis_index_groups=groups
    )
    return jnp.transpose(encoded, (1, 2, 0, 3, 4)).reshape(tm, row_count, SLABS * width, chans)


def solution(mesh):
    placed = (P("tm", "rows", None, None), P(), P(), P())
    return jax.shard_map(
        per_device,
        mesh=mesh,
        in_specs=placed,
        out_specs=P(None, "rows", "tm", None),
        check_vma=False,
    )
```

```python
import jax
import jax.numpy as jnp
from jax import lax
from jax.experimental import pallas as pl
from jax.experimental.pallas import tpu as pltpu
from jax.sharding import PartitionSpec as P

SLABS = 4
HALO = 3
PLANE_ROWS = 8
WIDTH = 16
SPAN = 24
KEPT = 20
VMEM_BYTES = 32 * 1024 * 1024


def windows_kernel(frames, out):
    count = out.shape[0]
    parts = [(f, r) for f in range(frames.shape[0]) for r in range(frames.shape[1])]
    size = out.shape[1] // len(parts)
    width = size - 2 * HALO
    padded = []
    for f, r in parts:
        row = frames[f, r].astype(jnp.float32)
        edge = jnp.zeros((HALO, row.shape[1]), jnp.float32)
        padded.append(jnp.concatenate([edge, row, edge], axis=0))
    for k in range(count):
        cut = [row[k * width : k * width + size] for row in padded]
        out[k] = jnp.concatenate(cut, axis=0).astype(jnp.bfloat16)


def column_taps(sums):
    chans = sums.shape[1] // 3
    left, mid, right = sums[:, :chans], sums[:, chans : 2 * chans], sums[:, 2 * chans :]
    return mid + pltpu.roll(left, 1, 0) + pltpu.roll(right, sums.shape[0] - 1, 0)


def inside(value, mask):
    rows, chans = value.shape
    shown = value.reshape(rows // mask.shape[0], *mask.shape) * mask[...][None]
    return shown.reshape(rows, chans)


def temporal_weight_to(wt, weight):
    chans = weight.shape[3]
    for a in range(3):
        for b in range(3):
            for c in range(3):
                k = (b * 3 + a) * chans
                wt[k : k + chans, c * chans : (c + 1) * chans] = weight[a, b, c]


def plane_weight_to(wt, weight):
    chans = weight.shape[2]
    for b in range(3):
        for c in range(3):
            wt[b * chans : (b + 1) * chans, c * chans : (c + 1) * chans] = weight[b, c]


def frames_to(xs, at, own, row, rows_each):
    frames, chans = own.shape[0], own.shape[3]
    size = own.shape[2] // (2 * rows_each)

    def pick(m, f):
        part = own[m, row // rows_each].astype(jnp.float32)
        start = (f * rows_each + row % rows_each) * size
        part = part[start : start + SPAN]
        if part.shape[0] < SPAN:
            part = jnp.concatenate([part, jnp.zeros((SPAN - part.shape[0], chans), jnp.float32)], axis=0)
        return part

    for t in range(0, frames, 2):
        here = at + t * SPAN
        for a, f in ((1, 0), (2, 1)):
            pair = jnp.concatenate([pick(t, f), pick(t + 1, f)], axis=0)
            xs[a, here : here + 2 * SPAN] = pair.astype(jnp.bfloat16)
        before = pick(t - 1, 1) if t else jnp.zeros((SPAN, chans), jnp.float32)
        pair = jnp.concatenate([before, pick(t, 1)], axis=0)
        xs[0, here : here + 2 * SPAN] = pair.astype(jnp.bfloat16)


def silu(value):
    return value * (0.5 * jnp.tanh(0.5 * value) + 0.5)


def rows_of(ref, first, count, pitch):
    return ref[first * pitch : (first + count) * pitch]


def row_taps(ref, first, count, pitch):
    return jnp.concatenate([rows_of(ref, first + b, count, pitch) for b in range(3)], axis=1)


def temporal_taps(weight, row_taps):
    return jnp.concatenate(
        [
            jnp.concatenate([weight[a, b, c] for c in range(3)], axis=1)
            for b in row_taps
            for a in range(3)
        ],
        axis=0,
    )


def halves(value):
    high = value.astype(jnp.bfloat16).astype(jnp.float32)
    return high, value - high


def pack(value):
    kept = [value[at + 1 : at + 1 + KEPT] for at in range(0, value.shape[0], SPAN)]
    return jnp.concatenate(kept, axis=0).astype(jnp.bfloat16)


def unpack(packed):
    value = packed.astype(jnp.float32)
    before = jnp.zeros((1, value.shape[1]), jnp.float32)
    after = jnp.zeros((SPAN - KEPT - 1, value.shape[1]), jnp.float32)
    parts = []
    for at in range(0, value.shape[0], KEPT):
        parts += [before, value[at : at + KEPT], after]
    return jnp.concatenate(parts, axis=0)


def edge_kernel(masks, own, weight, t_edge, edges, send_down, send_up, xs):
    frames, span, chans = own.shape[0], SPAN, own.shape[3]
    rows_each = PLANE_ROWS // own.shape[1]
    rows = own.shape[1] * rows_each
    pitch = frames * span

    for i in range(3):
        frames_to(xs, i * pitch, own, i, rows_each)
        frames_to(xs, (3 + i) * pitch, own, rows - 3 + i, rows_each)

    def taps_of(i):
        return jnp.concatenate([xs[a, i * pitch : (i + 1) * pitch] for a in range(3)], axis=1)

    def dot(lhs, rhs):
        return column_taps(jnp.dot(lhs, rhs, preferred_element_type=jnp.float32))

    deep = 3 * chans
    x = [taps_of(i) for i in range(6)]
    low = dot(
        jnp.concatenate([jnp.concatenate(x[0:2], axis=1), jnp.concatenate(x[1:3], axis=1)], axis=0),
        temporal_taps(weight, (1, 2)),
    )
    high = dot(
        jnp.concatenate([jnp.concatenate(x[3:5], axis=1), jnp.concatenate(x[4:6], axis=1)], axis=0),
        temporal_taps(weight, (0, 1)),
    )
    outer = jnp.dot(
        jnp.concatenate([x[0], x[5]], axis=0),
        jnp.concatenate([temporal_taps(weight, (b,)) for b in (0, 2)], axis=1),
        preferred_element_type=jnp.float32,
    )
    upper, lower = column_taps(outer[:, :deep]), column_taps(outer[:, deep:])
    first, last = low[:pitch], high[pitch:]
    before, after = lower[:pitch], upper[pitch:]
    edges[0], edges[1], edges[2], edges[3] = first, last, before, after
    near = inside(low[pitch:] + upper[:pitch], masks[0])
    far = inside(high[:pitch] + lower[pitch:], masks[0])
    t_edge[0], t_edge[1] = near.astype(jnp.bfloat16), far.astype(jnp.bfloat16)
    for i, value in enumerate((far, *halves(last), *halves(after))):
        send_up[i] = pack(value)
    for i, value in enumerate((near, *halves(first), *halves(before))):
        send_down[i] = pack(value)


def crop(value, frames, span):
    shape = (value.shape[0] // (frames * span), frames, span, value.shape[1])
    return value.reshape(shape)[:, :, HALO : HALO + WIDTH].astype(jnp.bfloat16)


def dot_taps(lhs, rhs):
    lhs = jnp.concatenate([jnp.concatenate(blocks, axis=1) for blocks in lhs], axis=0)
    return column_taps(jnp.dot(lhs, rhs, preferred_element_type=jnp.float32))


def split_rows(value, pitch):
    return [value[at : at + pitch] for at in range(0, value.shape[0], pitch)]


def known_rows(first, second, before_last, last, weight):
    pitch, chans = first.shape
    none = jnp.zeros_like(first)
    top = dot_taps([[none, first], [first, second]], weight[chans:])
    end = dot_taps([[before_last, last], [last, none]], weight[: 2 * chans])
    return split_rows(top, pitch) + split_rows(end, pitch)


def outer_rows(top, end, weight, known):
    pitch, chans = top[0].shape
    none = jnp.zeros_like(top[0])
    first, last = split_rows(dot_taps([top, end], weight[...]), pitch)
    near = split_rows(dot_taps([top[1:], [top[2], none]], weight[: 2 * chans]), pitch)
    far = split_rows(dot_taps([[none, end[0]], end[:2]], weight[chans:]), pitch)
    inner = [value + known[i] for i, value in enumerate(near + far)]
    return [first, *inner, last]


def inner_kernel(
    masks, own, weight, t_edge, w_first, w_second, known_h, known_o, o_mid, w1, w2,
    xs, tall, hs, wt,
):
    frames, span = own.shape[0], SPAN
    rows_each = PLANE_ROWS // own.shape[1]
    rows = own.shape[1] * rows_each
    pitch = frames * span
    temporal_weight_to(wt, weight)
    plane_weight_to(w1, w_first)
    plane_weight_to(w2, w_second)
    for row in range(1, rows - 1):
        frames_to(xs, (row - 1) * pitch, own, row, rows_each)
    lhs = jnp.concatenate(
        [xs[a, b * pitch : (b + rows - 4) * pitch] for b in range(3) for a in range(3)], axis=1
    )
    sums = column_taps(jnp.dot(lhs, wt[...], preferred_element_type=jnp.float32))

    tall[:pitch] = t_edge[0]
    tall[pitch : (rows - 3) * pitch] = inside(sums, masks[0]).astype(jnp.bfloat16)
    tall[(rows - 3) * pitch :] = t_edge[1]
    inner = rows - 4
    sums = column_taps(
        jnp.dot(row_taps(tall, 0, inner, pitch), w1[...], preferred_element_type=jnp.float32)
    )
    hs[...] = inside(silu(sums), masks[0]).astype(jnp.bfloat16)
    temporal = [rows_of(tall, i, 1, pitch) for i in (0, 1, inner, inner + 1)]
    for i, value in enumerate(known_rows(*temporal, w1)):
        known_h[i] = value

    sums = column_taps(
        jnp.dot(row_taps(hs, 0, inner - 2, pitch), w2[...], preferred_element_type=jnp.float32)
    )
    sums = sums + rows_of(tall, 2, inner - 2, pitch).astype(jnp.float32)
    o_mid[...] = crop(sums, frames, span)
    hidden = [rows_of(hs, i, 1, pitch) for i in (0, 1, inner - 2, inner - 1)]
    for i, value in enumerate(known_rows(*hidden, w2)):
        known_o[i] = value + temporal[i].astype(jnp.float32)


def outer_kernel(frames, masks, edges, known_h, known_o, o_mid, below, above, w1, w2, out):
    rows = out.shape[0] * out.shape[2]
    pitch = edges.shape[1]
    span = pitch // frames

    def shown(value, row):
        mask = masks[1] if row < 0 else masks[2] if row >= rows else masks[0]
        return inside(value, mask).astype(jnp.bfloat16)

    top = [
        shown(unpack(above[0]), -2),
        shown(unpack(above[1]) + unpack(above[2]) + edges[2], -1),
        shown(unpack(above[3]) + unpack(above[4]) + edges[0], 0),
    ]
    end = [
        shown(unpack(below[3]) + unpack(below[4]) + edges[1], rows - 1),
        shown(unpack(below[1]) + unpack(below[2]) + edges[3], rows),
        shown(unpack(below[0]), rows + 1),
    ]
    sums = outer_rows(top, end, w1, known_h)
    places = (-1, 0, 1, rows - 2, rows - 1, rows)
    hidden = [shown(silu(value), row) for value, row in zip(sums, places)]

    sums = outer_rows(hidden[:3], hidden[3:], w2, known_o)
    sums[0] = sums[0] + top[2].astype(jnp.float32)
    sums[5] = sums[5] + end[0].astype(jnp.float32)
    for value, row in zip(sums, (0, 1, 2, rows - 3, rows - 2, rows - 1)):
        out[row // 2, :, row % 2] = crop(value, frames, span)[0]
    for row in range(3, rows - 3):
        out[row // 2, :, row % 2] = o_mid[row - 3]


def per_device(frames_in, temporal_weight, first_weight, second_weight):
    tm, slabs = lax.axis_size("tm"), lax.axis_size("rows")
    planes = slabs // SLABS
    frame_count, row_count, col_count, chans = frames_in.shape
    count = tm * SLABS
    width = col_count // count
    span = SPAN
    size = width + 2 * HALO
    plane_rows = SLABS * row_count
    pitch = tm * span
    column, slab = lax.axis_index("tm"), lax.axis_index("rows")
    plane = slab // SLABS
    first_col = (column * SLABS + slab % SLABS) * width - HALO
    col = lax.broadcasted_iota(jnp.int32, (3, span, chans), 1) + first_col
    part = lax.broadcasted_iota(jnp.int32, (3, span, chans), 0)
    shown = (col >= 0) & (col < col_count)
    shown &= ((part != 1) | (plane > 0)) & ((part != 2) | (plane < planes - 1))
    masks = shown.astype(jnp.float32)
    vmem = pl.BlockSpec(memory_space=pltpu.VMEM)
    params = pltpu.CompilerParams(vmem_limit_bytes=VMEM_BYTES)

    def brain(*shape):
        return jax.ShapeDtypeStruct(shape, jnp.bfloat16)

    def held(*shape):
        return pltpu.VMEM(shape, jnp.bfloat16)

    cut = pl.pallas_call(
        windows_kernel,
        out_shape=brain(count, frame_count * row_count * size, chans),
        in_specs=[vmem],
        out_specs=vmem,
        compiler_params=params,
        name="windows",
    )(frames_in)
    cut, masks = lax.optimization_barrier((cut, masks))
    members = [[m * slabs + z * SLABS + j for m in range(tm) for j in range(SLABS)] for z in range(planes)]
    own = lax.all_to_all(
        cut, ("tm", "rows"), split_axis=0, concat_axis=0, tiled=True, axis_index_groups=members
    ).reshape(tm, SLABS, frame_count * row_count * size, chans)

    t_edge, edges, send_down, send_up = pl.pallas_call(
        edge_kernel,
        out_shape=[
            brain(2, pitch, chans),
            jax.ShapeDtypeStruct((4, pitch, chans), jnp.float32),
            brain(5, tm * KEPT, chans),
            brain(5, tm * KEPT, chans),
        ],
        in_specs=[vmem] * 3,
        out_specs=[vmem] * 4,
        scratch_shapes=[held(3, 6 * pitch, chans)],
        compiler_params=params,
        name="edge",
    )(masks, own, temporal_weight)

    reach = range(slabs - SLABS)
    above = lax.ppermute(send_up, "rows", [(r, r + SLABS) for r in reach])
    below = lax.ppermute(send_down, "rows", [(r + SLABS, r) for r in reach])

    inner = plane_rows - 4
    partial = jax.ShapeDtypeStruct((4, pitch, chans), jnp.float32)
    known_h, known_o, o_mid, w1, w2 = pl.pallas_call(
        inner_kernel,
        out_shape=[
            partial,
            partial,
            brain(inner - 2, tm, width, chans),
            brain(3 * chans, 3 * chans),
            brain(3 * chans, 3 * chans),
        ],
        in_specs=[vmem] * 6,
        out_specs=[vmem] * 5,
        scratch_shapes=[
            held(3, (inner + 2) * pitch, chans),
            held((inner + 2) * pitch, chans),
            held(inner * pitch, chans),
            held(9 * chans, 3 * chans),
        ],
        compiler_params=params,
        cost_estimate=pl.CostEstimate(flops=10**9, bytes_accessed=4 * 10**6, transcendentals=10**5),
        name="inner",
    )(masks, own, temporal_weight, t_edge, first_weight, second_weight)
    encoded = pl.pallas_call(
        lambda *refs: outer_kernel(tm, *refs),
        out_shape=brain(SLABS, tm, row_count, width, chans),
        in_specs=[vmem] * 9,
        out_specs=vmem,
        compiler_params=params,
        name="outer",
    )(masks, edges, known_h, known_o, o_mid, below, above, w1, w2)

    groups = [[z * SLABS + j for j in range(SLABS)] for z in range(planes)]
    encoded = lax.all_to_all(
        encoded, "rows", split_axis=0, concat_axis=0, tiled=True, axis_index_groups=groups
    )
    return jnp.transpose(encoded, (1, 2, 0, 3, 4)).reshape(tm, row_count, SLABS * width, chans)


def solution(mesh):
    placed = (P("tm", "rows", None, None), P(), P(), P())
    return jax.shard_map(
        per_device,
        mesh=mesh,
        in_specs=placed,
        out_specs=P(None, "rows", "tm", None),
        check_vma=False,
    )
```

```python
import jax
import jax.numpy as jnp
from jax import lax
from jax.experimental import pallas as pl
from jax.experimental.pallas import tpu as pltpu
from jax.sharding import PartitionSpec as P

SLABS = 4
HALO = 3
PLANE_ROWS = 8
WIDTH = 16
SPAN = 24
KEPT = 20
VMEM_BYTES = 32 * 1024 * 1024


def windows_kernel(frames, out):
    count = out.shape[0]
    parts = [(f, r) for f in range(frames.shape[0]) for r in range(frames.shape[1])]
    size = out.shape[1] // len(parts)
    width = size - 2 * HALO
    padded = []
    for f, r in parts:
        row = frames[f, r].astype(jnp.float32)
        edge = jnp.zeros((HALO, row.shape[1]), jnp.float32)
        padded.append(jnp.concatenate([edge, row, edge], axis=0))
    for k in range(count):
        cut = [row[k * width : k * width + size] for row in padded]
        out[k] = jnp.concatenate(cut, axis=0).astype(jnp.bfloat16)


def column_taps(sums):
    chans = sums.shape[1] // 3
    left, mid, right = sums[:, :chans], sums[:, chans : 2 * chans], sums[:, 2 * chans :]
    return mid + pltpu.roll(left, 1, 0) + pltpu.roll(right, sums.shape[0] - 1, 0)


def inside(value, mask):
    rows, chans = value.shape
    shown = value.reshape(rows // mask.shape[0], *mask.shape) * mask[...][None]
    return shown.reshape(rows, chans)


def temporal_weight_to(wt, weight):
    chans = weight.shape[3]
    for a in range(3):
        for b in range(3):
            for c in range(3):
                k = (b * 3 + a) * chans
                wt[k : k + chans, c * chans : (c + 1) * chans] = weight[a, b, c]


def plane_weight_to(wt, weight):
    chans = weight.shape[2]
    for b in range(3):
        for c in range(3):
            wt[b * chans : (b + 1) * chans, c * chans : (c + 1) * chans] = weight[b, c]


def frames_to(xs, at, own, row, rows_each):
    frames, chans = own.shape[0], own.shape[3]
    size = own.shape[2] // (2 * rows_each)

    def pick(m, f):
        part = own[m, row // rows_each].astype(jnp.float32)
        start = (f * rows_each + row % rows_each) * size
        part = part[start : start + SPAN]
        if part.shape[0] < SPAN:
            part = jnp.concatenate([part, jnp.zeros((SPAN - part.shape[0], chans), jnp.float32)], axis=0)
        return part

    for t in range(0, frames, 2):
        here = at + t * SPAN
        for a, f in ((1, 0), (2, 1)):
            pair = jnp.concatenate([pick(t, f), pick(t + 1, f)], axis=0)
            xs[a, here : here + 2 * SPAN] = pair.astype(jnp.bfloat16)
        before = pick(t - 1, 1) if t else jnp.zeros((SPAN, chans), jnp.float32)
        pair = jnp.concatenate([before, pick(t, 1)], axis=0)
        xs[0, here : here + 2 * SPAN] = pair.astype(jnp.bfloat16)


def silu(value):
    return value * (0.5 * jnp.tanh(0.5 * value) + 0.5)


def rows_of(ref, first, count, pitch):
    return ref[first * pitch : (first + count) * pitch]


def row_taps(ref, first, count, pitch):
    return jnp.concatenate([rows_of(ref, first + b, count, pitch) for b in range(3)], axis=1)


def temporal_taps(weight, row_taps):
    return jnp.concatenate(
        [
            jnp.concatenate([weight[a, b, c] for c in range(3)], axis=1)
            for b in row_taps
            for a in range(3)
        ],
        axis=0,
    )


def pack(value):
    kept = [value[at + 1 : at + 1 + KEPT] for at in range(0, value.shape[0], SPAN)]
    return jnp.concatenate(kept, axis=0).astype(jnp.bfloat16)


def unpack(packed):
    value = packed.astype(jnp.float32)
    before = jnp.zeros((1, value.shape[1]), jnp.float32)
    after = jnp.zeros((SPAN - KEPT - 1, value.shape[1]), jnp.float32)
    parts = []
    for at in range(0, value.shape[0], KEPT):
        parts += [before, value[at : at + KEPT], after]
    return jnp.concatenate(parts, axis=0)


def edge_kernel(masks, own, weight, t_edge, edges, send_down, send_up, xs):
    frames, span, chans = own.shape[0], SPAN, own.shape[3]
    rows_each = PLANE_ROWS // own.shape[1]
    rows = own.shape[1] * rows_each
    pitch = frames * span

    for i in range(3):
        frames_to(xs, i * pitch, own, i, rows_each)
        frames_to(xs, (3 + i) * pitch, own, rows - 3 + i, rows_each)

    def taps_of(i):
        return jnp.concatenate([xs[a, i * pitch : (i + 1) * pitch] for a in range(3)], axis=1)

    deep = 3 * chans
    x = [taps_of(i) for i in range(6)]
    sums = jnp.dot(
        jnp.concatenate([jnp.concatenate(pair, axis=1) for pair in (x[0:2], x[4:6])], axis=0),
        jnp.concatenate([temporal_taps(weight, taps) for taps in ((1, 2), (0, 1))], axis=1),
        preferred_element_type=jnp.float32,
    )
    lower, upper = column_taps(sums[:, :deep]), column_taps(sums[:, deep:])
    first, last = lower[:pitch], upper[pitch:]
    second, before = split_rows(dot_taps([[x[2]], [x[0]]], temporal_taps(weight, (2,))), pitch)
    third, after = split_rows(dot_taps([[x[3]], [x[5]]], temporal_taps(weight, (0,))), pitch)
    edges[0], edges[1], edges[2], edges[3] = first, last, before, after
    near = inside(upper[:pitch] + second, masks[0])
    far = inside(lower[pitch:] + third, masks[0])
    t_edge[0], t_edge[1] = near.astype(jnp.bfloat16), far.astype(jnp.bfloat16)
    for i, value in enumerate((far, last, after)):
        send_up[i] = pack(value)
    for i, value in enumerate((near, first, before)):
        send_down[i] = pack(value)


def crop(value, frames, span):
    shape = (value.shape[0] // (frames * span), frames, span, value.shape[1])
    return value.reshape(shape)[:, :, HALO : HALO + WIDTH].astype(jnp.bfloat16)


def dot_taps(lhs, rhs):
    lhs = jnp.concatenate([jnp.concatenate(blocks, axis=1) for blocks in lhs], axis=0)
    return column_taps(jnp.dot(lhs, rhs, preferred_element_type=jnp.float32))


def split_rows(value, pitch):
    return [value[at : at + pitch] for at in range(0, value.shape[0], pitch)]


def known_rows(first, second, before_last, last, weight):
    pitch, chans = first.shape
    none = jnp.zeros_like(first)
    top = dot_taps([[none, first], [first, second]], weight[chans:])
    end = dot_taps([[before_last, last], [last, none]], weight[: 2 * chans])
    return split_rows(top, pitch) + split_rows(end, pitch)


def top_rows(rows, weight, known):
    none, chans = jnp.zeros_like(rows[0]), rows[0].shape[1]
    first = dot_taps([rows], weight[...])
    near = split_rows(dot_taps([rows[1:], [rows[2], none]], weight[: 2 * chans]), none.shape[0])
    return [first, near[0] + known[0], near[1] + known[1]]


def end_rows(rows, weight, known):
    none, chans = jnp.zeros_like(rows[0]), rows[0].shape[1]
    last = dot_taps([rows], weight[...])
    far = split_rows(dot_taps([[none, rows[0]], rows[:2]], weight[chans:]), none.shape[0])
    return [far[0] + known[2], far[1] + known[3], last]


def inner_kernel(
    masks, own, weight, t_edge, w_first, w_second, known_h, known_o, o_mid, w1, w2,
    xs, tall, hs, wt,
):
    frames, span = own.shape[0], SPAN
    rows_each = PLANE_ROWS // own.shape[1]
    rows = own.shape[1] * rows_each
    pitch = frames * span
    temporal_weight_to(wt, weight)
    plane_weight_to(w1, w_first)
    plane_weight_to(w2, w_second)
    for row in range(1, rows - 1):
        frames_to(xs, (row - 1) * pitch, own, row, rows_each)
    lhs = jnp.concatenate(
        [xs[a, b * pitch : (b + rows - 4) * pitch] for b in range(3) for a in range(3)], axis=1
    )
    sums = column_taps(jnp.dot(lhs, wt[...], preferred_element_type=jnp.float32))

    tall[:pitch] = t_edge[0]
    tall[pitch : (rows - 3) * pitch] = inside(sums, masks[0]).astype(jnp.bfloat16)
    tall[(rows - 3) * pitch :] = t_edge[1]
    inner = rows - 4
    sums = column_taps(
        jnp.dot(row_taps(tall, 0, inner, pitch), w1[...], preferred_element_type=jnp.float32)
    )
    hs[...] = inside(silu(sums), masks[0]).astype(jnp.bfloat16)
    temporal = [rows_of(tall, i, 1, pitch) for i in (0, 1, inner, inner + 1)]
    for i, value in enumerate(known_rows(*temporal, w1)):
        known_h[i] = value

    sums = column_taps(
        jnp.dot(row_taps(hs, 0, inner - 2, pitch), w2[...], preferred_element_type=jnp.float32)
    )
    sums = sums + rows_of(tall, 2, inner - 2, pitch).astype(jnp.float32)
    o_mid[...] = crop(sums, frames, span)
    hidden = [rows_of(hs, i, 1, pitch) for i in (0, 1, inner - 2, inner - 1)]
    for i, value in enumerate(known_rows(*hidden, w2)):
        known_o[i] = value + temporal[i].astype(jnp.float32)


def shown(value, mask):
    return inside(value, mask).astype(jnp.bfloat16)


def end_kernel(masks, edges, known_h, known_o, below, w1, w2, o_end):
    rows = [
        shown(unpack(below[2]) + edges[1], masks[0]),
        shown(unpack(below[1]) + edges[3], masks[2]),
        shown(unpack(below[0]), masks[2]),
    ]
    hidden = end_rows(rows, w1, known_h)
    hidden = [shown(silu(value), masks[part]) for value, part in zip(hidden, (0, 0, 2))]
    sums = end_rows(hidden, w2, known_o)
    sums[2] = sums[2] + rows[0].astype(jnp.float32)
    for i, value in enumerate(sums):
        o_end[i] = crop(value, value.shape[0] // SPAN, SPAN)[0]


def top_kernel(masks, edges, known_h, known_o, above, w1, w2, o_mid, o_end, out):
    rows = [
        shown(unpack(above[0]), masks[1]),
        shown(unpack(above[1]) + edges[2], masks[1]),
        shown(unpack(above[2]) + edges[0], masks[0]),
    ]
    hidden = top_rows(rows, w1, known_h)
    hidden = [shown(silu(value), masks[part]) for value, part in zip(hidden, (1, 0, 0))]
    sums = top_rows(hidden, w2, known_o)
    sums[0] = sums[0] + rows[2].astype(jnp.float32)
    done = [crop(value, value.shape[0] // SPAN, SPAN)[0] for value in sums]
    done += [o_mid[i] for i in range(o_mid.shape[0])] + [o_end[i] for i in range(3)]
    each = out.shape[2]
    for row, value in enumerate(done):
        out[row // each, :, row % each] = value


def per_device(frames_in, temporal_weight, first_weight, second_weight):
    tm, slabs = lax.axis_size("tm"), lax.axis_size("rows")
    planes = slabs // SLABS
    frame_count, row_count, col_count, chans = frames_in.shape
    count = tm * SLABS
    width = col_count // count
    span = SPAN
    size = width + 2 * HALO
    plane_rows = SLABS * row_count
    pitch = tm * span
    column, slab = lax.axis_index("tm"), lax.axis_index("rows")
    plane = slab // SLABS
    first_col = (column * SLABS + slab % SLABS) * width - HALO
    col = lax.broadcasted_iota(jnp.int32, (3, span, chans), 1) + first_col
    part = lax.broadcasted_iota(jnp.int32, (3, span, chans), 0)
    shown = (col >= 0) & (col < col_count)
    shown &= ((part != 1) | (plane > 0)) & ((part != 2) | (plane < planes - 1))
    masks = shown.astype(jnp.float32)
    vmem = pl.BlockSpec(memory_space=pltpu.VMEM)
    params = pltpu.CompilerParams(vmem_limit_bytes=VMEM_BYTES)

    def brain(*shape):
        return jax.ShapeDtypeStruct(shape, jnp.bfloat16)

    def held(*shape):
        return pltpu.VMEM(shape, jnp.bfloat16)

    cut = pl.pallas_call(
        windows_kernel,
        out_shape=brain(count, frame_count * row_count * size, chans),
        in_specs=[vmem],
        out_specs=vmem,
        compiler_params=params,
        name="windows",
    )(frames_in)
    cut, masks = lax.optimization_barrier((cut, masks))
    members = [[m * slabs + z * SLABS + j for m in range(tm) for j in range(SLABS)] for z in range(planes)]
    own = lax.all_to_all(
        cut, ("tm", "rows"), split_axis=0, concat_axis=0, tiled=True, axis_index_groups=members
    ).reshape(tm, SLABS, frame_count * row_count * size, chans)

    t_edge, edges, send_down, send_up = pl.pallas_call(
        edge_kernel,
        out_shape=[
            brain(2, pitch, chans),
            jax.ShapeDtypeStruct((4, pitch, chans), jnp.float32),
            brain(3, tm * KEPT, chans),
            brain(3, tm * KEPT, chans),
        ],
        in_specs=[vmem] * 3,
        out_specs=[vmem] * 4,
        scratch_shapes=[held(3, 6 * pitch, chans)],
        compiler_params=params,
        name="edge",
    )(masks, own, temporal_weight)

    reach = range(slabs - SLABS)
    above = lax.ppermute(send_up, "rows", [(r, r + SLABS) for r in reach])
    below = lax.ppermute(send_down, "rows", [(r + SLABS, r) for r in reach])

    inner = plane_rows - 4
    partial = jax.ShapeDtypeStruct((4, pitch, chans), jnp.float32)
    known_h, known_o, o_mid, w1, w2 = pl.pallas_call(
        inner_kernel,
        out_shape=[
            partial,
            partial,
            brain(inner - 2, tm, width, chans),
            brain(3 * chans, 3 * chans),
            brain(3 * chans, 3 * chans),
        ],
        in_specs=[vmem] * 6,
        out_specs=[vmem] * 5,
        scratch_shapes=[
            held(3, (inner + 2) * pitch, chans),
            held((inner + 2) * pitch, chans),
            held(inner * pitch, chans),
            held(9 * chans, 3 * chans),
        ],
        compiler_params=params,
        cost_estimate=pl.CostEstimate(flops=10**9, bytes_accessed=4 * 10**6, transcendentals=10**5),
        name="inner",
    )(masks, own, temporal_weight, t_edge, first_weight, second_weight)
    o_end = pl.pallas_call(
        end_kernel,
        out_shape=brain(3, tm, width, chans),
        in_specs=[vmem] * 7,
        out_specs=vmem,
        compiler_params=params,
        cost_estimate=pl.CostEstimate(flops=4 * 10**8, bytes_accessed=10**6, transcendentals=10**5),
        name="end",
    )(masks, edges, known_h, known_o, below, w1, w2)
    encoded = pl.pallas_call(
        top_kernel,
        out_shape=brain(SLABS, tm, row_count, width, chans),
        in_specs=[vmem] * 9,
        out_specs=vmem,
        compiler_params=params,
        name="top",
    )(masks, edges, known_h, known_o, above, w1, w2, o_mid, o_end)

    groups = [[z * SLABS + j for j in range(SLABS)] for z in range(planes)]
    encoded = lax.all_to_all(
        encoded, "rows", split_axis=0, concat_axis=0, tiled=True, axis_index_groups=groups
    )
    return jnp.transpose(encoded, (1, 2, 0, 3, 4)).reshape(tm, row_count, SLABS * width, chans)


def solution(mesh):
    placed = (P("tm", "rows", None, None), P(), P(), P())
    return jax.shard_map(
        per_device,
        mesh=mesh,
        in_specs=placed,
        out_specs=P(None, "rows", "tm", None),
        check_vma=False,
    )
```

```python
import jax
import jax.numpy as jnp
from jax import lax
from jax.experimental import pallas as pl
from jax.experimental.pallas import tpu as pltpu
from jax.sharding import PartitionSpec as P

SLABS = 4
HALO = 3
PLANE_ROWS = 8
WIDTH = 16
SPAN = 24
KEPT = 20
VMEM_BYTES = 32 * 1024 * 1024


def windows_kernel(frames, out):
    count = out.shape[0]
    parts = [(f, r) for f in range(frames.shape[0]) for r in range(frames.shape[1])]
    size = out.shape[1] // len(parts)
    width = size - 2 * HALO
    padded = []
    for f, r in parts:
        row = frames[f, r].astype(jnp.float32)
        edge = jnp.zeros((HALO, row.shape[1]), jnp.float32)
        padded.append(jnp.concatenate([edge, row, edge], axis=0))
    for k in range(count):
        cut = [row[k * width : k * width + size] for row in padded]
        out[k] = jnp.concatenate(cut, axis=0).astype(jnp.bfloat16)


def column_taps(sums):
    chans = sums.shape[1] // 3
    left, mid, right = sums[:, :chans], sums[:, chans : 2 * chans], sums[:, 2 * chans :]
    return mid + pltpu.roll(left, 1, 0) + pltpu.roll(right, sums.shape[0] - 1, 0)


def inside(value, mask):
    rows, chans = value.shape
    shown = value.reshape(rows // mask.shape[0], *mask.shape) * mask[...][None]
    return shown.reshape(rows, chans)


def temporal_weight_to(wt, weight):
    chans = weight.shape[3]
    for a in range(3):
        for b in range(3):
            for c in range(3):
                k = (b * 3 + a) * chans
                wt[k : k + chans, c * chans : (c + 1) * chans] = weight[a, b, c]


def plane_weight_to(wt, weight):
    chans = weight.shape[2]
    for b in range(3):
        for c in range(3):
            wt[b * chans : (b + 1) * chans, c * chans : (c + 1) * chans] = weight[b, c]


def frames_to(xs, at, own, row, rows_each):
    frames, chans = own.shape[0], own.shape[3]
    size = own.shape[2] // (2 * rows_each)

    def pick(m, f):
        part = own[m, row // rows_each].astype(jnp.float32)
        start = (f * rows_each + row % rows_each) * size
        part = part[start : start + SPAN]
        if part.shape[0] < SPAN:
            part = jnp.concatenate([part, jnp.zeros((SPAN - part.shape[0], chans), jnp.float32)], axis=0)
        return part

    for t in range(0, frames, 2):
        here = at + t * SPAN
        for a, f in ((1, 0), (2, 1)):
            pair = jnp.concatenate([pick(t, f), pick(t + 1, f)], axis=0)
            xs[a, here : here + 2 * SPAN] = pair.astype(jnp.bfloat16)
        before = pick(t - 1, 1) if t else jnp.zeros((SPAN, chans), jnp.float32)
        pair = jnp.concatenate([before, pick(t, 1)], axis=0)
        xs[0, here : here + 2 * SPAN] = pair.astype(jnp.bfloat16)


def silu(value):
    return value * (0.5 * jnp.tanh(0.5 * value) + 0.5)


def rows_of(ref, first, count, pitch):
    return ref[first * pitch : (first + count) * pitch]


def row_taps(ref, first, count, pitch):
    return jnp.concatenate([rows_of(ref, first + b, count, pitch) for b in range(3)], axis=1)


def temporal_taps(weight, row_taps):
    return jnp.concatenate(
        [
            jnp.concatenate([weight[a, b, c] for c in range(3)], axis=1)
            for b in row_taps
            for a in range(3)
        ],
        axis=0,
    )


def halves(value):
    high = value.astype(jnp.bfloat16).astype(jnp.float32)
    return high, value - high


def pack(value):
    kept = [value[at + 1 : at + 1 + KEPT] for at in range(0, value.shape[0], SPAN)]
    return jnp.concatenate(kept, axis=0).astype(jnp.bfloat16)


def unpack(packed):
    value = packed.astype(jnp.float32)
    before = jnp.zeros((1, value.shape[1]), jnp.float32)
    after = jnp.zeros((SPAN - KEPT - 1, value.shape[1]), jnp.float32)
    parts = []
    for at in range(0, value.shape[0], KEPT):
        parts += [before, value[at : at + KEPT], after]
    return jnp.concatenate(parts, axis=0)


def edge_kernel(masks, own, weight, t_edge, edges, send_down, send_up, xs):
    frames, span, chans = own.shape[0], SPAN, own.shape[3]
    rows_each = PLANE_ROWS // own.shape[1]
    rows = own.shape[1] * rows_each
    pitch = frames * span

    for i in range(3):
        frames_to(xs, i * pitch, own, i, rows_each)
        frames_to(xs, (3 + i) * pitch, own, rows - 3 + i, rows_each)

    def taps_of(i):
        return jnp.concatenate([xs[a, i * pitch : (i + 1) * pitch] for a in range(3)], axis=1)

    deep = 3 * chans
    x = [taps_of(i) for i in range(6)]
    sums = jnp.dot(
        jnp.concatenate([jnp.concatenate(pair, axis=1) for pair in (x[0:2], x[4:6])], axis=0),
        jnp.concatenate([temporal_taps(weight, taps) for taps in ((1, 2), (0, 1))], axis=1),
        preferred_element_type=jnp.float32,
    )
    lower, upper = column_taps(sums[:, :deep]), column_taps(sums[:, deep:])
    first, last = lower[:pitch], upper[pitch:]
    second, before = split_rows(dot_taps([[x[2]], [x[0]]], temporal_taps(weight, (2,))), pitch)
    third, after = split_rows(dot_taps([[x[3]], [x[5]]], temporal_taps(weight, (0,))), pitch)
    edges[0], edges[1], edges[2], edges[3] = first, last, before, after
    near = inside(upper[:pitch] + second, masks[0])
    far = inside(lower[pitch:] + third, masks[0])
    t_edge[0], t_edge[1] = near.astype(jnp.bfloat16), far.astype(jnp.bfloat16)
    for i, value in enumerate((far, *halves(last), *halves(after))):
        send_up[i] = pack(value)
    for i, value in enumerate((near, *halves(first), *halves(before))):
        send_down[i] = pack(value)


def crop(value, frames, span):
    shape = (value.shape[0] // (frames * span), frames, span, value.shape[1])
    return value.reshape(shape)[:, :, HALO : HALO + WIDTH].astype(jnp.bfloat16)


def dot_taps(lhs, rhs):
    lhs = jnp.concatenate([jnp.concatenate(blocks, axis=1) for blocks in lhs], axis=0)
    return column_taps(jnp.dot(lhs, rhs, preferred_element_type=jnp.float32))


def split_rows(value, pitch):
    return [value[at : at + pitch] for at in range(0, value.shape[0], pitch)]


def known_rows(first, second, before_last, last, weight):
    pitch, chans = first.shape
    none = jnp.zeros_like(first)
    top = dot_taps([[none, first], [first, second]], weight[chans:])
    end = dot_taps([[before_last, last], [last, none]], weight[: 2 * chans])
    return split_rows(top, pitch) + split_rows(end, pitch)


def top_rows(rows, weight, known):
    none, chans = jnp.zeros_like(rows[0]), rows[0].shape[1]
    first = dot_taps([rows], weight[...])
    near = split_rows(dot_taps([rows[1:], [rows[2], none]], weight[: 2 * chans]), none.shape[0])
    return [first, near[0] + known[0], near[1] + known[1]]


def end_rows(rows, weight, known):
    none, chans = jnp.zeros_like(rows[0]), rows[0].shape[1]
    last = dot_taps([rows], weight[...])
    far = split_rows(dot_taps([[none, rows[0]], rows[:2]], weight[chans:]), none.shape[0])
    return [far[0] + known[2], far[1] + known[3], last]


def inner_kernel(
    masks, own, weight, t_edge, w_first, w_second, known_h, known_o, o_mid, w1, w2,
    xs, tall, hs, wt,
):
    frames, span = own.shape[0], SPAN
    rows_each = PLANE_ROWS // own.shape[1]
    rows = own.shape[1] * rows_each
    pitch = frames * span
    temporal_weight_to(wt, weight)
    plane_weight_to(w1, w_first)
    plane_weight_to(w2, w_second)
    for row in range(1, rows - 1):
        frames_to(xs, (row - 1) * pitch, own, row, rows_each)
    lhs = jnp.concatenate(
        [xs[a, b * pitch : (b + rows - 4) * pitch] for b in range(3) for a in range(3)], axis=1
    )
    sums = column_taps(jnp.dot(lhs, wt[...], preferred_element_type=jnp.float32))

    tall[:pitch] = t_edge[0]
    tall[pitch : (rows - 3) * pitch] = inside(sums, masks[0]).astype(jnp.bfloat16)
    tall[(rows - 3) * pitch :] = t_edge[1]
    inner = rows - 4
    sums = column_taps(
        jnp.dot(row_taps(tall, 0, inner, pitch), w1[...], preferred_element_type=jnp.float32)
    )
    hs[...] = inside(silu(sums), masks[0]).astype(jnp.bfloat16)
    temporal = [rows_of(tall, i, 1, pitch) for i in (0, 1, inner, inner + 1)]
    for i, value in enumerate(known_rows(*temporal, w1)):
        known_h[i] = value

    sums = column_taps(
        jnp.dot(row_taps(hs, 0, inner - 2, pitch), w2[...], preferred_element_type=jnp.float32)
    )
    sums = sums + rows_of(tall, 2, inner - 2, pitch).astype(jnp.float32)
    o_mid[...] = crop(sums, frames, span)
    hidden = [rows_of(hs, i, 1, pitch) for i in (0, 1, inner - 2, inner - 1)]
    for i, value in enumerate(known_rows(*hidden, w2)):
        known_o[i] = value + temporal[i].astype(jnp.float32)


def shown(value, mask):
    return inside(value, mask).astype(jnp.bfloat16)


def end_kernel(masks, edges, known_h, known_o, below, w1, w2, o_end):
    rows = [
        shown(unpack(below[3]) + unpack(below[4]) + edges[1], masks[0]),
        shown(unpack(below[1]) + unpack(below[2]) + edges[3], masks[2]),
        shown(unpack(below[0]), masks[2]),
    ]
    hidden = end_rows(rows, w1, known_h)
    hidden = [shown(silu(value), masks[part]) for value, part in zip(hidden, (0, 0, 2))]
    sums = end_rows(hidden, w2, known_o)
    sums[2] = sums[2] + rows[0].astype(jnp.float32)
    for i, value in enumerate(sums):
        o_end[i] = crop(value, value.shape[0] // SPAN, SPAN)[0]


def top_kernel(masks, edges, known_h, known_o, above, w1, w2, o_mid, o_end, out):
    rows = [
        shown(unpack(above[0]), masks[1]),
        shown(unpack(above[1]) + unpack(above[2]) + edges[2], masks[1]),
        shown(unpack(above[3]) + unpack(above[4]) + edges[0], masks[0]),
    ]
    hidden = top_rows(rows, w1, known_h)
    hidden = [shown(silu(value), masks[part]) for value, part in zip(hidden, (1, 0, 0))]
    sums = top_rows(hidden, w2, known_o)
    sums[0] = sums[0] + rows[2].astype(jnp.float32)
    done = [crop(value, value.shape[0] // SPAN, SPAN)[0] for value in sums]
    done += [o_mid[i] for i in range(o_mid.shape[0])] + [o_end[i] for i in range(3)]
    each = out.shape[2]
    for row, value in enumerate(done):
        out[row // each, :, row % each] = value


def per_device(frames_in, temporal_weight, first_weight, second_weight):
    tm, slabs = lax.axis_size("tm"), lax.axis_size("rows")
    planes = slabs // SLABS
    frame_count, row_count, col_count, chans = frames_in.shape
    count = tm * SLABS
    width = col_count // count
    span = SPAN
    size = width + 2 * HALO
    plane_rows = SLABS * row_count
    pitch = tm * span
    column, slab = lax.axis_index("tm"), lax.axis_index("rows")
    plane = slab // SLABS
    first_col = (column * SLABS + slab % SLABS) * width - HALO
    col = lax.broadcasted_iota(jnp.int32, (3, span, chans), 1) + first_col
    part = lax.broadcasted_iota(jnp.int32, (3, span, chans), 0)
    shown = (col >= 0) & (col < col_count)
    shown &= ((part != 1) | (plane > 0)) & ((part != 2) | (plane < planes - 1))
    masks = shown.astype(jnp.float32)
    vmem = pl.BlockSpec(memory_space=pltpu.VMEM)
    params = pltpu.CompilerParams(vmem_limit_bytes=VMEM_BYTES)

    def brain(*shape):
        return jax.ShapeDtypeStruct(shape, jnp.bfloat16)

    def held(*shape):
        return pltpu.VMEM(shape, jnp.bfloat16)

    cut = pl.pallas_call(
        windows_kernel,
        out_shape=brain(count, frame_count * row_count * size, chans),
        in_specs=[vmem],
        out_specs=vmem,
        compiler_params=params,
        name="windows",
    )(frames_in)
    cut, masks = lax.optimization_barrier((cut, masks))
    members = [[m * slabs + z * SLABS + j for m in range(tm) for j in range(SLABS)] for z in range(planes)]
    own = lax.all_to_all(
        cut, ("tm", "rows"), split_axis=0, concat_axis=0, tiled=True, axis_index_groups=members
    ).reshape(tm, SLABS, frame_count * row_count * size, chans)

    t_edge, edges, send_down, send_up = pl.pallas_call(
        edge_kernel,
        out_shape=[
            brain(2, pitch, chans),
            jax.ShapeDtypeStruct((4, pitch, chans), jnp.float32),
            brain(5, tm * KEPT, chans),
            brain(5, tm * KEPT, chans),
        ],
        in_specs=[vmem] * 3,
        out_specs=[vmem] * 4,
        scratch_shapes=[held(3, 6 * pitch, chans)],
        compiler_params=params,
        name="edge",
    )(masks, own, temporal_weight)

    reach = range(slabs - SLABS)
    above = lax.ppermute(send_up, "rows", [(r, r + SLABS) for r in reach])
    below = lax.ppermute(send_down, "rows", [(r + SLABS, r) for r in reach])

    inner = plane_rows - 4
    partial = jax.ShapeDtypeStruct((4, pitch, chans), jnp.float32)
    known_h, known_o, o_mid, w1, w2 = pl.pallas_call(
        inner_kernel,
        out_shape=[
            partial,
            partial,
            brain(inner - 2, tm, width, chans),
            brain(3 * chans, 3 * chans),
            brain(3 * chans, 3 * chans),
        ],
        in_specs=[vmem] * 6,
        out_specs=[vmem] * 5,
        scratch_shapes=[
            held(3, (inner + 2) * pitch, chans),
            held((inner + 2) * pitch, chans),
            held(inner * pitch, chans),
            held(9 * chans, 3 * chans),
        ],
        compiler_params=params,
        cost_estimate=pl.CostEstimate(flops=10**9, bytes_accessed=4 * 10**6, transcendentals=10**5),
        name="inner",
    )(masks, own, temporal_weight, t_edge, first_weight, second_weight)
    o_end = pl.pallas_call(
        end_kernel,
        out_shape=brain(3, tm, width, chans),
        in_specs=[vmem] * 7,
        out_specs=vmem,
        compiler_params=params,
        cost_estimate=pl.CostEstimate(flops=4 * 10**8, bytes_accessed=10**6, transcendentals=10**5),
        name="end",
    )(masks, edges, known_h, known_o, below, w1, w2)
    encoded = pl.pallas_call(
        top_kernel,
        out_shape=brain(SLABS, tm, row_count, width, chans),
        in_specs=[vmem] * 9,
        out_specs=vmem,
        compiler_params=params,
        name="top",
    )(masks, edges, known_h, known_o, above, w1, w2, o_mid, o_end)

    groups = [[z * SLABS + j for j in range(SLABS)] for z in range(planes)]
    encoded = lax.all_to_all(
        encoded, "rows", split_axis=0, concat_axis=0, tiled=True, axis_index_groups=groups
    )
    return jnp.transpose(encoded, (1, 2, 0, 3, 4)).reshape(tm, row_count, SLABS * width, chans)


def solution(mesh):
    placed = (P("tm", "rows", None, None), P(), P(), P())
    return jax.shard_map(
        per_device,
        mesh=mesh,
        in_specs=placed,
        out_specs=P(None, "rows", "tm", None),
        check_vma=False,
    )
```

```python
import jax
import jax.numpy as jnp
from jax import lax
from jax.experimental import pallas as pl
from jax.experimental.pallas import tpu as pltpu
from jax.sharding import PartitionSpec as P

SLABS = 4
HALO = 3
PLANE_ROWS = 8
WIDTH = 16
SPAN = 24
KEPT = 20
VMEM_BYTES = 32 * 1024 * 1024


def windows_kernel(frames, out):
    count = out.shape[0]
    parts = [(f, r) for f in range(frames.shape[0]) for r in range(frames.shape[1])]
    size = out.shape[1] // len(parts)
    width = size - 2 * HALO
    padded = []
    for f, r in parts:
        row = frames[f, r].astype(jnp.float32)
        edge = jnp.zeros((HALO, row.shape[1]), jnp.float32)
        padded.append(jnp.concatenate([edge, row, edge], axis=0))
    for k in range(count):
        cut = [row[k * width : k * width + size] for row in padded]
        out[k] = jnp.concatenate(cut, axis=0).astype(jnp.bfloat16)


def column_taps(sums):
    chans = sums.shape[1] // 3
    left, mid, right = sums[:, :chans], sums[:, chans : 2 * chans], sums[:, 2 * chans :]
    return mid + pltpu.roll(left, 1, 0) + pltpu.roll(right, sums.shape[0] - 1, 0)


def inside(value, mask):
    rows, chans = value.shape
    shown = value.reshape(rows // mask.shape[0], *mask.shape) * mask[...][None]
    return shown.reshape(rows, chans)


def temporal_weight_to(wt, weight):
    chans = weight.shape[3]
    for a in range(3):
        for b in range(3):
            for c in range(3):
                k = (b * 3 + a) * chans
                wt[k : k + chans, c * chans : (c + 1) * chans] = weight[a, b, c]


def plane_weight_to(wt, weight):
    chans = weight.shape[2]
    for b in range(3):
        for c in range(3):
            wt[b * chans : (b + 1) * chans, c * chans : (c + 1) * chans] = weight[b, c]


def frames_to(xs, at, own, row, rows_each):
    frames, chans = own.shape[0], own.shape[3]
    size = own.shape[2] // (2 * rows_each)

    def pick(m, f):
        part = own[m, row // rows_each].astype(jnp.float32)
        start = (f * rows_each + row % rows_each) * size
        part = part[start : start + SPAN]
        if part.shape[0] < SPAN:
            part = jnp.concatenate([part, jnp.zeros((SPAN - part.shape[0], chans), jnp.float32)], axis=0)
        return part

    for t in range(0, frames, 2):
        here = at + t * SPAN
        for a, f in ((1, 0), (2, 1)):
            pair = jnp.concatenate([pick(t, f), pick(t + 1, f)], axis=0)
            xs[a, here : here + 2 * SPAN] = pair.astype(jnp.bfloat16)
        before = pick(t - 1, 1) if t else jnp.zeros((SPAN, chans), jnp.float32)
        pair = jnp.concatenate([before, pick(t, 1)], axis=0)
        xs[0, here : here + 2 * SPAN] = pair.astype(jnp.bfloat16)


def silu(value):
    return value * (0.5 * jnp.tanh(0.5 * value) + 0.5)


def rows_of(ref, first, count, pitch):
    return ref[first * pitch : (first + count) * pitch]


def row_taps(ref, first, count, pitch):
    return jnp.concatenate([rows_of(ref, first + b, count, pitch) for b in range(3)], axis=1)


def temporal_taps(weight, row_taps):
    return jnp.concatenate(
        [
            jnp.concatenate([weight[a, b, c] for c in range(3)], axis=1)
            for b in row_taps
            for a in range(3)
        ],
        axis=0,
    )


def pack(value):
    kept = [value[at + 1 : at + 1 + KEPT] for at in range(0, value.shape[0], SPAN)]
    return jnp.concatenate(kept, axis=0)


def edge_kernel(masks, own, weight, t_edge, edges, send_down, send_up, xs):
    frames, span, chans = own.shape[0], SPAN, own.shape[3]
    rows_each = PLANE_ROWS // own.shape[1]
    rows = own.shape[1] * rows_each
    pitch = frames * span

    for i in range(3):
        frames_to(xs, i * pitch, own, i, rows_each)
        frames_to(xs, (3 + i) * pitch, own, rows - 3 + i, rows_each)

    def taps_of(i):
        return jnp.concatenate([xs[a, i * pitch : (i + 1) * pitch] for a in range(3)], axis=1)

    deep = 3 * chans
    x = [taps_of(i) for i in range(6)]
    sums = jnp.dot(
        jnp.concatenate([jnp.concatenate(pair, axis=1) for pair in (x[0:2], x[4:6])], axis=0),
        jnp.concatenate([temporal_taps(weight, taps) for taps in ((1, 2), (0, 1))], axis=1),
        preferred_element_type=jnp.float32,
    )
    lower, upper = column_taps(sums[:, :deep]), column_taps(sums[:, deep:])
    first, last = lower[:pitch], upper[pitch:]
    second, before = split_rows(dot_taps([[x[2]], [x[0]]], temporal_taps(weight, (2,))), pitch)
    third, after = split_rows(dot_taps([[x[3]], [x[5]]], temporal_taps(weight, (0,))), pitch)
    near = inside(upper[:pitch] + second, masks[0])
    far = inside(lower[pitch:] + third, masks[0])
    t_edge[0], t_edge[1] = near.astype(jnp.bfloat16), far.astype(jnp.bfloat16)
    first, last, before, after = [pack(value) for value in (first, last, before, after)]
    edges[0], edges[1], edges[2], edges[3] = first, last, before, after
    for i, value in enumerate((pack(far), last, after)):
        send_up[i] = value.astype(jnp.bfloat16)
    for i, value in enumerate((pack(near), first, before)):
        send_down[i] = value.astype(jnp.bfloat16)


def crop(value, frames, span):
    shape = (value.shape[0] // (frames * span), frames, span, value.shape[1])
    return value.reshape(shape)[:, :, HALO : HALO + WIDTH].astype(jnp.bfloat16)


def dot_taps(lhs, rhs):
    lhs = jnp.concatenate([jnp.concatenate(blocks, axis=1) for blocks in lhs], axis=0)
    return column_taps(jnp.dot(lhs, rhs, preferred_element_type=jnp.float32))


def split_rows(value, pitch):
    return [value[at : at + pitch] for at in range(0, value.shape[0], pitch)]


def known_rows(first, second, before_last, last, weight):
    pitch, chans = first.shape
    none = jnp.zeros_like(first)
    top = dot_taps([[none, first], [first, second]], weight[chans:])
    end = dot_taps([[before_last, last], [last, none]], weight[: 2 * chans])
    return split_rows(top, pitch) + split_rows(end, pitch)


def top_rows(rows, weight, known):
    none, chans = jnp.zeros_like(rows[0]), rows[0].shape[1]
    first = dot_taps([rows], weight[...])
    near = split_rows(dot_taps([rows[1:], [rows[2], none]], weight[: 2 * chans]), none.shape[0])
    return [first, near[0] + known[0], near[1] + known[1]]


def end_rows(rows, weight, known):
    none, chans = jnp.zeros_like(rows[0]), rows[0].shape[1]
    last = dot_taps([rows], weight[...])
    far = split_rows(dot_taps([[none, rows[0]], rows[:2]], weight[chans:]), none.shape[0])
    return [far[0] + known[2], far[1] + known[3], last]


def inner_kernel(
    masks, own, weight, t_edge, w_first, w_second, known_h, known_o, o_mid, shown, w1, w2,
    xs, tall, hs, wt,
):
    frames, span = own.shape[0], SPAN
    rows_each = PLANE_ROWS // own.shape[1]
    rows = own.shape[1] * rows_each
    pitch = frames * span
    temporal_weight_to(wt, weight)
    plane_weight_to(w1, w_first)
    plane_weight_to(w2, w_second)
    for row in range(1, rows - 1):
        frames_to(xs, (row - 1) * pitch, own, row, rows_each)
    lhs = jnp.concatenate(
        [xs[a, b * pitch : (b + rows - 4) * pitch] for b in range(3) for a in range(3)], axis=1
    )
    sums = column_taps(jnp.dot(lhs, wt[...], preferred_element_type=jnp.float32))

    tall[:pitch] = t_edge[0]
    tall[pitch : (rows - 3) * pitch] = inside(sums, masks[0]).astype(jnp.bfloat16)
    tall[(rows - 3) * pitch :] = t_edge[1]
    inner = rows - 4
    sums = column_taps(
        jnp.dot(row_taps(tall, 0, inner, pitch), w1[...], preferred_element_type=jnp.float32)
    )
    hs[...] = inside(silu(sums), masks[0]).astype(jnp.bfloat16)
    temporal = [rows_of(tall, i, 1, pitch) for i in (0, 1, inner, inner + 1)]
    for i, value in enumerate(known_rows(*temporal, w1)):
        known_h[i] = pack(value)

    sums = column_taps(
        jnp.dot(row_taps(hs, 0, inner - 2, pitch), w2[...], preferred_element_type=jnp.float32)
    )
    sums = sums + rows_of(tall, 2, inner - 2, pitch).astype(jnp.float32)
    o_mid[...] = crop(sums, frames, span)
    hidden = [rows_of(hs, i, 1, pitch) for i in (0, 1, inner - 2, inner - 1)]
    for i, value in enumerate(known_rows(*hidden, w2)):
        known_o[i] = pack(value + temporal[i].astype(jnp.float32))
    for i in range(3):
        shown[i] = pack(jnp.concatenate([masks[i]] * frames, axis=0))


def cut(value, frames):
    kept = [value[at + HALO - 1 : at + HALO - 1 + WIDTH] for at in range(0, value.shape[0], KEPT)]
    return jnp.concatenate(kept, axis=0).reshape(frames, WIDTH, value.shape[1]).astype(jnp.bfloat16)


def end_kernel(shown, edges, known_h, known_o, below, w1, w2, o_end):
    rows = [
        (below[2] + edges[1]) * shown[0],
        (below[1] + edges[3]) * shown[2],
        below[0] * shown[2],
    ]
    rows = [row.astype(jnp.bfloat16) for row in rows]
    hidden = end_rows(rows, w1, known_h)
    hidden = [(silu(v) * shown[part]).astype(jnp.bfloat16) for v, part in zip(hidden, (0, 0, 2))]
    sums = end_rows(hidden, w2, known_o)
    sums[2] = sums[2] + rows[0].astype(jnp.float32)
    for i, value in enumerate(sums):
        o_end[i] = cut(value, o_end.shape[1])


def top_kernel(shown, edges, known_h, known_o, above, w1, w2, o_mid, o_end, out):
    rows = [
        above[0] * shown[1],
        (above[1] + edges[2]) * shown[1],
        (above[2] + edges[0]) * shown[0],
    ]
    rows = [row.astype(jnp.bfloat16) for row in rows]
    hidden = top_rows(rows, w1, known_h)
    hidden = [(silu(v) * shown[part]).astype(jnp.bfloat16) for v, part in zip(hidden, (1, 0, 0))]
    sums = top_rows(hidden, w2, known_o)
    sums[0] = sums[0] + rows[2].astype(jnp.float32)
    done = [cut(value, out.shape[1]) for value in sums]
    done += [o_mid[i] for i in range(o_mid.shape[0])] + [o_end[i] for i in range(3)]
    each = out.shape[2]
    for row, value in enumerate(done):
        out[row // each, :, row % each] = value


def per_device(frames_in, temporal_weight, first_weight, second_weight):
    tm, slabs = lax.axis_size("tm"), lax.axis_size("rows")
    planes = slabs // SLABS
    frame_count, row_count, col_count, chans = frames_in.shape
    count = tm * SLABS
    width = col_count // count
    span = SPAN
    size = width + 2 * HALO
    plane_rows = SLABS * row_count
    pitch = tm * span
    column, slab = lax.axis_index("tm"), lax.axis_index("rows")
    plane = slab // SLABS
    first_col = (column * SLABS + slab % SLABS) * width - HALO
    col = lax.broadcasted_iota(jnp.int32, (3, span, chans), 1) + first_col
    part = lax.broadcasted_iota(jnp.int32, (3, span, chans), 0)
    visible = (col >= 0) & (col < col_count)
    visible &= ((part != 1) | (plane > 0)) & ((part != 2) | (plane < planes - 1))
    masks = visible.astype(jnp.float32)
    vmem = pl.BlockSpec(memory_space=pltpu.VMEM)
    params = pltpu.CompilerParams(vmem_limit_bytes=VMEM_BYTES)

    def brain(*shape):
        return jax.ShapeDtypeStruct(shape, jnp.bfloat16)

    def held(*shape):
        return pltpu.VMEM(shape, jnp.bfloat16)

    cut = pl.pallas_call(
        windows_kernel,
        out_shape=brain(count, frame_count * row_count * size, chans),
        in_specs=[vmem],
        out_specs=vmem,
        compiler_params=params,
        name="windows",
    )(frames_in)
    cut, masks = lax.optimization_barrier((cut, masks))
    members = [[m * slabs + z * SLABS + j for m in range(tm) for j in range(SLABS)] for z in range(planes)]
    own = lax.all_to_all(
        cut, ("tm", "rows"), split_axis=0, concat_axis=0, tiled=True, axis_index_groups=members
    ).reshape(tm, SLABS, frame_count * row_count * size, chans)

    t_edge, edges, send_down, send_up = pl.pallas_call(
        edge_kernel,
        out_shape=[
            brain(2, pitch, chans),
            jax.ShapeDtypeStruct((4, tm * KEPT, chans), jnp.float32),
            brain(3, tm * KEPT, chans),
            brain(3, tm * KEPT, chans),
        ],
        in_specs=[vmem] * 3,
        out_specs=[vmem] * 4,
        scratch_shapes=[held(3, 6 * pitch, chans)],
        compiler_params=params,
        name="edge",
    )(masks, own, temporal_weight)

    reach = range(slabs - SLABS)
    above = lax.ppermute(send_up, "rows", [(r, r + SLABS) for r in reach])
    below = lax.ppermute(send_down, "rows", [(r + SLABS, r) for r in reach])

    inner = plane_rows - 4
    partial = jax.ShapeDtypeStruct((4, tm * KEPT, chans), jnp.float32)
    known_h, known_o, o_mid, shown, w1, w2 = pl.pallas_call(
        inner_kernel,
        out_shape=[
            partial,
            partial,
            brain(inner - 2, tm, width, chans),
            jax.ShapeDtypeStruct((3, tm * KEPT, chans), jnp.float32),
            brain(3 * chans, 3 * chans),
            brain(3 * chans, 3 * chans),
        ],
        in_specs=[vmem] * 6,
        out_specs=[vmem] * 6,
        scratch_shapes=[
            held(3, (inner + 2) * pitch, chans),
            held((inner + 2) * pitch, chans),
            held(inner * pitch, chans),
            held(9 * chans, 3 * chans),
        ],
        compiler_params=params,
        cost_estimate=pl.CostEstimate(flops=10**9, bytes_accessed=4 * 10**6, transcendentals=10**5),
        name="inner",
    )(masks, own, temporal_weight, t_edge, first_weight, second_weight)
    o_end = pl.pallas_call(
        end_kernel,
        out_shape=brain(3, tm, width, chans),
        in_specs=[vmem] * 7,
        out_specs=vmem,
        compiler_params=params,
        cost_estimate=pl.CostEstimate(flops=4 * 10**8, bytes_accessed=10**6, transcendentals=10**5),
        name="end",
    )(shown, edges, known_h, known_o, below, w1, w2)
    encoded = pl.pallas_call(
        top_kernel,
        out_shape=brain(SLABS, tm, row_count, width, chans),
        in_specs=[vmem] * 9,
        out_specs=vmem,
        compiler_params=params,
        name="top",
    )(shown, edges, known_h, known_o, above, w1, w2, o_mid, o_end)

    groups = [[z * SLABS + j for j in range(SLABS)] for z in range(planes)]
    encoded = lax.all_to_all(
        encoded, "rows", split_axis=0, concat_axis=0, tiled=True, axis_index_groups=groups
    )
    return jnp.transpose(encoded, (1, 2, 0, 3, 4)).reshape(tm, row_count, SLABS * width, chans)


def solution(mesh):
    placed = (P("tm", "rows", None, None), P(), P(), P())
    return jax.shard_map(
        per_device,
        mesh=mesh,
        in_specs=placed,
        out_specs=P(None, "rows", "tm", None),
        check_vma=False,
    )
```

```python
import jax
import jax.numpy as jnp
from jax import lax
from jax.experimental import pallas as pl
from jax.experimental.pallas import tpu as pltpu
from jax.sharding import PartitionSpec as P

SLABS = 4
HALO = 3
PLANE_ROWS = 8
WIDTH = 16
SPAN = 24
KEPT = 20
VMEM_BYTES = 32 * 1024 * 1024


def windows_kernel(frames, out):
    count = out.shape[0]
    parts = [(f, r) for f in range(frames.shape[0]) for r in range(frames.shape[1])]
    size = out.shape[1] // len(parts)
    width = size - 2 * HALO
    padded = []
    for f, r in parts:
        row = frames[f, r].astype(jnp.float32)
        edge = jnp.zeros((HALO, row.shape[1]), jnp.float32)
        padded.append(jnp.concatenate([edge, row, edge], axis=0))
    for k in range(count):
        cut = [row[k * width : k * width + size] for row in padded]
        out[k] = jnp.concatenate(cut, axis=0).astype(jnp.bfloat16)


def column_taps(sums):
    chans = sums.shape[1] // 3
    left, mid, right = sums[:, :chans], sums[:, chans : 2 * chans], sums[:, 2 * chans :]
    return mid + pltpu.roll(left, 1, 0) + pltpu.roll(right, sums.shape[0] - 1, 0)


def inside(value, mask):
    rows, chans = value.shape
    shown = value.reshape(rows // mask.shape[0], *mask.shape) * mask[...][None]
    return shown.reshape(rows, chans)


def temporal_weight_to(wt, weight):
    chans = weight.shape[3]
    for a in range(3):
        for b in range(3):
            for c in range(3):
                k = (b * 3 + a) * chans
                wt[k : k + chans, c * chans : (c + 1) * chans] = weight[a, b, c]


def plane_weight_to(wt, weight):
    chans = weight.shape[2]
    for b in range(3):
        for c in range(3):
            wt[b * chans : (b + 1) * chans, c * chans : (c + 1) * chans] = weight[b, c]


def part_of(rows, index, size):
    part = rows[index * size : index * size + SPAN]
    if part.shape[0] < SPAN:
        none = jnp.zeros((SPAN - part.shape[0], part.shape[1]), jnp.float32)
        part = jnp.concatenate([part, none], axis=0)
    return part


def frames_to(xs, at, frames, pick):
    for t in range(0, frames, 2):
        here = at + t * SPAN
        for a, f in ((1, 0), (2, 1)):
            pair = jnp.concatenate([pick(t, f), pick(t + 1, f)], axis=0)
            xs[a, here : here + 2 * SPAN] = pair.astype(jnp.bfloat16)
        last = pick(t, 1)
        before = pick(t - 1, 1) if t else jnp.zeros_like(last)
        xs[0, here : here + 2 * SPAN] = jnp.concatenate([before, last], axis=0).astype(jnp.bfloat16)


def own_row(own, row):
    rows_each = PLANE_ROWS // own.shape[1]
    size = own.shape[2] // (2 * rows_each)

    def pick(m, f):
        part = f * rows_each + row % rows_each
        return part_of(own[m, row // rows_each].astype(jnp.float32), part, size)

    return pick


def sent_row(below, row):
    size = below.shape[1] // 6

    def pick(m, f):
        return part_of(below[m].astype(jnp.float32), f * 2 + row if row < 2 else 4 + f, size)

    return pick


def taps_of(xs, i, pitch):
    return jnp.concatenate([xs[a, i * pitch : (i + 1) * pitch] for a in range(3)], axis=1)


def silu(value):
    return value * (0.5 * jnp.tanh(0.5 * value) + 0.5)


def rows_of(ref, first, count, pitch):
    return ref[first * pitch : (first + count) * pitch]


def row_taps(ref, first, count, pitch):
    return jnp.concatenate([rows_of(ref, first + b, count, pitch) for b in range(3)], axis=1)


def temporal_taps(weight, row_taps):
    return jnp.concatenate(
        [
            jnp.concatenate([weight[a, b, c] for c in range(3)], axis=1)
            for b in row_taps
            for a in range(3)
        ],
        axis=0,
    )


def pack(value):
    kept = [value[at + 1 : at + 1 + KEPT] for at in range(0, value.shape[0], SPAN)]
    return jnp.concatenate(kept, axis=0)


def down_kernel(own, send):
    size = own.shape[2] // 4
    for m in range(own.shape[0]):
        third = own[m, 1].astype(jnp.float32)
        third = [third[:size], third[2 * size : 3 * size]]
        rows = jnp.concatenate([own[m, 0].astype(jnp.float32), *third], axis=0)
        send[m] = rows.astype(jnp.bfloat16)


def both_taps(pair, weights):
    deep = weights.shape[1] // 2
    lhs = jnp.concatenate(pair, axis=1)
    sums = jnp.dot(lhs, weights, preferred_element_type=jnp.float32)
    return column_taps(sums[:, :deep]), column_taps(sums[:, deep:])


def edge_kernel(masks, own, weight, far, edges, send_up, xs):
    frames = own.shape[0]
    pitch = frames * SPAN
    for i in range(3):
        frames_to(xs, i * pitch, frames, own_row(own, PLANE_ROWS - 3 + i))
    x = [taps_of(xs, i, pitch) for i in range(3)]
    weights = jnp.concatenate([temporal_taps(weight, taps) for taps in ((1, 2), (0, 1))], axis=1)
    lower, upper = both_taps(x[1:], weights)
    third, after = split_rows(dot_taps([[x[0]], [x[2]]], temporal_taps(weight, (0,))), pitch)
    value = inside(lower + third, masks[0])
    far[...] = value.astype(jnp.bfloat16)
    edges[0], edges[1] = last, after = pack(upper), pack(after)
    for i, value in enumerate((pack(value), last, after)):
        send_up[i] = value.astype(jnp.bfloat16)


def crop(value, frames, span):
    shape = (value.shape[0] // (frames * span), frames, span, value.shape[1])
    return value.reshape(shape)[:, :, HALO : HALO + WIDTH].astype(jnp.bfloat16)


def dot_taps(lhs, rhs):
    lhs = jnp.concatenate([jnp.concatenate(blocks, axis=1) for blocks in lhs], axis=0)
    return column_taps(jnp.dot(lhs, rhs, preferred_element_type=jnp.float32))


def split_rows(value, pitch):
    return [value[at : at + pitch] for at in range(0, value.shape[0], pitch)]


def known_rows(first, second, before_last, last, weight):
    pitch, chans = first.shape
    none = jnp.zeros_like(first)
    top = dot_taps([[none, first], [first, second]], weight[chans:])
    end = dot_taps([[before_last, last], [last, none]], weight[: 2 * chans])
    return split_rows(top, pitch) + split_rows(end, pitch)


def top_rows(rows, weight, known):
    none, chans = jnp.zeros_like(rows[0]), rows[0].shape[1]
    first = dot_taps([rows], weight[...])
    near = split_rows(dot_taps([rows[1:], [rows[2], none]], weight[: 2 * chans]), none.shape[0])
    return [first, near[0] + known[0], near[1] + known[1]]


def end_rows(rows, weight, known):
    none, chans = jnp.zeros_like(rows[0]), rows[0].shape[1]
    last = dot_taps([rows], weight[...])
    far = split_rows(dot_taps([[none, rows[0]], rows[:2]], weight[chans:]), none.shape[0])
    return [far[0] + known[2], far[1] + known[3], last]


def inner_kernel(
    masks, own, weight, far, w_first, w_second, edges, known_h, known_o, o_mid, shown, w1, w2,
    xs, tall, hs, wt,
):
    frames, span, rows = own.shape[0], SPAN, PLANE_ROWS
    pitch = frames * span
    deep = wt.shape[1]
    temporal_weight_to(wt, weight)
    plane_weight_to(w1, w_first)
    plane_weight_to(w2, w_second)
    for row in range(rows - 1):
        frames_to(xs, row * pitch, frames, own_row(own, row))
    lhs = jnp.concatenate(
        [xs[a, (b + 1) * pitch : (b + rows - 3) * pitch] for b in range(3) for a in range(3)], axis=1
    )
    sums = column_taps(jnp.dot(lhs, wt[...], preferred_element_type=jnp.float32))

    x = [taps_of(xs, i, pitch) for i in range(3)]
    lower, upper = both_taps(x[:2], jnp.concatenate([wt[deep:], wt[: 2 * deep]], axis=1))
    second, before = split_rows(dot_taps([[x[2]], [x[0]]], wt[2 * deep :]), pitch)
    edges[0], edges[1] = pack(lower), pack(before)

    tall[:pitch] = inside(upper + second, masks[0]).astype(jnp.bfloat16)
    tall[pitch : (rows - 3) * pitch] = inside(sums, masks[0]).astype(jnp.bfloat16)
    tall[(rows - 3) * pitch :] = far[...]
    inner = rows - 4
    sums = column_taps(
        jnp.dot(row_taps(tall, 0, inner, pitch), w1[...], preferred_element_type=jnp.float32)
    )
    hs[...] = inside(silu(sums), masks[0]).astype(jnp.bfloat16)
    temporal = [rows_of(tall, i, 1, pitch) for i in (0, 1, inner, inner + 1)]
    for i, value in enumerate(known_rows(*temporal, w1)):
        known_h[i] = pack(value)

    sums = column_taps(
        jnp.dot(row_taps(hs, 0, inner - 2, pitch), w2[...], preferred_element_type=jnp.float32)
    )
    sums = sums + rows_of(tall, 2, inner - 2, pitch).astype(jnp.float32)
    o_mid[...] = crop(sums, frames, span)
    hidden = [rows_of(hs, i, 1, pitch) for i in (0, 1, inner - 2, inner - 1)]
    for i, value in enumerate(known_rows(*hidden, w2)):
        known_o[i] = pack(value + temporal[i].astype(jnp.float32))
    for i in range(3):
        shown[i] = pack(jnp.concatenate([masks[i]] * frames, axis=0))


def cut(value, frames):
    kept = [value[at + HALO - 1 : at + HALO - 1 + WIDTH] for at in range(0, value.shape[0], KEPT)]
    return jnp.concatenate(kept, axis=0).reshape(frames, WIDTH, value.shape[1]).astype(jnp.bfloat16)


def end_kernel(shown, weight, edges, known_h, known_o, below, w1, w2, o_end, xs):
    frames = below.shape[0]
    pitch = frames * SPAN
    for i in range(3):
        frames_to(xs, i * pitch, frames, sent_row(below, i))
    x = [taps_of(xs, i, pitch) for i in range(3)]
    weights = jnp.concatenate([temporal_taps(weight, taps) for taps in ((1, 2), (0, 1))], axis=1)
    lower, upper = both_taps(x[:2], weights)
    third, first = split_rows(dot_taps([[x[2]], [x[0]]], temporal_taps(weight, (2,))), pitch)
    rows = [
        (pack(first) + edges[0]) * shown[0],
        (pack(lower) + edges[1]) * shown[2],
        pack(upper + third) * shown[2],
    ]
    rows = [row.astype(jnp.bfloat16) for row in rows]
    hidden = end_rows(rows, w1, known_h)
    hidden = [(silu(v) * shown[part]).astype(jnp.bfloat16) for v, part in zip(hidden, (0, 0, 2))]
    sums = end_rows(hidden, w2, known_o)
    sums[2] = sums[2] + rows[0].astype(jnp.float32)
    for i, value in enumerate(sums):
        o_end[i] = cut(value, o_end.shape[1])


def top_kernel(shown, edges, known_h, known_o, above, w1, w2, o_mid, o_end, out):
    rows = [
        above[0] * shown[1],
        (above[1] + edges[1]) * shown[1],
        (above[2] + edges[0]) * shown[0],
    ]
    rows = [row.astype(jnp.bfloat16) for row in rows]
    hidden = top_rows(rows, w1, known_h)
    hidden = [(silu(v) * shown[part]).astype(jnp.bfloat16) for v, part in zip(hidden, (1, 0, 0))]
    sums = top_rows(hidden, w2, known_o)
    sums[0] = sums[0] + rows[2].astype(jnp.float32)
    done = [cut(value, out.shape[1]) for value in sums]
    done += [o_mid[i] for i in range(o_mid.shape[0])] + [o_end[i] for i in range(3)]
    each = out.shape[2]
    for row, value in enumerate(done):
        out[row // each, :, row % each] = value


def per_device(frames_in, temporal_weight, first_weight, second_weight):
    tm, slabs = lax.axis_size("tm"), lax.axis_size("rows")
    planes = slabs // SLABS
    frame_count, row_count, col_count, chans = frames_in.shape
    count = tm * SLABS
    width = col_count // count
    span = SPAN
    size = width + 2 * HALO
    plane_rows = SLABS * row_count
    pitch = tm * span
    column, slab = lax.axis_index("tm"), lax.axis_index("rows")
    plane = slab // SLABS
    first_col = (column * SLABS + slab % SLABS) * width - HALO
    col = lax.broadcasted_iota(jnp.int32, (3, span, chans), 1) + first_col
    part = lax.broadcasted_iota(jnp.int32, (3, span, chans), 0)
    visible = (col >= 0) & (col < col_count)
    visible &= ((part != 1) | (plane > 0)) & ((part != 2) | (plane < planes - 1))
    masks = visible.astype(jnp.float32)
    vmem = pl.BlockSpec(memory_space=pltpu.VMEM)
    params = pltpu.CompilerParams(vmem_limit_bytes=VMEM_BYTES)

    def brain(*shape):
        return jax.ShapeDtypeStruct(shape, jnp.bfloat16)

    def held(*shape):
        return pltpu.VMEM(shape, jnp.bfloat16)

    cut = pl.pallas_call(
        windows_kernel,
        out_shape=brain(count, frame_count * row_count * size, chans),
        in_specs=[vmem],
        out_specs=vmem,
        compiler_params=params,
        name="windows",
    )(frames_in)
    cut, masks = lax.optimization_barrier((cut, masks))
    members = [[m * slabs + z * SLABS + j for m in range(tm) for j in range(SLABS)] for z in range(planes)]
    own = lax.all_to_all(
        cut, ("tm", "rows"), split_axis=0, concat_axis=0, tiled=True, axis_index_groups=members
    ).reshape(tm, SLABS, frame_count * row_count * size, chans)

    reach = range(slabs - SLABS)
    send_down = pl.pallas_call(
        down_kernel,
        out_shape=brain(tm, 6 * size, chans),
        in_specs=[vmem],
        out_specs=vmem,
        compiler_params=params,
        name="down",
    )(own)
    partial = jax.ShapeDtypeStruct((2, tm * KEPT, chans), jnp.float32)
    far, edges_end, send_up = pl.pallas_call(
        edge_kernel,
        out_shape=[brain(pitch, chans), partial, brain(3, tm * KEPT, chans)],
        in_specs=[vmem] * 3,
        out_specs=[vmem] * 3,
        scratch_shapes=[held(3, 3 * pitch, chans)],
        compiler_params=params,
        cost_estimate=pl.CostEstimate(flops=4 * 10**8, bytes_accessed=10**6, transcendentals=0),
        name="edge",
    )(masks, own, temporal_weight)
    above = lax.ppermute(send_up, "rows", [(r, r + SLABS) for r in reach])
    below = lax.ppermute(send_down, "rows", [(r + SLABS, r) for r in reach])

    inner = plane_rows - 4
    known = jax.ShapeDtypeStruct((4, tm * KEPT, chans), jnp.float32)
    edges_top, known_h, known_o, o_mid, shown, w1, w2 = pl.pallas_call(
        inner_kernel,
        out_shape=[
            partial,
            known,
            known,
            brain(inner - 2, tm, width, chans),
            jax.ShapeDtypeStruct((3, tm * KEPT, chans), jnp.float32),
            brain(3 * chans, 3 * chans),
            brain(3 * chans, 3 * chans),
        ],
        in_specs=[vmem] * 6,
        out_specs=[vmem] * 7,
        scratch_shapes=[
            held(3, (inner + 3) * pitch, chans),
            held((inner + 2) * pitch, chans),
            held(inner * pitch, chans),
            held(9 * chans, 3 * chans),
        ],
        compiler_params=params,
        cost_estimate=pl.CostEstimate(flops=10**9, bytes_accessed=4 * 10**6, transcendentals=10**5),
        name="inner",
    )(masks, own, temporal_weight, far, first_weight, second_weight)
    o_end = pl.pallas_call(
        end_kernel,
        out_shape=brain(3, tm, width, chans),
        in_specs=[vmem] * 8,
        out_specs=vmem,
        scratch_shapes=[held(3, 3 * pitch, chans)],
        compiler_params=params,
        cost_estimate=pl.CostEstimate(flops=4 * 10**8, bytes_accessed=10**6, transcendentals=10**5),
        name="end",
    )(shown, temporal_weight, edges_end, known_h, known_o, below, w1, w2)
    encoded = pl.pallas_call(
        top_kernel,
        out_shape=brain(SLABS, tm, row_count, width, chans),
        in_specs=[vmem] * 9,
        out_specs=vmem,
        compiler_params=params,
        name="top",
    )(shown, edges_top, known_h, known_o, above, w1, w2, o_mid, o_end)

    groups = [[z * SLABS + j for j in range(SLABS)] for z in range(planes)]
    encoded = lax.all_to_all(
        encoded, "rows", split_axis=0, concat_axis=0, tiled=True, axis_index_groups=groups
    )
    return jnp.transpose(encoded, (1, 2, 0, 3, 4)).reshape(tm, row_count, SLABS * width, chans)


def solution(mesh):
    placed = (P("tm", "rows", None, None), P(), P(), P())
    return jax.shard_map(
        per_device,
        mesh=mesh,
        in_specs=placed,
        out_specs=P(None, "rows", "tm", None),
        check_vma=False,
    )
```

```python
import jax
import jax.numpy as jnp
from jax import lax
from jax.experimental import pallas as pl
from jax.experimental.pallas import tpu as pltpu
from jax.sharding import PartitionSpec as P

SLABS = 4
HALO = 3
PLANE_ROWS = 8
WIDTH = 16
SPAN = 24
KEPT = 20
VMEM_BYTES = 32 * 1024 * 1024


def windows_kernel(frames, out):
    count = out.shape[0]
    parts = [(f, r) for f in range(frames.shape[0]) for r in range(frames.shape[1])]
    size = out.shape[1] // len(parts)
    width = size - 2 * HALO
    padded = []
    for f, r in parts:
        row = frames[f, r].astype(jnp.float32)
        edge = jnp.zeros((HALO, row.shape[1]), jnp.float32)
        padded.append(jnp.concatenate([edge, row, edge], axis=0))
    for k in range(count):
        cut = [row[k * width : k * width + size] for row in padded]
        out[k] = jnp.concatenate(cut, axis=0).astype(jnp.bfloat16)


def column_taps(sums):
    chans = sums.shape[1] // 3
    left, mid, right = sums[:, :chans], sums[:, chans : 2 * chans], sums[:, 2 * chans :]
    return mid + pltpu.roll(left, 1, 0) + pltpu.roll(right, sums.shape[0] - 1, 0)


def inside(value, mask):
    rows, chans = value.shape
    shown = value.reshape(rows // mask.shape[0], *mask.shape) * mask[...][None]
    return shown.reshape(rows, chans)


def temporal_weight_to(wt, weight):
    chans = weight.shape[3]
    for a in range(3):
        for b in range(3):
            for c in range(3):
                k = (b * 3 + a) * chans
                wt[k : k + chans, c * chans : (c + 1) * chans] = weight[a, b, c]


def plane_weight_to(wt, weight):
    chans = weight.shape[2]
    for b in range(3):
        for c in range(3):
            wt[b * chans : (b + 1) * chans, c * chans : (c + 1) * chans] = weight[b, c]


def part_of(rows, index, size):
    part = rows[index * size : index * size + SPAN]
    if part.shape[0] < SPAN:
        none = jnp.zeros((SPAN - part.shape[0], part.shape[1]), jnp.float32)
        part = jnp.concatenate([part, none], axis=0)
    return part


def frames_to(xs, at, frames, pick):
    for t in range(0, frames, 2):
        here = at + t * SPAN
        for a, f in ((1, 0), (2, 1)):
            pair = jnp.concatenate([pick(t, f), pick(t + 1, f)], axis=0)
            xs[a, here : here + 2 * SPAN] = pair.astype(jnp.bfloat16)
        last = pick(t, 1)
        before = pick(t - 1, 1) if t else jnp.zeros_like(last)
        xs[0, here : here + 2 * SPAN] = jnp.concatenate([before, last], axis=0).astype(jnp.bfloat16)


def own_row(own, row):
    rows_each = PLANE_ROWS // own.shape[1]
    size = own.shape[2] // (2 * rows_each)

    def pick(m, f):
        part = f * rows_each + row % rows_each
        return part_of(own[m, row // rows_each].astype(jnp.float32), part, size)

    return pick


def sent_row(below, row):
    size = below.shape[1] // 6

    def pick(m, f):
        return part_of(below[m].astype(jnp.float32), f * 2 + row if row < 2 else 4 + f, size)

    return pick


def taps_of(xs, i, pitch):
    return jnp.concatenate([xs[a, i * pitch : (i + 1) * pitch] for a in range(3)], axis=1)


def silu(value):
    return value * (0.5 * jnp.tanh(0.5 * value) + 0.5)


def rows_of(ref, first, count, pitch):
    return ref[first * pitch : (first + count) * pitch]


def row_taps(ref, first, count, pitch):
    return jnp.concatenate([rows_of(ref, first + b, count, pitch) for b in range(3)], axis=1)


def temporal_taps(weight, row_taps):
    return jnp.concatenate(
        [
            jnp.concatenate([weight[a, b, c] for c in range(3)], axis=1)
            for b in row_taps
            for a in range(3)
        ],
        axis=0,
    )


def halves(value):
    high = value.astype(jnp.bfloat16).astype(jnp.float32)
    return high, value - high


def pack(value):
    kept = [value[at + 1 : at + 1 + KEPT] for at in range(0, value.shape[0], SPAN)]
    return jnp.concatenate(kept, axis=0)


def down_kernel(own, send):
    size = own.shape[2] // 4
    for m in range(own.shape[0]):
        third = own[m, 1].astype(jnp.float32)
        third = [third[:size], third[2 * size : 3 * size]]
        rows = jnp.concatenate([own[m, 0].astype(jnp.float32), *third], axis=0)
        send[m] = rows.astype(jnp.bfloat16)


def both_taps(pair, weights):
    deep = weights.shape[1] // 2
    lhs = jnp.concatenate(pair, axis=1)
    sums = jnp.dot(lhs, weights, preferred_element_type=jnp.float32)
    return column_taps(sums[:, :deep]), column_taps(sums[:, deep:])


def edge_kernel(masks, own, weight, far, edges, send_up, xs):
    frames = own.shape[0]
    pitch = frames * SPAN
    for i in range(3):
        frames_to(xs, i * pitch, frames, own_row(own, PLANE_ROWS - 3 + i))
    x = [taps_of(xs, i, pitch) for i in range(3)]
    weights = jnp.concatenate([temporal_taps(weight, taps) for taps in ((1, 2), (0, 1))], axis=1)
    lower, upper = both_taps(x[1:], weights)
    third, after = split_rows(dot_taps([[x[0]], [x[2]]], temporal_taps(weight, (0,))), pitch)
    value = inside(lower + third, masks[0])
    far[...] = value.astype(jnp.bfloat16)
    edges[0], edges[1] = last, after = pack(upper), pack(after)
    for i, value in enumerate((pack(value), *halves(last), *halves(after))):
        send_up[i] = value.astype(jnp.bfloat16)


def crop(value, frames, span):
    shape = (value.shape[0] // (frames * span), frames, span, value.shape[1])
    return value.reshape(shape)[:, :, HALO : HALO + WIDTH].astype(jnp.bfloat16)


def dot_taps(lhs, rhs):
    lhs = jnp.concatenate([jnp.concatenate(blocks, axis=1) for blocks in lhs], axis=0)
    return column_taps(jnp.dot(lhs, rhs, preferred_element_type=jnp.float32))


def split_rows(value, pitch):
    return [value[at : at + pitch] for at in range(0, value.shape[0], pitch)]


def known_rows(first, second, before_last, last, weight):
    pitch, chans = first.shape
    none = jnp.zeros_like(first)
    top = dot_taps([[none, first], [first, second]], weight[chans:])
    end = dot_taps([[before_last, last], [last, none]], weight[: 2 * chans])
    return split_rows(top, pitch) + split_rows(end, pitch)


def top_rows(rows, weight, known):
    none, chans = jnp.zeros_like(rows[0]), rows[0].shape[1]
    first = dot_taps([rows], weight[...])
    near = split_rows(dot_taps([rows[1:], [rows[2], none]], weight[: 2 * chans]), none.shape[0])
    return [first, near[0] + known[0], near[1] + known[1]]


def end_rows(rows, weight, known):
    none, chans = jnp.zeros_like(rows[0]), rows[0].shape[1]
    last = dot_taps([rows], weight[...])
    far = split_rows(dot_taps([[none, rows[0]], rows[:2]], weight[chans:]), none.shape[0])
    return [far[0] + known[2], far[1] + known[3], last]


def inner_kernel(
    masks, own, weight, far, w_first, w_second, edges, known_h, known_o, o_mid, shown, w1, w2,
    xs, tall, hs, wt,
):
    frames, span, rows = own.shape[0], SPAN, PLANE_ROWS
    pitch = frames * span
    deep = wt.shape[1]
    temporal_weight_to(wt, weight)
    plane_weight_to(w1, w_first)
    plane_weight_to(w2, w_second)
    for row in range(rows - 1):
        frames_to(xs, row * pitch, frames, own_row(own, row))
    lhs = jnp.concatenate(
        [xs[a, (b + 1) * pitch : (b + rows - 3) * pitch] for b in range(3) for a in range(3)], axis=1
    )
    sums = column_taps(jnp.dot(lhs, wt[...], preferred_element_type=jnp.float32))

    x = [taps_of(xs, i, pitch) for i in range(3)]
    lower, upper = both_taps(x[:2], jnp.concatenate([wt[deep:], wt[: 2 * deep]], axis=1))
    second, before = split_rows(dot_taps([[x[2]], [x[0]]], wt[2 * deep :]), pitch)
    edges[0], edges[1] = pack(lower), pack(before)

    tall[:pitch] = inside(upper + second, masks[0]).astype(jnp.bfloat16)
    tall[pitch : (rows - 3) * pitch] = inside(sums, masks[0]).astype(jnp.bfloat16)
    tall[(rows - 3) * pitch :] = far[...]
    inner = rows - 4
    sums = column_taps(
        jnp.dot(row_taps(tall, 0, inner, pitch), w1[...], preferred_element_type=jnp.float32)
    )
    hs[...] = inside(silu(sums), masks[0]).astype(jnp.bfloat16)
    temporal = [rows_of(tall, i, 1, pitch) for i in (0, 1, inner, inner + 1)]
    for i, value in enumerate(known_rows(*temporal, w1)):
        known_h[i] = pack(value)

    sums = column_taps(
        jnp.dot(row_taps(hs, 0, inner - 2, pitch), w2[...], preferred_element_type=jnp.float32)
    )
    sums = sums + rows_of(tall, 2, inner - 2, pitch).astype(jnp.float32)
    o_mid[...] = crop(sums, frames, span)
    hidden = [rows_of(hs, i, 1, pitch) for i in (0, 1, inner - 2, inner - 1)]
    for i, value in enumerate(known_rows(*hidden, w2)):
        known_o[i] = pack(value + temporal[i].astype(jnp.float32))
    for i in range(3):
        shown[i] = pack(jnp.concatenate([masks[i]] * frames, axis=0))


def cut(value, frames):
    kept = [value[at + HALO - 1 : at + HALO - 1 + WIDTH] for at in range(0, value.shape[0], KEPT)]
    return jnp.concatenate(kept, axis=0).reshape(frames, WIDTH, value.shape[1]).astype(jnp.bfloat16)


def end_kernel(shown, weight, edges, known_h, known_o, below, w1, w2, o_end, xs):
    frames = below.shape[0]
    pitch = frames * SPAN
    for i in range(3):
        frames_to(xs, i * pitch, frames, sent_row(below, i))
    x = [taps_of(xs, i, pitch) for i in range(3)]
    weights = jnp.concatenate([temporal_taps(weight, taps) for taps in ((1, 2), (0, 1))], axis=1)
    lower, upper = both_taps(x[:2], weights)
    third, first = split_rows(dot_taps([[x[2]], [x[0]]], temporal_taps(weight, (2,))), pitch)
    rows = [
        (pack(first) + edges[0]) * shown[0],
        (pack(lower) + edges[1]) * shown[2],
        pack(upper + third) * shown[2],
    ]
    rows = [row.astype(jnp.bfloat16) for row in rows]
    hidden = end_rows(rows, w1, known_h)
    hidden = [(silu(v) * shown[part]).astype(jnp.bfloat16) for v, part in zip(hidden, (0, 0, 2))]
    sums = end_rows(hidden, w2, known_o)
    sums[2] = sums[2] + rows[0].astype(jnp.float32)
    for i, value in enumerate(sums):
        o_end[i] = cut(value, o_end.shape[1])


def join(ref, i):
    return ref[i].astype(jnp.float32) + ref[i + 1].astype(jnp.float32)


def top_kernel(shown, edges, known_h, known_o, above, w1, w2, o_mid, o_end, out):
    rows = [
        above[0] * shown[1],
        (join(above, 1) + edges[1]) * shown[1],
        (join(above, 3) + edges[0]) * shown[0],
    ]
    rows = [row.astype(jnp.bfloat16) for row in rows]
    hidden = top_rows(rows, w1, known_h)
    hidden = [(silu(v) * shown[part]).astype(jnp.bfloat16) for v, part in zip(hidden, (1, 0, 0))]
    sums = top_rows(hidden, w2, known_o)
    sums[0] = sums[0] + rows[2].astype(jnp.float32)
    done = [cut(value, out.shape[1]) for value in sums]
    done += [o_mid[i] for i in range(o_mid.shape[0])] + [o_end[i] for i in range(3)]
    each = out.shape[2]
    for row, value in enumerate(done):
        out[row // each, :, row % each] = value


def per_device(frames_in, temporal_weight, first_weight, second_weight):
    tm, slabs = lax.axis_size("tm"), lax.axis_size("rows")
    planes = slabs // SLABS
    frame_count, row_count, col_count, chans = frames_in.shape
    count = tm * SLABS
    width = col_count // count
    span = SPAN
    size = width + 2 * HALO
    plane_rows = SLABS * row_count
    pitch = tm * span
    column, slab = lax.axis_index("tm"), lax.axis_index("rows")
    plane = slab // SLABS
    first_col = (column * SLABS + slab % SLABS) * width - HALO
    col = lax.broadcasted_iota(jnp.int32, (3, span, chans), 1) + first_col
    part = lax.broadcasted_iota(jnp.int32, (3, span, chans), 0)
    visible = (col >= 0) & (col < col_count)
    visible &= ((part != 1) | (plane > 0)) & ((part != 2) | (plane < planes - 1))
    masks = visible.astype(jnp.float32)
    vmem = pl.BlockSpec(memory_space=pltpu.VMEM)
    params = pltpu.CompilerParams(vmem_limit_bytes=VMEM_BYTES)

    def brain(*shape):
        return jax.ShapeDtypeStruct(shape, jnp.bfloat16)

    def held(*shape):
        return pltpu.VMEM(shape, jnp.bfloat16)

    cut = pl.pallas_call(
        windows_kernel,
        out_shape=brain(count, frame_count * row_count * size, chans),
        in_specs=[vmem],
        out_specs=vmem,
        compiler_params=params,
        name="windows",
    )(frames_in)
    cut, masks = lax.optimization_barrier((cut, masks))
    members = [[m * slabs + z * SLABS + j for m in range(tm) for j in range(SLABS)] for z in range(planes)]
    own = lax.all_to_all(
        cut, ("tm", "rows"), split_axis=0, concat_axis=0, tiled=True, axis_index_groups=members
    ).reshape(tm, SLABS, frame_count * row_count * size, chans)

    reach = range(slabs - SLABS)
    send_down = pl.pallas_call(
        down_kernel,
        out_shape=brain(tm, 6 * size, chans),
        in_specs=[vmem],
        out_specs=vmem,
        compiler_params=params,
        name="down",
    )(own)
    partial = jax.ShapeDtypeStruct((2, tm * KEPT, chans), jnp.float32)
    far, edges_end, send_up = pl.pallas_call(
        edge_kernel,
        out_shape=[brain(pitch, chans), partial, brain(5, tm * KEPT, chans)],
        in_specs=[vmem] * 3,
        out_specs=[vmem] * 3,
        scratch_shapes=[held(3, 3 * pitch, chans)],
        compiler_params=params,
        cost_estimate=pl.CostEstimate(flops=4 * 10**8, bytes_accessed=10**6, transcendentals=0),
        name="edge",
    )(masks, own, temporal_weight)
    above = lax.ppermute(send_up, "rows", [(r, r + SLABS) for r in reach])
    below = lax.ppermute(send_down, "rows", [(r + SLABS, r) for r in reach])

    inner = plane_rows - 4
    known = jax.ShapeDtypeStruct((4, tm * KEPT, chans), jnp.float32)
    edges_top, known_h, known_o, o_mid, shown, w1, w2 = pl.pallas_call(
        inner_kernel,
        out_shape=[
            partial,
            known,
            known,
            brain(inner - 2, tm, width, chans),
            jax.ShapeDtypeStruct((3, tm * KEPT, chans), jnp.float32),
            brain(3 * chans, 3 * chans),
            brain(3 * chans, 3 * chans),
        ],
        in_specs=[vmem] * 6,
        out_specs=[vmem] * 7,
        scratch_shapes=[
            held(3, (inner + 3) * pitch, chans),
            held((inner + 2) * pitch, chans),
            held(inner * pitch, chans),
            held(9 * chans, 3 * chans),
        ],
        compiler_params=params,
        cost_estimate=pl.CostEstimate(flops=10**9, bytes_accessed=4 * 10**6, transcendentals=10**5),
        name="inner",
    )(masks, own, temporal_weight, far, first_weight, second_weight)
    o_end = pl.pallas_call(
        end_kernel,
        out_shape=brain(3, tm, width, chans),
        in_specs=[vmem] * 8,
        out_specs=vmem,
        scratch_shapes=[held(3, 3 * pitch, chans)],
        compiler_params=params,
        cost_estimate=pl.CostEstimate(flops=4 * 10**8, bytes_accessed=10**6, transcendentals=10**5),
        name="end",
    )(shown, temporal_weight, edges_end, known_h, known_o, below, w1, w2)
    encoded = pl.pallas_call(
        top_kernel,
        out_shape=brain(SLABS, tm, row_count, width, chans),
        in_specs=[vmem] * 9,
        out_specs=vmem,
        compiler_params=params,
        name="top",
    )(shown, edges_top, known_h, known_o, above, w1, w2, o_mid, o_end)

    groups = [[z * SLABS + j for j in range(SLABS)] for z in range(planes)]
    encoded = lax.all_to_all(
        encoded, "rows", split_axis=0, concat_axis=0, tiled=True, axis_index_groups=groups
    )
    return jnp.transpose(encoded, (1, 2, 0, 3, 4)).reshape(tm, row_count, SLABS * width, chans)


def solution(mesh):
    placed = (P("tm", "rows", None, None), P(), P(), P())
    return jax.shard_map(
        per_device,
        mesh=mesh,
        in_specs=placed,
        out_specs=P(None, "rows", "tm", None),
        check_vma=False,
    )
```

```python
import jax
import jax.numpy as jnp
from jax import lax
from jax.experimental import pallas as pl
from jax.experimental.pallas import tpu as pltpu
from jax.sharding import PartitionSpec as P

SLABS = 4
HALO = 3
PLANE_ROWS = 8
WIDTH = 16
SPAN = 24
KEPT = 20
VMEM_BYTES = 32 * 1024 * 1024


def windows_kernel(frames, out):
    count = out.shape[0]
    parts = [(f, r) for f in range(frames.shape[0]) for r in range(frames.shape[1])]
    size = out.shape[1] // len(parts)
    width = size - 2 * HALO
    padded = []
    for f, r in parts:
        row = frames[f, r].astype(jnp.float32)
        edge = jnp.zeros((HALO, row.shape[1]), jnp.float32)
        padded.append(jnp.concatenate([edge, row, edge], axis=0))
    for k in range(count):
        cut = [row[k * width : k * width + size] for row in padded]
        out[k] = jnp.concatenate(cut, axis=0).astype(jnp.bfloat16)


def column_taps(sums):
    chans = sums.shape[1] // 3
    left, mid, right = sums[:, :chans], sums[:, chans : 2 * chans], sums[:, 2 * chans :]
    return mid + pltpu.roll(left, 1, 0) + pltpu.roll(right, sums.shape[0] - 1, 0)


def inside(value, mask):
    rows, chans = value.shape
    shown = value.reshape(rows // mask.shape[0], *mask.shape) * mask[...][None]
    return shown.reshape(rows, chans)


def temporal_weight_to(wt, weight):
    chans = weight.shape[3]
    for a in range(3):
        for b in range(3):
            for c in range(3):
                k = (b * 3 + a) * chans
                wt[k : k + chans, c * chans : (c + 1) * chans] = weight[a, b, c]


def plane_weight_to(wt, weight):
    chans = weight.shape[2]
    for b in range(3):
        for c in range(3):
            wt[b * chans : (b + 1) * chans, c * chans : (c + 1) * chans] = weight[b, c]


def frames_to(xs, at, own, row, rows_each):
    frames, chans = own.shape[0], own.shape[3]
    size = own.shape[2] // (2 * rows_each)

    def pick(m, f):
        part = own[m, row // rows_each].astype(jnp.float32)
        start = (f * rows_each + row % rows_each) * size
        part = part[start : start + SPAN]
        if part.shape[0] < SPAN:
            part = jnp.concatenate([part, jnp.zeros((SPAN - part.shape[0], chans), jnp.float32)], axis=0)
        return part

    for t in range(0, frames, 2):
        here = at + t * SPAN
        for a, f in ((1, 0), (2, 1)):
            pair = jnp.concatenate([pick(t, f), pick(t + 1, f)], axis=0)
            xs[a, here : here + 2 * SPAN] = pair.astype(jnp.bfloat16)
        before = pick(t - 1, 1) if t else jnp.zeros((SPAN, chans), jnp.float32)
        pair = jnp.concatenate([before, pick(t, 1)], axis=0)
        xs[0, here : here + 2 * SPAN] = pair.astype(jnp.bfloat16)


def silu(value):
    return value * (0.5 * jnp.tanh(0.5 * value) + 0.5)


def rows_of(ref, first, count, pitch):
    return ref[first * pitch : (first + count) * pitch]


def row_taps(ref, first, count, pitch):
    return jnp.concatenate([rows_of(ref, first + b, count, pitch) for b in range(3)], axis=1)


def temporal_taps(weight, row_taps):
    return jnp.concatenate(
        [
            jnp.concatenate([weight[a, b, c] for c in range(3)], axis=1)
            for b in row_taps
            for a in range(3)
        ],
        axis=0,
    )


def pack(value):
    kept = [value[at + 1 : at + 1 + KEPT] for at in range(0, value.shape[0], SPAN)]
    return jnp.concatenate(kept, axis=0)


def edge_kernel(masks, own, weight, t_edge, edges, send_down, send_up, xs):
    frames, span, chans = own.shape[0], SPAN, own.shape[3]
    rows_each = PLANE_ROWS // own.shape[1]
    rows = own.shape[1] * rows_each
    pitch = frames * span

    for i in range(3):
        frames_to(xs, i * pitch, own, i, rows_each)
        frames_to(xs, (3 + i) * pitch, own, rows - 3 + i, rows_each)

    def taps_of(i):
        return jnp.concatenate([xs[a, i * pitch : (i + 1) * pitch] for a in range(3)], axis=1)

    deep = 3 * chans
    x = [taps_of(i) for i in range(6)]
    sums = jnp.dot(
        jnp.concatenate([jnp.concatenate(pair, axis=1) for pair in (x[0:2], x[4:6])], axis=0),
        jnp.concatenate([temporal_taps(weight, taps) for taps in ((1, 2), (0, 1))], axis=1),
        preferred_element_type=jnp.float32,
    )
    lower, upper = column_taps(sums[:, :deep]), column_taps(sums[:, deep:])
    first, last = lower[:pitch], upper[pitch:]
    second, before = split_rows(dot_taps([[x[2]], [x[0]]], temporal_taps(weight, (2,))), pitch)
    third, after = split_rows(dot_taps([[x[3]], [x[5]]], temporal_taps(weight, (0,))), pitch)
    near = inside(upper[:pitch] + second, masks[0])
    far = inside(lower[pitch:] + third, masks[0])
    t_edge[0], t_edge[1] = near.astype(jnp.bfloat16), far.astype(jnp.bfloat16)
    first, last, before, after = [pack(value) for value in (first, last, before, after)]
    edges[0], edges[1], edges[2], edges[3] = first, last, before, after
    for i, value in enumerate((pack(far), last, after)):
        send_up[i] = value.astype(jnp.bfloat16)
    for i, value in enumerate((pack(near), first, before)):
        send_down[i] = value.astype(jnp.bfloat16)


def crop(value, frames, span):
    shape = (value.shape[0] // (frames * span), frames, span, value.shape[1])
    return value.reshape(shape)[:, :, HALO : HALO + WIDTH].astype(jnp.bfloat16)


def dot_taps(lhs, rhs):
    lhs = jnp.concatenate([jnp.concatenate(blocks, axis=1) for blocks in lhs], axis=0)
    return column_taps(jnp.dot(lhs, rhs, preferred_element_type=jnp.float32))


def split_rows(value, pitch):
    return [value[at : at + pitch] for at in range(0, value.shape[0], pitch)]


def known_rows(first, second, before_last, last, weight):
    pitch, chans = first.shape
    none = jnp.zeros_like(first)
    top = dot_taps([[none, first], [first, second]], weight[chans:])
    end = dot_taps([[before_last, last], [last, none]], weight[: 2 * chans])
    return split_rows(top, pitch) + split_rows(end, pitch)


def pair_rows(pair, weight):
    deep, chans = weight.shape[1], weight.shape[0] // 3
    sums = jnp.dot(
        jnp.concatenate(pair, axis=1),
        jnp.concatenate([weight[chans:], weight[: 2 * chans]], axis=1),
        preferred_element_type=jnp.float32,
    )
    return column_taps(sums[:, :deep]), column_taps(sums[:, deep:])


def top_rows(rows, weight, known):
    pitch, chans = rows[0].shape
    lower, upper = pair_rows(rows[1:], weight)
    through = split_rows(dot_taps([[rows[0]], [rows[2]]], weight[:chans]), pitch)
    return [lower + through[0], upper + known[0], through[1] + known[1]]


def end_rows(rows, weight, known):
    pitch, chans = rows[0].shape
    lower, upper = pair_rows(rows[:2], weight)
    through = split_rows(dot_taps([[rows[0]], [rows[2]]], weight[2 * chans :]), pitch)
    return [through[0] + known[2], lower + known[3], upper + through[1]]


def inner_kernel(
    masks, own, weight, t_edge, w_first, w_second, known_h, known_o, o_mid, shown, w1, w2,
    xs, tall, hs, wt,
):
    frames, span = own.shape[0], SPAN
    rows_each = PLANE_ROWS // own.shape[1]
    rows = own.shape[1] * rows_each
    pitch = frames * span
    temporal_weight_to(wt, weight)
    plane_weight_to(w1, w_first)
    plane_weight_to(w2, w_second)
    for row in range(1, rows - 1):
        frames_to(xs, (row - 1) * pitch, own, row, rows_each)
    lhs = jnp.concatenate(
        [xs[a, b * pitch : (b + rows - 4) * pitch] for b in range(3) for a in range(3)], axis=1
    )
    sums = column_taps(jnp.dot(lhs, wt[...], preferred_element_type=jnp.float32))

    tall[:pitch] = t_edge[0]
    tall[pitch : (rows - 3) * pitch] = inside(sums, masks[0]).astype(jnp.bfloat16)
    tall[(rows - 3) * pitch :] = t_edge[1]
    inner = rows - 4
    sums = column_taps(
        jnp.dot(row_taps(tall, 0, inner, pitch), w1[...], preferred_element_type=jnp.float32)
    )
    hs[...] = inside(silu(sums), masks[0]).astype(jnp.bfloat16)
    temporal = [rows_of(tall, i, 1, pitch) for i in (0, 1, inner, inner + 1)]
    for i, value in enumerate(known_rows(*temporal, w1)):
        known_h[i] = pack(value)

    sums = column_taps(
        jnp.dot(row_taps(hs, 0, inner - 2, pitch), w2[...], preferred_element_type=jnp.float32)
    )
    sums = sums + rows_of(tall, 2, inner - 2, pitch).astype(jnp.float32)
    o_mid[...] = crop(sums, frames, span)
    hidden = [rows_of(hs, i, 1, pitch) for i in (0, 1, inner - 2, inner - 1)]
    for i, value in enumerate(known_rows(*hidden, w2)):
        known_o[i] = pack(value + temporal[i].astype(jnp.float32))
    for i in range(3):
        shown[i] = pack(jnp.concatenate([masks[i]] * frames, axis=0))


def cut(value, frames):
    kept = [value[at + HALO - 1 : at + HALO - 1 + WIDTH] for at in range(0, value.shape[0], KEPT)]
    return jnp.concatenate(kept, axis=0).reshape(frames, WIDTH, value.shape[1]).astype(jnp.bfloat16)


def end_kernel(shown, edges, known_h, known_o, below, w1, w2, o_end):
    rows = [
        (below[2] + edges[1]) * shown[0],
        (below[1] + edges[3]) * shown[2],
        below[0] * shown[2],
    ]
    rows = [row.astype(jnp.bfloat16) for row in rows]
    hidden = end_rows(rows, w1, known_h)
    hidden = [(silu(v) * shown[part]).astype(jnp.bfloat16) for v, part in zip(hidden, (0, 0, 2))]
    sums = end_rows(hidden, w2, known_o)
    sums[2] = sums[2] + rows[0].astype(jnp.float32)
    for i, value in enumerate(sums):
        o_end[i] = cut(value, o_end.shape[1])


def top_kernel(shown, edges, known_h, known_o, above, w1, w2, o_mid, o_end, out):
    rows = [
        above[0] * shown[1],
        (above[1] + edges[2]) * shown[1],
        (above[2] + edges[0]) * shown[0],
    ]
    rows = [row.astype(jnp.bfloat16) for row in rows]
    hidden = top_rows(rows, w1, known_h)
    hidden = [(silu(v) * shown[part]).astype(jnp.bfloat16) for v, part in zip(hidden, (1, 0, 0))]
    sums = top_rows(hidden, w2, known_o)
    sums[0] = sums[0] + rows[2].astype(jnp.float32)
    done = [cut(value, out.shape[1]) for value in sums]
    done += [o_mid[i] for i in range(o_mid.shape[0])] + [o_end[i] for i in range(3)]
    each = out.shape[2]
    for row, value in enumerate(done):
        out[row // each, :, row % each] = value


def per_device(frames_in, temporal_weight, first_weight, second_weight):
    tm, slabs = lax.axis_size("tm"), lax.axis_size("rows")
    planes = slabs // SLABS
    frame_count, row_count, col_count, chans = frames_in.shape
    count = tm * SLABS
    width = col_count // count
    span = SPAN
    size = width + 2 * HALO
    plane_rows = SLABS * row_count
    pitch = tm * span
    column, slab = lax.axis_index("tm"), lax.axis_index("rows")
    plane = slab // SLABS
    first_col = (column * SLABS + slab % SLABS) * width - HALO
    col = lax.broadcasted_iota(jnp.int32, (3, span, chans), 1) + first_col
    part = lax.broadcasted_iota(jnp.int32, (3, span, chans), 0)
    visible = (col >= 0) & (col < col_count)
    visible &= ((part != 1) | (plane > 0)) & ((part != 2) | (plane < planes - 1))
    masks = visible.astype(jnp.float32)
    vmem = pl.BlockSpec(memory_space=pltpu.VMEM)
    params = pltpu.CompilerParams(vmem_limit_bytes=VMEM_BYTES)

    def brain(*shape):
        return jax.ShapeDtypeStruct(shape, jnp.bfloat16)

    def held(*shape):
        return pltpu.VMEM(shape, jnp.bfloat16)

    cut = pl.pallas_call(
        windows_kernel,
        out_shape=brain(count, frame_count * row_count * size, chans),
        in_specs=[vmem],
        out_specs=vmem,
        compiler_params=params,
        name="windows",
    )(frames_in)
    cut, masks = lax.optimization_barrier((cut, masks))
    members = [[m * slabs + z * SLABS + j for m in range(tm) for j in range(SLABS)] for z in range(planes)]
    own = lax.all_to_all(
        cut, ("tm", "rows"), split_axis=0, concat_axis=0, tiled=True, axis_index_groups=members
    ).reshape(tm, SLABS, frame_count * row_count * size, chans)

    t_edge, edges, send_down, send_up = pl.pallas_call(
        edge_kernel,
        out_shape=[
            brain(2, pitch, chans),
            jax.ShapeDtypeStruct((4, tm * KEPT, chans), jnp.float32),
            brain(3, tm * KEPT, chans),
            brain(3, tm * KEPT, chans),
        ],
        in_specs=[vmem] * 3,
        out_specs=[vmem] * 4,
        scratch_shapes=[held(3, 6 * pitch, chans)],
        compiler_params=params,
        name="edge",
    )(masks, own, temporal_weight)

    reach = range(slabs - SLABS)
    above = lax.ppermute(send_up, "rows", [(r, r + SLABS) for r in reach])
    below = lax.ppermute(send_down, "rows", [(r + SLABS, r) for r in reach])

    inner = plane_rows - 4
    partial = jax.ShapeDtypeStruct((4, tm * KEPT, chans), jnp.float32)
    known_h, known_o, o_mid, shown, w1, w2 = pl.pallas_call(
        inner_kernel,
        out_shape=[
            partial,
            partial,
            brain(inner - 2, tm, width, chans),
            jax.ShapeDtypeStruct((3, tm * KEPT, chans), jnp.float32),
            brain(3 * chans, 3 * chans),
            brain(3 * chans, 3 * chans),
        ],
        in_specs=[vmem] * 6,
        out_specs=[vmem] * 6,
        scratch_shapes=[
            held(3, (inner + 2) * pitch, chans),
            held((inner + 2) * pitch, chans),
            held(inner * pitch, chans),
            held(9 * chans, 3 * chans),
        ],
        compiler_params=params,
        cost_estimate=pl.CostEstimate(flops=10**9, bytes_accessed=4 * 10**6, transcendentals=10**5),
        name="inner",
    )(masks, own, temporal_weight, t_edge, first_weight, second_weight)
    o_end = pl.pallas_call(
        end_kernel,
        out_shape=brain(3, tm, width, chans),
        in_specs=[vmem] * 7,
        out_specs=vmem,
        compiler_params=params,
        cost_estimate=pl.CostEstimate(flops=4 * 10**8, bytes_accessed=10**6, transcendentals=10**5),
        name="end",
    )(shown, edges, known_h, known_o, below, w1, w2)
    encoded = pl.pallas_call(
        top_kernel,
        out_shape=brain(SLABS, tm, row_count, width, chans),
        in_specs=[vmem] * 9,
        out_specs=vmem,
        compiler_params=params,
        name="top",
    )(shown, edges, known_h, known_o, above, w1, w2, o_mid, o_end)

    groups = [[z * SLABS + j for j in range(SLABS)] for z in range(planes)]
    encoded = lax.all_to_all(
        encoded, "rows", split_axis=0, concat_axis=0, tiled=True, axis_index_groups=groups
    )
    return jnp.transpose(encoded, (1, 2, 0, 3, 4)).reshape(tm, row_count, SLABS * width, chans)


def solution(mesh):
    placed = (P("tm", "rows", None, None), P(), P(), P())
    return jax.shard_map(
        per_device,
        mesh=mesh,
        in_specs=placed,
        out_specs=P(None, "rows", "tm", None),
        check_vma=False,
    )
```

```python
import jax
import jax.numpy as jnp
from jax import lax
from jax.experimental import pallas as pl
from jax.experimental.pallas import tpu as pltpu
from jax.sharding import PartitionSpec as P

SLABS = 4
HALO = 3
PLANE_ROWS = 8
WIDTH = 16
SPAN = 24
KEPT = 20
VMEM_BYTES = 32 * 1024 * 1024


def windows_kernel(frames, out):
    count = out.shape[0]
    parts = [(f, r) for f in range(frames.shape[0]) for r in range(frames.shape[1])]
    size = out.shape[1] // len(parts)
    width = size - 2 * HALO
    padded = []
    for f, r in parts:
        row = frames[f, r].astype(jnp.float32)
        edge = jnp.zeros((HALO, row.shape[1]), jnp.float32)
        padded.append(jnp.concatenate([edge, row, edge], axis=0))
    for k in range(count):
        cut = [row[k * width : k * width + size] for row in padded]
        out[k] = jnp.concatenate(cut, axis=0).astype(jnp.bfloat16)


def column_taps(sums):
    chans = sums.shape[1] // 3
    left, mid, right = sums[:, :chans], sums[:, chans : 2 * chans], sums[:, 2 * chans :]
    return mid + pltpu.roll(left, 1, 0) + pltpu.roll(right, sums.shape[0] - 1, 0)


def inside(value, mask):
    rows, chans = value.shape
    shown = value.reshape(rows // mask.shape[0], *mask.shape) * mask[...][None]
    return shown.reshape(rows, chans)


def temporal_weight_to(wt, weight):
    chans = weight.shape[3]
    for a in range(3):
        for b in range(3):
            for c in range(3):
                k = (b * 3 + a) * chans
                wt[k : k + chans, c * chans : (c + 1) * chans] = weight[a, b, c]


def plane_weight_to(wt, weight):
    chans = weight.shape[2]
    for b in range(3):
        for c in range(3):
            wt[b * chans : (b + 1) * chans, c * chans : (c + 1) * chans] = weight[b, c]


def frames_to(xs, at, own, row, rows_each):
    frames, chans = own.shape[0], own.shape[3]
    size = own.shape[2] // (2 * rows_each)

    def pick(m, f):
        part = own[m, row // rows_each].astype(jnp.float32)
        start = (f * rows_each + row % rows_each) * size
        part = part[start : start + SPAN]
        if part.shape[0] < SPAN:
            part = jnp.concatenate([part, jnp.zeros((SPAN - part.shape[0], chans), jnp.float32)], axis=0)
        return part

    for t in range(0, frames, 2):
        here = at + t * SPAN
        for a, f in ((1, 0), (2, 1)):
            pair = jnp.concatenate([pick(t, f), pick(t + 1, f)], axis=0)
            xs[a, here : here + 2 * SPAN] = pair.astype(jnp.bfloat16)
        before = pick(t - 1, 1) if t else jnp.zeros((SPAN, chans), jnp.float32)
        pair = jnp.concatenate([before, pick(t, 1)], axis=0)
        xs[0, here : here + 2 * SPAN] = pair.astype(jnp.bfloat16)


def silu(value):
    return value * (0.5 * jnp.tanh(0.5 * value) + 0.5)


def rows_of(ref, first, count, pitch):
    return ref[first * pitch : (first + count) * pitch]


def row_taps(ref, first, count, pitch):
    return jnp.concatenate([rows_of(ref, first + b, count, pitch) for b in range(3)], axis=1)


def temporal_taps(weight, row_taps):
    return jnp.concatenate(
        [
            jnp.concatenate([weight[a, b, c] for c in range(3)], axis=1)
            for b in row_taps
            for a in range(3)
        ],
        axis=0,
    )


def pack(value):
    kept = [value[at + 1 : at + 1 + KEPT] for at in range(0, value.shape[0], SPAN)]
    return jnp.concatenate(kept, axis=0)


def side_kernel(at, masks, own, weight, near, edges, send, xs):
    frames, chans = own.shape[0], own.shape[3]
    pitch = frames * SPAN
    deep = 3 * chans
    for i in range(3):
        frames_to(xs, i * pitch, own, at + i, PLANE_ROWS // own.shape[1])
    x = [
        jnp.concatenate([xs[a, i * pitch : (i + 1) * pitch] for a in range(3)], axis=1)
        for i in range(3)
    ]
    pair, (inner, outer), tap = (x[:2], (x[2], x[0]), 2) if at == 0 else (x[1:], (x[0], x[2]), 0)
    sums = jnp.dot(
        jnp.concatenate(pair, axis=1),
        jnp.concatenate([temporal_taps(weight, taps) for taps in ((1, 2), (0, 1))], axis=1),
        preferred_element_type=jnp.float32,
    )
    lower, upper = column_taps(sums[:, :deep]), column_taps(sums[:, deep:])
    part, whole = (lower, upper) if at == 0 else (upper, lower)
    more, beside = split_rows(dot_taps([[inner], [outer]], temporal_taps(weight, (tap,))), pitch)
    whole = inside(whole + more, masks[0])
    near[...] = whole.astype(jnp.bfloat16)
    part, beside = pack(part), pack(beside)
    edges[0], edges[1] = part, beside
    for i, value in enumerate((pack(whole), part, beside)):
        send[i] = value.astype(jnp.bfloat16)


def crop(value, frames, span):
    shape = (value.shape[0] // (frames * span), frames, span, value.shape[1])
    return value.reshape(shape)[:, :, HALO : HALO + WIDTH].astype(jnp.bfloat16)


def dot_taps(lhs, rhs):
    lhs = jnp.concatenate([jnp.concatenate(blocks, axis=1) for blocks in lhs], axis=0)
    return column_taps(jnp.dot(lhs, rhs, preferred_element_type=jnp.float32))


def split_rows(value, pitch):
    return [value[at : at + pitch] for at in range(0, value.shape[0], pitch)]


def known_rows(first, second, before_last, last, weight):
    pitch, chans = first.shape
    none = jnp.zeros_like(first)
    top = dot_taps([[none, first], [first, second]], weight[chans:])
    end = dot_taps([[before_last, last], [last, none]], weight[: 2 * chans])
    return split_rows(top, pitch) + split_rows(end, pitch)


def pair_rows(pair, weight):
    deep, chans = weight.shape[1], weight.shape[0] // 3
    sums = jnp.dot(
        jnp.concatenate(pair, axis=1),
        jnp.concatenate([weight[chans:], weight[: 2 * chans]], axis=1),
        preferred_element_type=jnp.float32,
    )
    return column_taps(sums[:, :deep]), column_taps(sums[:, deep:])


def top_rows(rows, weight, known):
    pitch, chans = rows[0].shape
    lower, upper = pair_rows(rows[1:], weight)
    through = split_rows(dot_taps([[rows[0]], [rows[2]]], weight[:chans]), pitch)
    return [lower + through[0], upper + known[0], through[1] + known[1]]


def end_rows(rows, weight, known):
    pitch, chans = rows[0].shape
    lower, upper = pair_rows(rows[:2], weight)
    through = split_rows(dot_taps([[rows[0]], [rows[2]]], weight[2 * chans :]), pitch)
    return [through[0] + known[2], lower + known[3], upper + through[1]]


def inner_kernel(
    masks, own, weight, near, far, w_first, w_second, known_h, known_o, o_mid, shown, w1, w2,
    xs, tall, hs, wt,
):
    frames, span = own.shape[0], SPAN
    rows_each = PLANE_ROWS // own.shape[1]
    rows = own.shape[1] * rows_each
    pitch = frames * span
    temporal_weight_to(wt, weight)
    plane_weight_to(w1, w_first)
    plane_weight_to(w2, w_second)
    for row in range(1, rows - 1):
        frames_to(xs, (row - 1) * pitch, own, row, rows_each)
    lhs = jnp.concatenate(
        [xs[a, b * pitch : (b + rows - 4) * pitch] for b in range(3) for a in range(3)], axis=1
    )
    sums = column_taps(jnp.dot(lhs, wt[...], preferred_element_type=jnp.float32))

    tall[:pitch] = near[...]
    tall[pitch : (rows - 3) * pitch] = inside(sums, masks[0]).astype(jnp.bfloat16)
    tall[(rows - 3) * pitch :] = far[...]
    inner = rows - 4
    sums = column_taps(
        jnp.dot(row_taps(tall, 0, inner, pitch), w1[...], preferred_element_type=jnp.float32)
    )
    hs[...] = inside(silu(sums), masks[0]).astype(jnp.bfloat16)
    temporal = [rows_of(tall, i, 1, pitch) for i in (0, 1, inner, inner + 1)]
    for i, value in enumerate(known_rows(*temporal, w1)):
        known_h[i] = pack(value)

    sums = column_taps(
        jnp.dot(row_taps(hs, 0, inner - 2, pitch), w2[...], preferred_element_type=jnp.float32)
    )
    sums = sums + rows_of(tall, 2, inner - 2, pitch).astype(jnp.float32)
    o_mid[...] = crop(sums, frames, span)
    hidden = [rows_of(hs, i, 1, pitch) for i in (0, 1, inner - 2, inner - 1)]
    for i, value in enumerate(known_rows(*hidden, w2)):
        known_o[i] = pack(value + temporal[i].astype(jnp.float32))
    for i in range(3):
        shown[i] = pack(jnp.concatenate([masks[i]] * frames, axis=0))


def cut(value, frames):
    kept = [value[at + HALO - 1 : at + HALO - 1 + WIDTH] for at in range(0, value.shape[0], KEPT)]
    return jnp.concatenate(kept, axis=0).reshape(frames, WIDTH, value.shape[1]).astype(jnp.bfloat16)


def end_kernel(shown, edges, known_h, known_o, below, w1, w2, o_end):
    rows = [
        (below[2] + edges[0]) * shown[0],
        (below[1] + edges[1]) * shown[2],
        below[0] * shown[2],
    ]
    rows = [row.astype(jnp.bfloat16) for row in rows]
    hidden = end_rows(rows, w1, known_h)
    hidden = [(silu(v) * shown[part]).astype(jnp.bfloat16) for v, part in zip(hidden, (0, 0, 2))]
    sums = end_rows(hidden, w2, known_o)
    sums[2] = sums[2] + rows[0].astype(jnp.float32)
    for i, value in enumerate(sums):
        o_end[i] = cut(value, o_end.shape[1])


def top_kernel(shown, edges, known_h, known_o, above, w1, w2, o_mid, o_end, out):
    rows = [
        above[0] * shown[1],
        (above[1] + edges[1]) * shown[1],
        (above[2] + edges[0]) * shown[0],
    ]
    rows = [row.astype(jnp.bfloat16) for row in rows]
    hidden = top_rows(rows, w1, known_h)
    hidden = [(silu(v) * shown[part]).astype(jnp.bfloat16) for v, part in zip(hidden, (1, 0, 0))]
    sums = top_rows(hidden, w2, known_o)
    sums[0] = sums[0] + rows[2].astype(jnp.float32)
    done = [cut(value, out.shape[1]) for value in sums]
    done += [o_mid[i] for i in range(o_mid.shape[0])] + [o_end[i] for i in range(3)]
    each = out.shape[2]
    for row, value in enumerate(done):
        out[row // each, :, row % each] = value


def per_device(frames_in, temporal_weight, first_weight, second_weight):
    tm, slabs = lax.axis_size("tm"), lax.axis_size("rows")
    planes = slabs // SLABS
    frame_count, row_count, col_count, chans = frames_in.shape
    count = tm * SLABS
    width = col_count // count
    span = SPAN
    size = width + 2 * HALO
    plane_rows = SLABS * row_count
    pitch = tm * span
    column, slab = lax.axis_index("tm"), lax.axis_index("rows")
    plane = slab // SLABS
    first_col = (column * SLABS + slab % SLABS) * width - HALO
    col = lax.broadcasted_iota(jnp.int32, (3, span, chans), 1) + first_col
    part = lax.broadcasted_iota(jnp.int32, (3, span, chans), 0)
    visible = (col >= 0) & (col < col_count)
    visible &= ((part != 1) | (plane > 0)) & ((part != 2) | (plane < planes - 1))
    masks = visible.astype(jnp.float32)
    vmem = pl.BlockSpec(memory_space=pltpu.VMEM)
    params = pltpu.CompilerParams(vmem_limit_bytes=VMEM_BYTES)

    def brain(*shape):
        return jax.ShapeDtypeStruct(shape, jnp.bfloat16)

    def held(*shape):
        return pltpu.VMEM(shape, jnp.bfloat16)

    cut = pl.pallas_call(
        windows_kernel,
        out_shape=brain(count, frame_count * row_count * size, chans),
        in_specs=[vmem],
        out_specs=vmem,
        compiler_params=params,
        name="windows",
    )(frames_in)
    cut, masks = lax.optimization_barrier((cut, masks))
    members = [[m * slabs + z * SLABS + j for m in range(tm) for j in range(SLABS)] for z in range(planes)]
    own = lax.all_to_all(
        cut, ("tm", "rows"), split_axis=0, concat_axis=0, tiled=True, axis_index_groups=members
    ).reshape(tm, SLABS, frame_count * row_count * size, chans)

    def side(at, name):
        return pl.pallas_call(
            lambda *refs: side_kernel(at, *refs),
            out_shape=[
                brain(pitch, chans),
                jax.ShapeDtypeStruct((2, tm * KEPT, chans), jnp.float32),
                brain(3, tm * KEPT, chans),
            ],
            in_specs=[vmem] * 3,
            out_specs=[vmem] * 3,
            scratch_shapes=[held(3, 3 * pitch, chans)],
            compiler_params=params,
            cost_estimate=pl.CostEstimate(flops=4 * 10**8, bytes_accessed=10**6, transcendentals=0),
            name=name,
        )(masks, own, temporal_weight)

    near, edges_top, send_down = side(0, "first")
    far, edges_end, send_up = side(plane_rows - 3, "last")

    reach = range(slabs - SLABS)
    above = lax.ppermute(send_up, "rows", [(r, r + SLABS) for r in reach])
    below = lax.ppermute(send_down, "rows", [(r + SLABS, r) for r in reach])

    inner = plane_rows - 4
    partial = jax.ShapeDtypeStruct((4, tm * KEPT, chans), jnp.float32)
    known_h, known_o, o_mid, shown, w1, w2 = pl.pallas_call(
        inner_kernel,
        out_shape=[
            partial,
            partial,
            brain(inner - 2, tm, width, chans),
            jax.ShapeDtypeStruct((3, tm * KEPT, chans), jnp.float32),
            brain(3 * chans, 3 * chans),
            brain(3 * chans, 3 * chans),
        ],
        in_specs=[vmem] * 7,
        out_specs=[vmem] * 6,
        scratch_shapes=[
            held(3, (inner + 2) * pitch, chans),
            held((inner + 2) * pitch, chans),
            held(inner * pitch, chans),
            held(9 * chans, 3 * chans),
        ],
        compiler_params=params,
        cost_estimate=pl.CostEstimate(flops=10**9, bytes_accessed=4 * 10**6, transcendentals=10**5),
        name="inner",
    )(masks, own, temporal_weight, near, far, first_weight, second_weight)
    o_end = pl.pallas_call(
        end_kernel,
        out_shape=brain(3, tm, width, chans),
        in_specs=[vmem] * 7,
        out_specs=vmem,
        compiler_params=params,
        cost_estimate=pl.CostEstimate(flops=4 * 10**8, bytes_accessed=10**6, transcendentals=10**5),
        name="end",
    )(shown, edges_end, known_h, known_o, below, w1, w2)
    encoded = pl.pallas_call(
        top_kernel,
        out_shape=brain(SLABS, tm, row_count, width, chans),
        in_specs=[vmem] * 9,
        out_specs=vmem,
        compiler_params=params,
        name="top",
    )(shown, edges_top, known_h, known_o, above, w1, w2, o_mid, o_end)

    groups = [[z * SLABS + j for j in range(SLABS)] for z in range(planes)]
    encoded = lax.all_to_all(
        encoded, "rows", split_axis=0, concat_axis=0, tiled=True, axis_index_groups=groups
    )
    return jnp.transpose(encoded, (1, 2, 0, 3, 4)).reshape(tm, row_count, SLABS * width, chans)


def solution(mesh):
    placed = (P("tm", "rows", None, None), P(), P(), P())
    return jax.shard_map(
        per_device,
        mesh=mesh,
        in_specs=placed,
        out_specs=P(None, "rows", "tm", None),
        check_vma=False,
    )
```

```python
import jax
import jax.numpy as jnp
from jax import lax
from jax.experimental import pallas as pl
from jax.experimental.pallas import tpu as pltpu
from jax.sharding import PartitionSpec as P

SLABS = 4
HALO = 3
PLANE_ROWS = 8
WIDTH = 16
SPAN = 24
KEPT = 20
VMEM_BYTES = 32 * 1024 * 1024


def windows_kernel(frames, out):
    count = out.shape[0]
    parts = [(f, r) for f in range(frames.shape[0]) for r in range(frames.shape[1])]
    size = out.shape[1] // len(parts)
    width = size - 2 * HALO
    padded = []
    for f, r in parts:
        row = frames[f, r].astype(jnp.float32)
        edge = jnp.zeros((HALO, row.shape[1]), jnp.float32)
        padded.append(jnp.concatenate([edge, row, edge], axis=0))
    for k in range(count):
        cut = [row[k * width : k * width + size] for row in padded]
        out[k] = jnp.concatenate(cut, axis=0).astype(jnp.bfloat16)


def column_taps(sums):
    chans = sums.shape[1] // 3
    left, mid, right = sums[:, :chans], sums[:, chans : 2 * chans], sums[:, 2 * chans :]
    return mid + pltpu.roll(left, 1, 0) + pltpu.roll(right, sums.shape[0] - 1, 0)


def inside(value, mask):
    rows, chans = value.shape
    shown = value.reshape(rows // mask.shape[0], *mask.shape) * mask[...][None]
    return shown.reshape(rows, chans)


def temporal_weight_to(wt, weight):
    chans = weight.shape[3]
    for a in range(3):
        for b in range(3):
            for c in range(3):
                k = (b * 3 + a) * chans
                wt[k : k + chans, c * chans : (c + 1) * chans] = weight[a, b, c]


def plane_weight_to(wt, weight):
    chans = weight.shape[2]
    for b in range(3):
        for c in range(3):
            wt[b * chans : (b + 1) * chans, c * chans : (c + 1) * chans] = weight[b, c]


def part_of(rows, index, size):
    part = rows[index * size : index * size + SPAN]
    if part.shape[0] < SPAN:
        none = jnp.zeros((SPAN - part.shape[0], part.shape[1]), jnp.float32)
        part = jnp.concatenate([part, none], axis=0)
    return part


def frames_to(xs, at, frames, pick):
    for t in range(0, frames, 2):
        here = at + t * SPAN
        for a, f in ((1, 0), (2, 1)):
            pair = jnp.concatenate([pick(t, f), pick(t + 1, f)], axis=0)
            xs[a, here : here + 2 * SPAN] = pair.astype(jnp.bfloat16)
        last = pick(t, 1)
        before = pick(t - 1, 1) if t else jnp.zeros_like(last)
        xs[0, here : here + 2 * SPAN] = jnp.concatenate([before, last], axis=0).astype(jnp.bfloat16)


def own_row(own, row):
    rows_each = PLANE_ROWS // own.shape[1]
    size = own.shape[2] // (2 * rows_each)

    def pick(m, f):
        part = f * rows_each + row % rows_each
        return part_of(own[m, row // rows_each].astype(jnp.float32), part, size)

    return pick


def sent_row(below, row):
    size = below.shape[1] // 6

    def pick(m, f):
        return part_of(below[m].astype(jnp.float32), f * 2 + row if row < 2 else 4 + f, size)

    return pick


def taps_of(xs, i, pitch):
    return jnp.concatenate([xs[a, i * pitch : (i + 1) * pitch] for a in range(3)], axis=1)


def silu(value):
    return value * (0.5 * jnp.tanh(0.5 * value) + 0.5)


def rows_of(ref, first, count, pitch):
    return ref[first * pitch : (first + count) * pitch]


def row_taps(ref, first, count, pitch):
    return jnp.concatenate([rows_of(ref, first + b, count, pitch) for b in range(3)], axis=1)


def temporal_taps(weight, row_taps):
    return jnp.concatenate(
        [
            jnp.concatenate([weight[a, b, c] for c in range(3)], axis=1)
            for b in row_taps
            for a in range(3)
        ],
        axis=0,
    )


def pack(value):
    kept = [value[at + 1 : at + 1 + KEPT] for at in range(0, value.shape[0], SPAN)]
    return jnp.concatenate(kept, axis=0)


def down_kernel(own, send):
    size = own.shape[2] // 4
    for m in range(own.shape[0]):
        third = own[m, 1].astype(jnp.float32)
        third = [third[:size], third[2 * size : 3 * size]]
        rows = jnp.concatenate([own[m, 0].astype(jnp.float32), *third], axis=0)
        send[m] = rows.astype(jnp.bfloat16)


def both_taps(pair, weights):
    deep = weights.shape[1] // 2
    lhs = jnp.concatenate(pair, axis=1)
    sums = jnp.dot(lhs, weights, preferred_element_type=jnp.float32)
    return column_taps(sums[:, :deep]), column_taps(sums[:, deep:])


def edge_kernel(masks, own, weight, far, edges, send_up, xs):
    frames = own.shape[0]
    pitch = frames * SPAN
    for i in range(3):
        frames_to(xs, i * pitch, frames, own_row(own, PLANE_ROWS - 3 + i))
    x = [taps_of(xs, i, pitch) for i in range(3)]
    weights = jnp.concatenate([temporal_taps(weight, taps) for taps in ((1, 2), (0, 1))], axis=1)
    lower, upper = both_taps(x[1:], weights)
    third, after = split_rows(dot_taps([[x[0]], [x[2]]], temporal_taps(weight, (0,))), pitch)
    value = inside(lower + third, masks[0])
    far[...] = value.astype(jnp.bfloat16)
    edges[0], edges[1] = last, after = pack(upper), pack(after)
    for i, value in enumerate((pack(value), last, after)):
        send_up[i] = value.astype(jnp.bfloat16)


def crop(value, frames, span):
    shape = (value.shape[0] // (frames * span), frames, span, value.shape[1])
    return value.reshape(shape)[:, :, HALO : HALO + WIDTH].astype(jnp.bfloat16)


def dot_taps(lhs, rhs):
    lhs = jnp.concatenate([jnp.concatenate(blocks, axis=1) for blocks in lhs], axis=0)
    return column_taps(jnp.dot(lhs, rhs, preferred_element_type=jnp.float32))


def split_rows(value, pitch):
    return [value[at : at + pitch] for at in range(0, value.shape[0], pitch)]


def known_rows(first, second, before_last, last, weight):
    pitch, chans = first.shape
    none = jnp.zeros_like(first)
    top = dot_taps([[none, first], [first, second]], weight[chans:])
    end = dot_taps([[before_last, last], [last, none]], weight[: 2 * chans])
    return split_rows(top, pitch) + split_rows(end, pitch)


def pair_rows(pair, weight):
    deep, chans = weight.shape[1], weight.shape[0] // 3
    sums = jnp.dot(
        jnp.concatenate(pair, axis=1),
        jnp.concatenate([weight[chans:], weight[: 2 * chans]], axis=1),
        preferred_element_type=jnp.float32,
    )
    return column_taps(sums[:, :deep]), column_taps(sums[:, deep:])


def top_rows(rows, weight, known):
    pitch, chans = rows[0].shape
    lower, upper = pair_rows(rows[1:], weight)
    through = split_rows(dot_taps([[rows[0]], [rows[2]]], weight[:chans]), pitch)
    return [lower + through[0], upper + known[0], through[1] + known[1]]


def end_rows(rows, weight, known):
    pitch, chans = rows[0].shape
    lower, upper = pair_rows(rows[:2], weight)
    through = split_rows(dot_taps([[rows[0]], [rows[2]]], weight[2 * chans :]), pitch)
    return [through[0] + known[2], lower + known[3], upper + through[1]]


def inner_kernel(
    masks, own, weight, far, w_first, w_second, edges, known_h, known_o, o_mid, shown, w1, w2,
    xs, tall, hs, wt,
):
    frames, span, rows = own.shape[0], SPAN, PLANE_ROWS
    pitch = frames * span
    deep = wt.shape[1]
    temporal_weight_to(wt, weight)
    plane_weight_to(w1, w_first)
    plane_weight_to(w2, w_second)
    for row in range(rows - 1):
        frames_to(xs, row * pitch, frames, own_row(own, row))
    lhs = jnp.concatenate(
        [xs[a, (b + 1) * pitch : (b + rows - 3) * pitch] for b in range(3) for a in range(3)], axis=1
    )
    sums = column_taps(jnp.dot(lhs, wt[...], preferred_element_type=jnp.float32))

    x = [taps_of(xs, i, pitch) for i in range(3)]
    lower, upper = both_taps(x[:2], jnp.concatenate([wt[deep:], wt[: 2 * deep]], axis=1))
    second, before = split_rows(dot_taps([[x[2]], [x[0]]], wt[2 * deep :]), pitch)
    edges[0], edges[1] = pack(lower), pack(before)

    tall[:pitch] = inside(upper + second, masks[0]).astype(jnp.bfloat16)
    tall[pitch : (rows - 3) * pitch] = inside(sums, masks[0]).astype(jnp.bfloat16)
    tall[(rows - 3) * pitch :] = far[...]
    inner = rows - 4
    sums = column_taps(
        jnp.dot(row_taps(tall, 0, inner, pitch), w1[...], preferred_element_type=jnp.float32)
    )
    hs[...] = inside(silu(sums), masks[0]).astype(jnp.bfloat16)
    temporal = [rows_of(tall, i, 1, pitch) for i in (0, 1, inner, inner + 1)]
    for i, value in enumerate(known_rows(*temporal, w1)):
        known_h[i] = pack(value)

    sums = column_taps(
        jnp.dot(row_taps(hs, 0, inner - 2, pitch), w2[...], preferred_element_type=jnp.float32)
    )
    sums = sums + rows_of(tall, 2, inner - 2, pitch).astype(jnp.float32)
    o_mid[...] = crop(sums, frames, span)
    hidden = [rows_of(hs, i, 1, pitch) for i in (0, 1, inner - 2, inner - 1)]
    for i, value in enumerate(known_rows(*hidden, w2)):
        known_o[i] = pack(value + temporal[i].astype(jnp.float32))
    for i in range(3):
        shown[i] = pack(jnp.concatenate([masks[i]] * frames, axis=0))


def cut(value, frames):
    kept = [value[at + HALO - 1 : at + HALO - 1 + WIDTH] for at in range(0, value.shape[0], KEPT)]
    return jnp.concatenate(kept, axis=0).reshape(frames, WIDTH, value.shape[1]).astype(jnp.bfloat16)


def end_kernel(shown, weight, edges, known_h, known_o, below, w1, w2, o_end, xs):
    frames = below.shape[0]
    pitch = frames * SPAN
    for i in range(3):
        frames_to(xs, i * pitch, frames, sent_row(below, i))
    x = [taps_of(xs, i, pitch) for i in range(3)]
    weights = jnp.concatenate([temporal_taps(weight, taps) for taps in ((1, 2), (0, 1))], axis=1)
    lower, upper = both_taps(x[:2], weights)
    third, first = split_rows(dot_taps([[x[2]], [x[0]]], temporal_taps(weight, (2,))), pitch)
    rows = [
        (pack(first) + edges[0]) * shown[0],
        (pack(lower) + edges[1]) * shown[2],
        pack(upper + third) * shown[2],
    ]
    rows = [row.astype(jnp.bfloat16) for row in rows]
    hidden = end_rows(rows, w1, known_h)
    hidden = [(silu(v) * shown[part]).astype(jnp.bfloat16) for v, part in zip(hidden, (0, 0, 2))]
    sums = end_rows(hidden, w2, known_o)
    sums[2] = sums[2] + rows[0].astype(jnp.float32)
    for i, value in enumerate(sums):
        o_end[i] = cut(value, o_end.shape[1])


def top_kernel(shown, edges, known_h, known_o, above, w1, w2, o_mid, o_end, out):
    rows = [
        above[0] * shown[1],
        (above[1] + edges[1]) * shown[1],
        (above[2] + edges[0]) * shown[0],
    ]
    rows = [row.astype(jnp.bfloat16) for row in rows]
    hidden = top_rows(rows, w1, known_h)
    hidden = [(silu(v) * shown[part]).astype(jnp.bfloat16) for v, part in zip(hidden, (1, 0, 0))]
    sums = top_rows(hidden, w2, known_o)
    sums[0] = sums[0] + rows[2].astype(jnp.float32)
    done = [cut(value, out.shape[1]) for value in sums]
    done += [o_mid[i] for i in range(o_mid.shape[0])] + [o_end[i] for i in range(3)]
    each = out.shape[2]
    for row, value in enumerate(done):
        out[row // each, :, row % each] = value


def per_device(frames_in, temporal_weight, first_weight, second_weight):
    tm, slabs = lax.axis_size("tm"), lax.axis_size("rows")
    planes = slabs // SLABS
    frame_count, row_count, col_count, chans = frames_in.shape
    count = tm * SLABS
    width = col_count // count
    span = SPAN
    size = width + 2 * HALO
    plane_rows = SLABS * row_count
    pitch = tm * span
    column, slab = lax.axis_index("tm"), lax.axis_index("rows")
    plane = slab // SLABS
    first_col = (column * SLABS + slab % SLABS) * width - HALO
    col = lax.broadcasted_iota(jnp.int32, (3, span, chans), 1) + first_col
    part = lax.broadcasted_iota(jnp.int32, (3, span, chans), 0)
    visible = (col >= 0) & (col < col_count)
    visible &= ((part != 1) | (plane > 0)) & ((part != 2) | (plane < planes - 1))
    masks = visible.astype(jnp.float32)
    vmem = pl.BlockSpec(memory_space=pltpu.VMEM)
    params = pltpu.CompilerParams(vmem_limit_bytes=VMEM_BYTES)

    def brain(*shape):
        return jax.ShapeDtypeStruct(shape, jnp.bfloat16)

    def held(*shape):
        return pltpu.VMEM(shape, jnp.bfloat16)

    cut = pl.pallas_call(
        windows_kernel,
        out_shape=brain(count, frame_count * row_count * size, chans),
        in_specs=[vmem],
        out_specs=vmem,
        compiler_params=params,
        name="windows",
    )(frames_in)
    cut, masks = lax.optimization_barrier((cut, masks))
    members = [[m * slabs + z * SLABS + j for m in range(tm) for j in range(SLABS)] for z in range(planes)]
    own = lax.all_to_all(
        cut, ("tm", "rows"), split_axis=0, concat_axis=0, tiled=True, axis_index_groups=members
    ).reshape(tm, SLABS, frame_count * row_count * size, chans)

    reach = range(slabs - SLABS)
    send_down = pl.pallas_call(
        down_kernel,
        out_shape=brain(tm, 6 * size, chans),
        in_specs=[vmem],
        out_specs=vmem,
        compiler_params=params,
        name="down",
    )(own)
    partial = jax.ShapeDtypeStruct((2, tm * KEPT, chans), jnp.float32)
    far, edges_end, send_up = pl.pallas_call(
        edge_kernel,
        out_shape=[brain(pitch, chans), partial, brain(3, tm * KEPT, chans)],
        in_specs=[vmem] * 3,
        out_specs=[vmem] * 3,
        scratch_shapes=[held(3, 3 * pitch, chans)],
        compiler_params=params,
        cost_estimate=pl.CostEstimate(flops=4 * 10**8, bytes_accessed=10**6, transcendentals=0),
        name="edge",
    )(masks, own, temporal_weight)
    above = lax.ppermute(send_up, "rows", [(r, r + SLABS) for r in reach])
    below = lax.ppermute(send_down, "rows", [(r + SLABS, r) for r in reach])

    inner = plane_rows - 4
    known = jax.ShapeDtypeStruct((4, tm * KEPT, chans), jnp.float32)
    edges_top, known_h, known_o, o_mid, shown, w1, w2 = pl.pallas_call(
        inner_kernel,
        out_shape=[
            partial,
            known,
            known,
            brain(inner - 2, tm, width, chans),
            jax.ShapeDtypeStruct((3, tm * KEPT, chans), jnp.float32),
            brain(3 * chans, 3 * chans),
            brain(3 * chans, 3 * chans),
        ],
        in_specs=[vmem] * 6,
        out_specs=[vmem] * 7,
        scratch_shapes=[
            held(3, (inner + 3) * pitch, chans),
            held((inner + 2) * pitch, chans),
            held(inner * pitch, chans),
            held(9 * chans, 3 * chans),
        ],
        compiler_params=params,
        cost_estimate=pl.CostEstimate(flops=10**9, bytes_accessed=4 * 10**6, transcendentals=10**5),
        name="inner",
    )(masks, own, temporal_weight, far, first_weight, second_weight)
    o_end = pl.pallas_call(
        end_kernel,
        out_shape=brain(3, tm, width, chans),
        in_specs=[vmem] * 8,
        out_specs=vmem,
        scratch_shapes=[held(3, 3 * pitch, chans)],
        compiler_params=params,
        cost_estimate=pl.CostEstimate(flops=4 * 10**8, bytes_accessed=10**6, transcendentals=10**5),
        name="end",
    )(shown, temporal_weight, edges_end, known_h, known_o, below, w1, w2)
    encoded = pl.pallas_call(
        top_kernel,
        out_shape=brain(SLABS, tm, row_count, width, chans),
        in_specs=[vmem] * 9,
        out_specs=vmem,
        compiler_params=params,
        name="top",
    )(shown, edges_top, known_h, known_o, above, w1, w2, o_mid, o_end)

    groups = [[z * SLABS + j for j in range(SLABS)] for z in range(planes)]
    encoded = lax.all_to_all(
        encoded, "rows", split_axis=0, concat_axis=0, tiled=True, axis_index_groups=groups
    )
    return jnp.transpose(encoded, (1, 2, 0, 3, 4)).reshape(tm, row_count, SLABS * width, chans)


def solution(mesh):
    placed = (P("tm", "rows", None, None), P(), P(), P())
    return jax.shard_map(
        per_device,
        mesh=mesh,
        in_specs=placed,
        out_specs=P(None, "rows", "tm", None),
        check_vma=False,
    )
```
